32 devices in a mesh: seq: 16 (over z, x, core), head: 2 (over y).
Axes of the slice: x: 2, y: 2, z: 4, core: 2. Of those that a mesh axis runs over, the one named last changes fastest.
Arguments:
- loaded: bfloat16 [2048, 2048], P('seq', 'head'), may hold values from -6 to 6
- out_grad: bfloat16 [2048, 512], P('seq', 'head'), may hold values from -6 to 6
- w_query: bfloat16 [2048, 512], P(None, 'head'), may hold values from -0.125 to 0.125
- w_key: bfloat16 [2048, 512], P(None, 'head'), may hold values from -0.125 to 0.125
- w_value: bfloat16 [2048, 512], P(None, 'head'), may hold values from -0.125 to 0.125
- w_beta: bfloat16 [2048, 4], P(None, 'head'), may hold values from -0.125 to 0.125
- beta_max: float32 [4], P('head'), may hold values from 0.0625 to 1
- out_gain: float32 [128], replicated, may hold values from 0.1 to 1.9
- clip_lengths: int32 [16], replicated, may hold values from 1 to 512, 2048 in all
- delay_offsets: int32 [4], replicated, may hold values from 0 to 3, each once
- block_order: int32 [16, 16], P('seq'), may hold values from 0 to 15, each once within a row
Outputs:
- head_out: bfloat16 [2048, 512], P('seq', 'head')
- input_grad: bfloat16 [2048, 2048], P('seq', 'head')
The draws below stay inside these ranges and needn't reach their ends.
Inputs may be any that keep to these rules, and one draw needn't show every extreme that they name: `clip_lengths`: the clip lengths sum to 2048; the longest is exactly 512. `delay_offsets`: each codebook has a different delay. `block_order`: each row is a permutation of 0 to 15.
All inputs are finite; a program needn't handle non-finite values.
Results may differ from the reference program's by a relative error of at most 0.022.
Values may be sent and summed in bfloat16 or wider, within the bound.
No kernel may reach another device: no remote copies, remote signals or barrier semaphores. Data moves between devices by JAX's collectives and lax.ppermute only.
A program may use at most 128 MiB of HBM per device.

```python
import math
import jax
import jax.numpy as jnp
import numpy as np
from jax import lax

D = 2048
DK = 128
DV = 128
CODEBOOKS = 4
SPAN = 128
CLIPS = 16
TOK_DEV = 128
HEADS = 4
TOKENS = 2048
MOST = 512
SOURCES = 16


def levels(stream_key, shape, split, least, high):
    factor_of, own = 1.0, jax.random.fold_in(stream_key, 6)
    for dim, blocks in split:
        heights = jnp.exp(jax.random.uniform(jax.random.fold_in(own, dim), (blocks,), jnp.float32, least / len(split), high / len(split)))
        factor_of = factor_of * jnp.repeat(heights, shape[dim] // blocks).reshape([-1 if axis == dim else 1 for axis in range(len(shape))])
    return factor_of


def profile(amount, total, bound, lean):
    weights = [(1 << 20) // math.isqrt(grade ** lean) + 1 for grade in range(2, amount + 1)]
    rest, given = total - bound - (amount - 1), [1] * (amount - 1)
    while rest > 0:
        movable = [i for i in range(amount - 1) if given[i] < bound]
        whole, budget = sum([weights[i] for i in movable]), rest
        for i in movable:
            addition = min(bound - given[i], max(1, budget * weights[i] // whole), rest)
            given[i] = given[i] + addition
            rest = rest - addition
    return np.array([bound] + given)


def uneven_parts(rng, number_of, total, most, lean):
    if number_of == 2:
        one = jax.random.randint(rng, (), max(1, total - most), min(most, total - 1) + 1)
        return jnp.stack([one, total - one])
    tallies = jnp.asarray(profile(number_of, total, most, lean), jnp.int32)
    couples = (number_of - 1) // 2
    giver, taker = tallies[1:1 + 2 * couples:2], tallies[2:2 + 2 * couples:2]
    slack = jnp.minimum(giver - 1, most - taker)
    moved = jax.random.randint(jax.random.fold_in(rng, 1), (couples,), 0, 1 << 20) % (slack + 1)
    tallies = tallies.at[1:1 + 2 * couples:2].set(giver - moved).at[2:2 + 2 * couples:2].set(taker + moved)
    return tallies[jax.random.permutation(jax.random.fold_in(rng, 2), number_of)]


def noise(own_key, dims, scale, most, cuts=(), kind=jnp.bfloat16):
    loudness = levels(own_key, dims, cuts, -0.22, 0.18) if cuts else 1.0
    values = jax.random.normal(own_key, dims, jnp.float32) * scale * loudness
    return jnp.minimum(jnp.maximum(values, -most), most).astype(kind)


def setup_inputs(seed: int = 0) -> dict:
    key_of = jax.random.split(jax.random.key(seed), 12)
    return {
        "loaded": noise(key_of[0], (TOKENS, D), 1.0, 6.0, ((0, 16), (1, 2))),
        "out_grad": noise(key_of[1], (TOKENS, HEADS * DV), 1.0, 6.0, ((0, 16), (1, 2))),
        "w_query": noise(key_of[2], (D, HEADS * DK), D ** -0.5, 0.125, ((1, 2),)),
        "w_key": noise(key_of[3], (D, HEADS * DK), D ** -0.5, 0.125, ((1, 2),)),
        "w_value": noise(key_of[4], (D, HEADS * DV), D ** -0.5, 0.125, ((1, 2),)),
        "w_beta": noise(key_of[5], (D, HEADS), D ** -0.5, 0.125, ((1, 2),)),
        "beta_max": jnp.clip(jnp.exp(math.log(1.0) - 2.7725887 * jax.random.uniform(key_of[6], (HEADS,), jnp.float32) ** levels(key_of[6], (HEADS,), ((0, 2),), -0.2, 0.2)), 0.0625, 1.0),
        "out_gain": jnp.clip(1.0 + 0.18 * jax.random.normal(key_of[7], (DV,), jnp.float32), 0.1, 1.9),
        "clip_lengths": uneven_parts(key_of[8], CLIPS, TOKENS, MOST, 2).astype(jnp.int32),
        "delay_offsets": jax.random.permutation(key_of[9], CODEBOOKS).astype(jnp.int32),
        "block_order": jax.vmap(lambda own: jax.random.permutation(own, SOURCES))(jax.random.split(key_of[10], SOURCES)).reshape((SOURCES, SOURCES)).astype(jnp.int32),
    }


EPSILON = 1e-06
HIGHEST = lax.Precision.HIGHEST

def clip_start(clip_lengths, positions):
    clip_ends = jnp.cumsum(clip_lengths).astype(jnp.int32)
    finished = clip_ends[None, :] <= positions[:, None]
    return lax.optimization_barrier(jnp.sum(jnp.where(finished, clip_lengths[None, :], 0), axis=1)).astype(jnp.int32)

def column_delays(delay_offsets, columns, group_width):
    codebook = columns // group_width
    matches = codebook[:, None] == jnp.arange(delay_offsets.shape[0], dtype=jnp.int32)[None, :]
    return lax.optimization_barrier(jnp.sum(jnp.where(matches, delay_offsets[None, :], 0), axis=1)).astype(jnp.int32)

def prepare(q_raw, k_raw, logit, rate_cap):
    query_rows = q_raw / jnp.sqrt(lax.optimization_barrier(jnp.sum(q_raw * q_raw, axis=-1, keepdims=True)) + EPSILON)
    key_rows = k_raw / jnp.sqrt(lax.optimization_barrier(jnp.sum(k_raw * k_raw, axis=-1, keepdims=True)) + EPSILON)
    beta_rate = rate_cap * jax.nn.sigmoid(logit[:, 0])
    return (query_rows, key_rows, beta_rate)

def span_terms(key_rows, value_rows, beta_rate, clip_begin, span_first):
    span_len = key_rows.shape[0]
    key_width = key_rows.shape[1]
    same_clip = (clip_begin[:, None] == clip_begin[None, :]).astype(jnp.float32)
    gram = beta_rate[:, None] * jnp.dot(key_rows, key_rows.T, precision=HIGHEST) * same_clip
    system = jnp.eye(span_len, dtype=jnp.float32) + jnp.tril(gram, -1)
    stacked = beta_rate[:, None] * jnp.concatenate([key_rows, value_rows], axis=1)
    solved = jax.scipy.linalg.solve_triangular(system, stacked, lower=True, unit_diagonal=True)
    carried = (clip_begin < span_first).astype(jnp.float32)
    final_mask = (clip_begin == clip_begin[-1]).astype(jnp.float32)
    return (solved[:, :key_width], solved[:, key_width:], carried, final_mask, same_clip)

def span_output(state_in, pieces):
    query_rows, key_rows, value_rows, beta_rate, clip_begin, span_first = pieces
    key_part, value_part, carried, final_mask, same_clip = span_terms(key_rows, value_rows, beta_rate, clip_begin, span_first)
    refreshed = value_part - carried[:, None] * jnp.dot(key_part, state_in, precision=HIGHEST)
    scores = jnp.tril(jnp.dot(query_rows, key_rows.T, precision=HIGHEST)) * same_clip
    outputs = carried[:, None] * jnp.dot(query_rows, state_in, precision=HIGHEST) + jnp.dot(scores, refreshed, precision=HIGHEST)
    state_out = carried[-1] * state_in + jnp.dot(key_rows.T, final_mask[:, None] * refreshed, precision=HIGHEST)
    return (state_out, outputs)

def run_head(q_raw, k_raw, v_raw, logit, rate_cap, out_gain, clip_begin, positions, state_in):
    query_rows, key_rows, beta_rate = prepare(q_raw, k_raw, logit, rate_cap)
    span_count = q_raw.shape[0] // SPAN
    pieces = (query_rows.reshape(span_count, SPAN, -1), key_rows.reshape(span_count, SPAN, -1), v_raw.reshape(span_count, SPAN, -1), beta_rate.reshape(span_count, SPAN), clip_begin.reshape(span_count, SPAN), positions.reshape(span_count, SPAN)[:, 0])
    state_out, outputs = lax.scan(span_output, state_in, pieces)
    raw_out = outputs.reshape(-1, outputs.shape[-1])
    normed = raw_out / jnp.sqrt(lax.optimization_barrier(jnp.mean(raw_out * raw_out, axis=-1, keepdims=True)) + EPSILON) * out_gain[None, :]
    return (normed, state_out)

def back_product(gradient, weight):
    return lax.dot_general(gradient.astype(jnp.float32), weight.astype(jnp.float32), (((1,), (1,)), ((), ())), preferred_element_type=jnp.float32)

def reference(loaded, out_grad, w_query, w_key, w_value, w_beta, beta_max, out_gain, clip_lengths, delay_offsets, block_order):
    sources = block_order.shape[0]
    block_rows = TOK_DEV // sources
    blocks = loaded.reshape(sources, sources, block_rows, D).transpose(1, 0, 2, 3)
    inverse = jnp.argsort(block_order, axis=1).astype(jnp.int32)
    arranged = jnp.take_along_axis(blocks, inverse[:, :, None, None], axis=1).reshape(TOKENS, D)
    positions = jnp.arange(TOKENS, dtype=jnp.int32)
    clip_begin = clip_start(clip_lengths, positions)
    col_delay = column_delays(delay_offsets, jnp.arange(D, dtype=jnp.int32), D // CODEBOOKS)
    delayed = jnp.zeros((TOKENS, D), jnp.bfloat16)
    for shift_by in range(CODEBOOKS):
        shifted = jnp.concatenate([jnp.zeros((shift_by, D), jnp.bfloat16), arranged[:TOKENS - shift_by]], axis=0)
        inside = positions - shift_by >= clip_begin
        delayed = jnp.where((col_delay[None, :] == shift_by) & inside[:, None], shifted, delayed)

    def one_head(summed, head_index):
        wq_head = lax.dynamic_slice_in_dim(w_query, head_index * DK, DK, 1)
        wk_head = lax.dynamic_slice_in_dim(w_key, head_index * DK, DK, 1)
        wv_head = lax.dynamic_slice_in_dim(w_value, head_index * DV, DV, 1)
        wb_head = lax.dynamic_slice_in_dim(w_beta, head_index, 1, 1)
        q_raw = jnp.dot(delayed.astype(jnp.float32), wq_head.astype(jnp.float32), preferred_element_type=jnp.float32)
        k_raw = jnp.dot(delayed.astype(jnp.float32), wk_head.astype(jnp.float32), preferred_element_type=jnp.float32)
        v_raw = jnp.dot(delayed.astype(jnp.float32), wv_head.astype(jnp.float32), preferred_element_type=jnp.float32)
        logit = jnp.dot(delayed.astype(jnp.float32), wb_head.astype(jnp.float32), preferred_element_type=jnp.float32)
        rate_cap = lax.dynamic_index_in_dim(beta_max, head_index, keepdims=False)

        def forward(query_in, key_in, value_in, logit_in):
            start_state = jnp.zeros((DK, DV), jnp.float32)
            return run_head(query_in, key_in, value_in, logit_in, rate_cap, out_gain, clip_begin, positions, start_state)[0]
        normed, pullback = jax.vjp(forward, q_raw, k_raw, v_raw, logit)
        cotangent = lax.dynamic_slice_in_dim(out_grad, head_index * DV, DV, 1).astype(jnp.float32)
        gradients = [grad_part.astype(jnp.bfloat16) for grad_part in pullback(cotangent)]
        backward = back_product(gradients[0], wq_head) + back_product(gradients[1], wk_head)
        backward = backward + back_product(gradients[2], wv_head) + back_product(gradients[3], wb_head)
        return (summed + backward, normed.astype(jnp.bfloat16))
    summed, outputs = lax.scan(one_head, jnp.zeros((TOKENS, D), jnp.float32), jnp.arange(HEADS, dtype=jnp.int32))
    head_out = outputs.transpose(1, 0, 2).reshape(TOKENS, HEADS * DV)
    delayed_grad = summed.astype(jnp.bfloat16)
    input_grad = jnp.zeros((TOKENS, D), jnp.bfloat16)
    for shift_by in range(CODEBOOKS):
        ahead = jnp.concatenate([delayed_grad[shift_by:], jnp.zeros((shift_by, D), jnp.bfloat16)], axis=0)
        inside = (positions + shift_by < TOKENS) & (clip_start(clip_lengths, positions + shift_by) <= positions)
        input_grad = jnp.where((col_delay[None, :] == shift_by) & inside[:, None], ahead, input_grad)
    return (head_out, input_grad)
```

```python
import functools

import jax
import jax.numpy as jnp
from jax import lax
from jax.experimental import pallas as pl
from jax.experimental.pallas import tpu as pltpu
from jax.sharding import PartitionSpec as P

EPSILON = 1e-06
F32 = jnp.float32
BF16 = jnp.bfloat16
HALO = 8
REACH = 16
LANES = 128
VMEM_LIMIT = 16 * 1024 * 1024


def halves(x):
    high = x.astype(BF16)
    return high, (x - high.astype(F32)).astype(BF16)


def dot(a, b):
    return jnp.dot(a, b, preferred_element_type=F32)


def dot_nt(a, b):
    return lax.dot_general(a, b, (((1,), (1,)), ((), ())), preferred_element_type=F32)


def mm(a, b):
    width = b.shape[1]
    b_high, b_low = halves(b)
    right = jnp.concatenate([b_high, b_low], axis=1)
    if a.dtype == BF16:
        both = dot(a, right)
    else:
        left = jnp.concatenate(halves(a), axis=1)
        both = dot(left, jnp.concatenate([right, right], axis=0))
    return both[:, :width] + both[:, width:]


def mm_nt(a, b):
    width = b.shape[0]
    left = jnp.concatenate(halves(a), axis=1)
    right = jnp.concatenate(halves(b), axis=0)
    both = dot_nt(left, jnp.concatenate([right, right], axis=1))
    return both[:, :width] + both[:, width:]


def begins(clips_ref, position):
    end = 0
    total = jnp.zeros_like(position)
    for clip in range(clips_ref.shape[0]):
        length = clips_ref[clip]
        end = end + length
        total = total + jnp.where(end <= position, length, 0)
    return total


def here():
    return lax.axis_index("seq"), lax.axis_index("head")


def solve_unit(low, right):
    size = low[0].shape[0]
    row = lax.broadcasted_iota(jnp.int32, (size, size), 0)
    col = lax.broadcasted_iota(jnp.int32, (size, size), 1)
    eye = jnp.where(row == col, 1.0, 0.0).astype(F32)

    def within(width):
        return (row // width) == (col // width)

    def wide_products(lefts, *rights):
        results = []
        for left, *several in zip(lefts, *rights):
            both, at, parts = mm(left, jnp.concatenate(several, axis=1)), 0, []
            for one in several:
                parts.append(both[:, at : at + one.shape[1]])
                at += one.shape[1]
            results.append(parts)
        return [list(part) for part in zip(*results)]

    block = 2
    inverse = [eye - jnp.where(within(block), x, 0.0) for x in low]
    while block < size:
        wide = min(8 * block, size)
        ring = within(wide) & jnp.logical_not(within(block))
        rest = [jnp.where(ring, n, 0.0) for n in low]
        if wide < size:
            (step,) = wide_products(inverse, rest)
            start = inverse
        else:
            step, solved = wide_products(inverse, rest, right)
            start = [jnp.concatenate(both, axis=1) for both in zip(inverse, solved)]
        square, moved = wide_products(step, step, start)
        start = [x - m for x, m in zip(start, moved)]
        fourth, moved = wide_products(square, square, start)
        start = [x + m for x, m in zip(start, moved)]
        inverse = [x + mm(f, x) for f, x in zip(fourth, start)]
        block = wide
    return [x[:, :size] for x in inverse], [x[:, size:] for x in inverse]


def prepare_kernel(kinds, local, order_ref, clips_ref, delays_ref, cap_ref, pick_ref, edge_ref, last_ref,
                   back_pick_ref, back_edge_ref, mask_ref, caps_ref):
    seq, head = here()
    frames = pick_ref.shape[1]
    parts = pick_ref.shape[0] // kinds
    width = local // parts
    group = (local * kinds) // delays_ref.shape[0]
    sources = order_ref.shape[1]
    rows_each = frames // sources
    base = seq * frames
    row = lax.broadcasted_iota(jnp.int32, (frames, frames), 0)
    col = lax.broadcasted_iota(jnp.int32, (frames, frames), 1)
    row_begin = begins(clips_ref, base + row) - base
    col_begin = begins(clips_ref, base + col[:1]) - base
    last_begin = begins(clips_ref, base + frames - 1) - base
    same = row_begin == col_begin
    carried_last = jnp.where(last_begin < 0, 1.0, 0.0)
    mask_ref[0] = jnp.where((row > col) & same, 1.0, 0.0).astype(F32)
    mask_ref[1] = jnp.where((row >= col) & same, 1.0, 0.0).astype(F32)
    mask_ref[2] = jnp.where(row_begin < 0, 1.0, 0.0).astype(F32)
    mask_ref[3] = jnp.where(row_begin == last_begin, 1.0, 0.0).astype(F32)
    mask_ref[4] = jnp.where(row == col, carried_last, 0.0).astype(F32)
    for index in range(caps_ref.shape[0]):
        caps_ref[index] = jnp.full(caps_ref.shape[1:], cap_ref[index], F32)
    lane = col[:1]
    landing = jnp.zeros((1, frames), jnp.int32)
    for source in range(sources):
        at = order_ref[0, source] * rows_each + (lane - source * rows_each)
        landing = jnp.where(lane // rows_each == source, at, landing)
    edge_row = row[:, :HALO]
    edge_col = lax.broadcasted_iota(jnp.int32, (frames, HALO), 1)
    last_ref[...] = jnp.where(landing == row[:HALO] + (frames - HALO), 1.0, 0.0).astype(BF16)
    for kind in range(kinds):
        owner = lax.rem(head + kinds - kind, kinds)
        for part in range(parts):
            source_row = row - delays_ref[(owner * local + part * width) // group]
            inside = source_row >= row_begin
            pick = jnp.where((landing == source_row) & inside, 1.0, 0.0).astype(BF16)
            pick_ref[kind * parts + part] = pick
            edge = (edge_col - HALO == source_row[:, :HALO]) & inside[:, :HALO]
            edge_ref[kind * parts + part] = jnp.where(edge, 1.0, 0.0).astype(BF16)
    edge_begin = begins(clips_ref, base + frames + edge_col[:1]) - base
    for part in range(parts):
        delay = delays_ref[(head * local + part * width) // group]
        pick = jnp.where((col == row + delay) & (col_begin <= row), 1.0, 0.0).astype(BF16)
        back_pick_ref[part] = pick
        edge = (edge_col + frames == edge_row + delay) & (edge_begin <= edge_row)
        back_edge_ref[part] = jnp.where(edge, 1.0, 0.0).astype(BF16)


def flip_kernel(*refs):
    for ref, out_ref in zip(refs[:4], refs[4:]):
        out_ref[...] = ref[...].T


def add_products(sums, kind, kinds, piece_ref, halo_ref, pick_ref, edge_ref, weights):
    local = halo_ref.shape[1] if piece_ref is None else piece_ref.shape[1]
    parts = pick_ref.shape[0] // kinds
    width = local // parts
    owner = lax.rem(here()[1] + kinds - kind, kinds)
    for part in range(parts):
        span = slice(part * width, (part + 1) * width)
        index = kind * parts + part
        if piece_ref is None:
            delayed = dot(edge_ref[index, :REACH], halo_ref[:, span])
        else:
            delayed = dot(pick_ref[index], piece_ref[:, span])
            if halo_ref is not None:
                delayed = delayed + dot(edge_ref[index], halo_ref[:, span])
        at = pl.ds(pl.multiple_of(owner * local + part * width, width), width)
        delayed = delayed.astype(BF16)
        new = [dot(delayed, weight[at, :]) for weight in weights]
        sums = new if sums is None else [a + b for a, b in zip(sums, new)]
    return sums


def own_kernel(kinds, piece_ref, pick_ref, edge_ref, *refs):
    sums = add_products(None, 0, kinds, piece_ref, None, pick_ref, edge_ref, refs[:4])
    for ref, part in zip(refs[4:], sums):
        ref[...] = part


def own_halo_kernel(kinds, halo_ref, edge_ref, *refs):
    sums = add_products(None, 0, kinds, None, halo_ref, edge_ref, edge_ref, refs[:4])
    for ref, part in zip(refs[4:], sums):
        ref[...] = part


def project_kernel(heads, kinds, mask_ref, cap_ref, *refs):
    sums, first, refs = [ref[...] for ref in refs[:4]], [ref[...] for ref in refs[4:8]], refs[8:]
    pieces, halos = refs[: kinds - 1], refs[kinds - 1 : 2 * kinds - 2]
    pick_ref, edge_ref = refs[2 * kinds - 2 : 2 * kinds]
    weights = refs[2 * kinds : 2 * kinds + 4]
    map_ref, q_ref, k_ref, v_ref, solve_ref, w_ref, aux_ref = refs[2 * kinds + 4 :]
    frames = sums[0].shape[0]
    strict, carried, final, eye = mask_ref[0], mask_ref[2], mask_ref[3], mask_ref[4]
    sums = [jnp.concatenate([x[:REACH] + a, x[REACH:]], axis=0) for x, a in zip(sums, first)]
    for kind in range(1, kinds):
        sums = add_products(
            sums, kind, kinds, pieces[kind - 1], halos[kind - 1], pick_ref, edge_ref, weights
        )
    q_all, k_all, v_all, logit_all = sums
    dk = q_all.shape[1] // heads
    dv = v_all.shape[1] // heads
    keys, rights, lows = [], [], []
    aux = jnp.zeros((frames, LANES), F32)
    aux_lane = lax.broadcasted_iota(jnp.int32, (frames, LANES), 1)
    for head in range(heads):
        q_raw = q_all[:, head * dk : (head + 1) * dk]
        k_raw = k_all[:, head * dk : (head + 1) * dk]
        value = v_all[:, head * dv : (head + 1) * dv]
        q_scale = lax.rsqrt(jnp.sum(q_raw * q_raw, axis=1, keepdims=True) + EPSILON)
        k_scale = lax.rsqrt(jnp.sum(k_raw * k_raw, axis=1, keepdims=True) + EPSILON)
        gate = 1.0 / (1.0 + jnp.exp(-logit_all[:, head : head + 1]))
        rate = cap_ref[head, :, :1] * gate
        key = k_raw * k_scale
        q_ref[head] = q_raw * q_scale
        k_ref[head] = key
        v_ref[head] = value
        for index, item in enumerate((q_scale, k_scale, rate, rate * (1.0 - gate))):
            aux = jnp.where(aux_lane == 4 * head + index, item, aux)
        gram = mm_nt(key, key)
        lows.append(strict * (rate * gram))
        keys.append(key)
        rights.append(rate * jnp.concatenate([key, value], axis=1))
    aux_ref[...] = aux
    solves, solutions = solve_unit(lows, rights)
    for head in range(heads):
        solved = solutions[head]
        solve_ref[head] = solves[head]
        w_ref[head] = solved
        ended = jnp.concatenate(
            [-(final * carried) * solved[:, :dk], final * solved[:, dk:]], axis=1
        )
        affine = mm(keys[head].T, ended)
        map_ref[head, :, :dk] = (affine[:, :dk] + eye).astype(BF16)
        map_ref[head, :, dk:] = affine[:, dk:].astype(BF16)


def local_kernel(heads, mask_ref, q_ref, k_ref, w_ref, solve_ref, early_ref, suffix_ref, prefix_ref,
                 gain_ref, grad_ref, score_t_ref, reach_ref, reach_t_ref, local_ref, solve_t_ref,
                 gram_ref, spread_ref, early_t_ref, suffix_t_ref, weighted_ref, gains_ref):
    frames, dk = q_ref.shape[1:]
    lower, carried, final = mask_ref[1], mask_ref[2], mask_ref[3]
    gains_ref[...] = gain_ref[...]
    for head in range(heads):
        query, key, solved = q_ref[head], k_ref[head], w_ref[head]
        scores = lower * mm_nt(query, key)
        both = mm(scores, solved)
        reach = carried * (query - both[:, :dk])
        score_t_ref[head] = scores.T
        prefix = prefix_ref[head]
        reach_t_ref[head] = reach.T
        grown = mm(reach, prefix.astype(F32))
        reach_ref[head] = grown[:, :dk]
        local_ref[head] = both[:, dk:] + grown[:, dk:]
        solve_t = solve_ref[head].T
        solve_t_ref[head] = solve_t
        gram_ref[head] = mm_nt(key, key)
        spread_ref[head] = mm(solve_t, final * key)
        early_t_ref[head] = early_ref[head].astype(F32).T
        suffix_t_ref[head] = suffix_ref[head].astype(F32).T
        dv = local_ref.shape[2]
        weighted_ref[head] = grad_ref[:, head * dv : (head + 1) * dv].astype(F32) * gain_ref[...]


def is_upper():
    return lax.rem(here()[0], 2) == 1


def join_kernel(heads, chips, own_ref, other_ref, *refs):
    joined_ref, prefix_ref, suffix_ref, early_ref = refs[:4]
    dk = own_ref.shape[1]
    upper = is_upper()
    row = lax.broadcasted_iota(jnp.int32, (dk, dk), 0)
    col = lax.broadcasted_iota(jnp.int32, (dk, dk), 1)
    eye = jnp.where(row == col, 1.0, 0.0)
    for head in range(heads):
        own, other = own_ref[head].astype(F32), other_ref[head].astype(F32)
        early = jnp.where(upper, other, own)
        late = jnp.where(upper, own, other)
        both = dot(late[:, :dk].astype(BF16), early.astype(BF16))
        offset = (both[:, dk:] + late[:, dk:]).astype(BF16)
        if chips > 1:
            joined_ref[head, :, :dk] = both[:, :dk].astype(BF16)
            joined_ref[head, :, dk:] = offset
            refs[4][head] = offset
        else:
            joined_ref[head] = offset
        early_ref[head] = early[:, :dk].astype(BF16)
        prefix_ref[head, :, :dk] = jnp.where(upper, other[:, :dk], eye).astype(BF16)
        prefix_ref[head, :, dk:] = jnp.where(upper, other[:, dk:], 0.0).astype(BF16)
        suffix_ref[head] = jnp.where(upper, eye, other[:, :dk]).astype(BF16)


def give_kernel(heads, even_ref, odd_ref, give_ref):
    upper = is_upper()
    width = odd_ref.shape[2]
    for head in range(heads):
        odd = odd_ref[head].astype(F32)
        even = even_ref[head].astype(F32)
        give_ref[head, :, -width:] = jnp.where(upper, odd, even[:, -width:]).astype(BF16)
        if width < even.shape[1]:
            give_ref[head, :, :-width] = even_ref[head, :, :-width]


def output_kernel(heads, chips, *refs):
    rows, swapped, refs = refs[:chips], refs[chips : chips + chips // 2], refs[chips + chips // 2 :]
    maps = []
    upper = is_upper()
    for index, row in enumerate(rows):
        other = swapped[index // 2]
        width = row.shape[2]
        mine = upper if index % 2 else jnp.logical_not(upper)
        maps.append([
            jnp.where(mine, row[head].astype(F32), other[head, :, -width:].astype(F32))
            for head in range(heads)
        ])
    (prefix_ref, reach_ref, reach_t_ref, local_ref, weighted_ref,
     state_ref, unit_ref, dout_ref, back_ref, send_ref) = refs[:10]
    flipped = refs[10:]
    seq = here()[0]
    dk = reach_ref.shape[2]
    for head in range(heads):
        state = jnp.where(seq >= 2 * chips, maps[-1][head], 0.0)
        for index in range(chips - 2, -1, -1):
            earlier = maps[index][head]
            state = earlier[:, dk:] + mm(earlier[:, :dk].astype(BF16), state)
            state = jnp.where(seq >= 2 * index + 2, state, 0.0)
        raw = local_ref[head] + mm(reach_ref[head], state)
        state_ref[head] = prefix_ref[head, :, dk:].astype(F32) + mm(prefix_ref[head, :, :dk], state)
        scale = lax.rsqrt(jnp.mean(raw * raw, axis=1, keepdims=True) + EPSILON)
        unit = raw * scale
        unit_ref[head] = unit
        weighted = weighted_ref[head]
        dout = scale * (weighted - unit * jnp.mean(unit * weighted, axis=1, keepdims=True))
        dout_ref[head] = dout
        back = mm(reach_t_ref[head], dout)
        back_ref[head] = back
        send_ref[head] = back.astype(BF16)
        product = None
        for earlier, flip_ref in zip(maps, flipped):
            move = earlier[head][:, :dk]
            product = move if product is None else mm(product, move)
            flip_ref[head] = product.T


def join_back_kernel(heads, chips, own_ref, other_ref, early_t_ref, *refs):
    flipped, later_ref, sends = refs[: chips - 1], refs[chips - 1], refs[chips:]
    upper = is_upper()
    for head in range(heads):
        own, other = own_ref[head], other_ref[head].astype(F32)
        late = jnp.where(upper, own, other)
        joined = jnp.where(upper, other, own) + mm(early_t_ref[head], late)
        later_ref[head] = jnp.where(upper, 0.0, other)
        sends[0][head] = joined.astype(BF16)
        for flip_ref, send in zip(flipped, sends[1:]):
            send[head] = mm(flip_ref[head], joined).astype(BF16)


def query_kernel(heads, mask_ref, dout_ref, state_ref, w_ref, score_t_ref, q_ref, k_ref, solve_t_ref,
                 aux_ref, unit_ref, gain_ref, spread_ref, suffix_t_ref, later_ref,
                 out_ref, gq_ref, u_ref, y_ref, dk_ref, reach_ref):
    frames, dk = q_ref.shape[1:]
    lower, carried, final = mask_ref[1], mask_ref[2], mask_ref[3]
    for head in range(heads):
        dv = unit_ref.shape[2]
        out_ref[:, head * dv : (head + 1) * dv] = (unit_ref[head] * gain_ref[...]).astype(BF16)
        dout, state, solved = dout_ref[head], state_ref[head], w_ref[head]
        query, key = q_ref[head], k_ref[head]
        fresh = solved[:, dk:] - carried * mm(solved[:, :dk], state)
        u_ref[head] = fresh
        later, suffix_t = later_ref[head], suffix_t_ref[head]
        ended = final * fresh
        reach = mm(spread_ref[head], jnp.concatenate([later, suffix_t], axis=1))
        reach_ref[head] = reach[:, dv:]
        y_ref[head] = mm(solve_t_ref[head], mm(score_t_ref[head], dout)) + reach[:, :dv]
        flow = lower * mm_nt(dout, fresh)
        dquery = carried * mm_nt(dout, state) + mm(flow, key)
        dk_ref[head] = mm(flow.T, query) + mm_nt(ended, later)
        scale = aux_ref[:, 4 * head : 4 * head + 1]
        along = jnp.sum(query * dquery, axis=1, keepdims=True)
        gq_ref[:, head * dk : (head + 1) * dk] = (scale * (dquery - query * along)).astype(BF16)


def key_kernel(heads, kinds, chips, count, mask_ref, *refs):
    arrived, refs = refs[:chips], refs[chips:]
    (suffix_t_ref, reach_ref, gq_ref, u_ref, y_ref, dk0_ref, state_ref, k_ref, v_ref, gram_ref,
     aux_ref), refs = refs[:11], refs[11:]
    seq = here()[0]
    weights, refs = refs[:4], refs[4:]
    outs, grads_ref = refs[:-1], refs[-1]
    frames, dk = k_ref.shape[1:]
    strict, carried, final = mask_ref[0], mask_ref[2], mask_ref[3]
    key_grads, value_grads = [], []
    lane = lax.broadcasted_iota(jnp.int32, (frames, LANES), 1)
    logit_grad = jnp.zeros((frames, LANES), F32)
    for head in range(heads):
        after = sum(
            jnp.where(seq + 2 * index + 2 < count, ref[head].astype(F32), 0.0)
            for index, ref in enumerate(arrived)
        )
        key, fresh = k_ref[head], u_ref[head]
        k_scale = aux_ref[:, 4 * head + 1 : 4 * head + 2]
        rate = aux_ref[:, 4 * head + 2 : 4 * head + 3]
        slope = aux_ref[:, 4 * head + 3 : 4 * head + 4]
        y = y_ref[head] + mm(reach_ref[head], after)
        both = mm_nt(y, jnp.concatenate([state_ref[head], fresh], axis=0))
        from_state = -carried * both[:, :dk]
        system = strict * -both[:, dk:]
        scaled = rate * system
        dkey = dk0_ref[head] + mm_nt(mm_nt(final * fresh, after), suffix_t_ref[head])
        dkey = dkey + mm(scaled + scaled.T, key) + rate * from_state
        drate = jnp.sum(
            system * gram_ref[head] + from_state * key + y * v_ref[head], axis=1, keepdims=True
        )
        logit_grad = jnp.where(lane == head, drate * slope, logit_grad)
        along = jnp.sum(key * dkey, axis=1, keepdims=True)
        key_grads.append((k_scale * (dkey - key * along)).astype(BF16))
        value_grads.append((rate * y).astype(BF16))
    grads_ref[...] = jnp.concatenate(
        [gq_ref[...]] + key_grads + value_grads + [logit_grad.astype(BF16)], axis=1
    )
    others, halos = outs[: kinds - 1], outs[kinds - 1 :]
    for turn in range(1, kinds):
        back_products(grads_ref, weights, turn, kinds, others[turn - 1], halos[turn - 1])


def back_products(grads_ref, weights, turn, kinds, sum_ref, halo_ref):
    local = sum_ref.shape[1]
    width = min(512, local)
    for part in range(local // width):
        first = lax.rem(here()[1] + turn, kinds) * local + part * width
        at = pl.ds(pl.multiple_of(first, width), width)
        row, total = 0, 0.0
        for weight in weights:
            total = total + dot(grads_ref[:, row : row + weight.shape[0]], weight[:, at])
            row += weight.shape[0]
        span = slice(part * width, (part + 1) * width)
        halo_ref[:, span] = total[:HALO].astype(BF16)
        sum_ref[:, span] = total.astype(sum_ref.dtype)


def own_back_kernel(kinds, grads_ref, *refs):
    back_products(grads_ref, refs[:4], 0, kinds, *refs[4:])


def finish_kernel(kinds, pick_ref, edge_ref, mine_ref, *refs):
    others, halos = refs[: kinds - 1], refs[kinds - 1 : 2 * kinds - 1]
    out_ref, held_ref, semaphores = refs[-3:]
    parts = pick_ref.shape[0]
    copies = []
    width = mine_ref.shape[1] // parts
    for part in range(parts):
        span = slice(part * width, (part + 1) * width)
        total = mine_ref[:, span]
        for other in others:
            total = total + other[:, span].astype(F32)
        edge = halos[0][:, span].astype(F32)
        for halo in halos[1:]:
            edge = edge + halo[:, span].astype(F32)
        moved = dot(pick_ref[part], total.astype(BF16)) + dot(edge_ref[part], edge.astype(BF16))
        held_ref[:, span] = moved.astype(BF16)
        copies.append(
            pltpu.make_async_copy(held_ref.at[:, span], out_ref.at[:, span], semaphores.at[part])
        )
        copies[-1].start()
    for copy in copies:
        copy.wait()


SMEM = pl.BlockSpec(memory_space=pltpu.SMEM)
VMEM = pl.BlockSpec(memory_space=pltpu.VMEM)


def call(body, name, scalars, arrays, outs, flops=0, out_space=VMEM, scratch=()):
    moved = sum(a.size * a.dtype.itemsize for a in arrays)
    moved += sum(o.size * o.dtype.itemsize for o in outs)
    return pl.pallas_call(
        body,
        name=name,
        out_shape=tuple(outs),
        in_specs=[SMEM] * len(scalars) + [VMEM] * len(arrays),
        out_specs=tuple([out_space] * len(outs)),
        scratch_shapes=list(scratch),
        cost_estimate=pl.CostEstimate(flops=flops, bytes_accessed=moved, transcendentals=0),
        compiler_params=pltpu.CompilerParams(vmem_limit_bytes=VMEM_LIMIT),
    )(*scalars, *arrays)


def shape(dims, kind=F32):
    return jax.ShapeDtypeStruct(tuple(dims), kind)


def row_shift(x, by, rising, count):
    chips = count // 2
    pairs = []
    for chip in range(chips):
        up, down = chip + by, chip - by
        pairs.append((2 * chip + rising, 2 * up + rising if up < chips else 2 * chip + 1 - rising))
        pairs.append((2 * chip + 1 - rising, 2 * down + 1 - rising if down >= 0 else 2 * chip + rising))
    return lax.ppermute(x, "seq", pairs)


def seq_shift(x, by, count):
    return lax.ppermute(x, "seq", [(i, (i + by) % count) for i in range(count)])


def core_swap(x, count):
    return lax.ppermute(x, "seq", [(i, i ^ 1) for i in range(count)])


def corner_shift(x, by, turn, count, kinds):
    pairs = []
    for i in range(count):
        for h in range(kinds):
            pairs.append((i * kinds + h, (i + by) % count * kinds + (h + turn) % kinds))
    return lax.ppermute(x, ("seq", "head"), pairs)


def head_turn(x, turn, kinds):
    return lax.ppermute(x, "head", [(h, (h + turn) % kinds) for h in range(kinds)])


def on_device(loaded, out_grad, w_query, w_key, w_value, w_beta, beta_max, out_gain, clip_lengths,
              delay_offsets, block_order):
    count = lax.axis_size("seq")
    kinds = lax.axis_size("head")
    frames, local = loaded.shape
    rows_each = frames // count
    heads = w_beta.shape[1]
    dk = w_query.shape[1] // heads
    dv = w_value.shape[1] // heads
    chips = count // 8
    group = (local * kinds) // delay_offsets.shape[0]
    parts = local // min(group, local)
    columns = heads * (2 * dk + dv) + LANES
    wb = jnp.pad(w_beta, ((0, 0), (0, LANES - heads)))
    gain = out_gain.reshape(1, dv)

    received = lax.all_to_all(
        loaded.reshape(count, rows_each, local), "seq", split_axis=0, concat_axis=0, tiled=True
    ).reshape(frames, local)
    prepared = call(
        functools.partial(prepare_kernel, kinds, local),
        "prepare",
        [block_order, clip_lengths, delay_offsets, beta_max],
        [],
        [
            shape((kinds * parts, frames, frames), BF16),
            shape((kinds * parts, frames, HALO), BF16),
            shape((HALO, frames), BF16),
            shape((parts, frames, frames), BF16),
            shape((parts, frames, HALO), BF16),
            shape((5, frames, frames)),
            shape((heads, 1, LANES)),
        ],
    )
    received, wb, *prepared = lax.optimization_barrier((received, wb, *prepared))
    pick, edge, last, back_pick, back_edge, masks, caps = prepared
    tail = jnp.dot(last, received, preferred_element_type=F32).astype(BF16)
    pieces = [head_turn(received, turn, kinds) for turn in range(1, kinds)]
    halos = [corner_shift(tail, 1, turn, count, kinds) for turn in range(kinds)]
    weights = [w_query, w_key, w_value, wb]
    sums = call(
        functools.partial(own_kernel, kinds),
        "project_own",
        [],
        [received, pick, edge] + weights,
        [shape((frames, weight.shape[1])) for weight in weights],
        flops=2 * frames * local * columns,
    )
    first = call(
        functools.partial(own_halo_kernel, kinds),
        "project_halo",
        [],
        [halos[0], edge] + weights,
        [shape((REACH, weight.shape[1])) for weight in weights],
        flops=2 * REACH * local * columns,
    )
    flipped = call(
        flip_kernel, "flip", [], weights, [shape(w.shape[::-1], BF16) for w in weights]
    )
    sums, first, flipped = lax.optimization_barrier((sums, first, flipped))

    square = shape((heads, frames, dk))
    values = shape((heads, frames, dv))
    times = shape((heads, frames, frames))
    maps = shape((heads, dk, dk + dv), BF16)
    moves = shape((heads, dk, dk))
    states = shape((heads, dk, dv))
    offsets = shape((heads, dk, dv), BF16)
    affine, q, k, v, solve, solved, aux = call(
        functools.partial(project_kernel, heads, kinds),
        "project",
        [],
        [masks, caps] + list(sums) + list(first) + pieces + halos[1:] + [pick, edge] + weights,
        [maps, square, square, values, times, shape((heads, frames, dk + dv)),
         shape((frames, LANES))],
        flops=2 * frames * local * columns,
    )
    results = call(
        functools.partial(join_kernel, heads, chips),
        "join",
        [],
        [affine, core_swap(affine, count)],
        [maps if chips > 1 else offsets, maps, shape(moves.shape, BF16), shape(moves.shape, BF16)]
        + [offsets] * (chips > 1),
        flops=10**7,
    )
    joined, prefix, suffix, early = results[:4]
    arrived = [row_shift(joined, by, (by - 1) % 2, count) for by in range(1, chips)]
    arrived.append(row_shift(results[-1], chips, (chips - 1) % 2, count))
    local_terms = call(
        functools.partial(local_kernel, heads),
        "local_terms",
        [],
        [masks, q, k, solved, solve, early, suffix, prefix, gain, out_grad],
        [times, square, shape((heads, dk, frames)), values, times, times, square, moves, moves,
         values, shape((1, dv))],
        flops=2 * 10**8,
    )
    arrived, local_terms = lax.optimization_barrier((arrived, local_terms))
    (score_t, reach, reach_t, local_out, solve_t, gram, spread, early_t, suffix_t, weighted,
     gains) = local_terms
    swapped = []
    for at in range(0, chips, 2):
        (give,) = call(
            functools.partial(give_kernel, heads), "give", [], arrived[at : at + 2], [maps],
        )
        swapped.append(core_swap(give, count))
    results = call(
        functools.partial(output_kernel, heads, chips),
        "outputs",
        [],
        arrived + swapped + [prefix, reach, reach_t, local_out, weighted],
        [states, values, values, states, offsets] + [moves] * (chips - 1),
        flops=2 * 10**8,
    )
    state, unit, dout, back, send = results[:5]
    results = call(
        functools.partial(join_back_kernel, heads, chips),
        "join_back",
        [],
        [back, core_swap(send, count), early_t] + list(results[5:]),
        [states] + [offsets] * chips,
        flops=10**7,
    )
    later = results[0]
    arrived = [seq_shift(x, -2 * by, count) for by, x in enumerate(results[1:], 1)]
    query_terms = call(
        functools.partial(query_kernel, heads),
        "query_grad",
        [],
        [masks, dout, state, solved, score_t, q, k, solve_t, aux, unit, gains, spread, suffix_t,
         later],
        [shape((frames, heads * dv), BF16), shape((frames, heads * dk), BF16), values, values,
         square, square],
        flops=2 * 10**8,
    )
    head_out, gq, fresh, y, dkey, reach = query_terms
    results = call(
        functools.partial(key_kernel, heads, kinds, chips, count),
        "key_grad",
        [],
        [masks] + arrived + [suffix_t, reach, gq, fresh, y, dkey, state, k, v, gram, aux] + list(flipped),
        [shape((frames, local), BF16)] * (kinds - 1)
        + [shape((HALO, local), BF16)] * (kinds - 1)
        + [shape((frames, columns), BF16)],
        flops=2 * 10**8,
    )
    others, edges, grads = results[: kinds - 1], results[kinds - 1 : -1], results[-1]
    mine, edge = call(
        functools.partial(own_back_kernel, kinds),
        "own_back",
        [],
        [grads] + list(flipped),
        [shape((frames, local)), shape((HALO, local), BF16)],
        flops=2 * frames * local * columns,
    )
    others = [head_turn(x, turn, kinds) for turn, x in enumerate(others, 1)]
    edges = [corner_shift(x, -1, turn, count, kinds) for turn, x in enumerate([edge] + list(edges))]
    (input_grad,) = call(
        functools.partial(finish_kernel, kinds),
        "finish",
        [],
        [back_pick, back_edge, mine] + others + edges,
        [shape((frames, local), BF16)],
        flops=10**8,
        out_space=pl.BlockSpec(memory_space=pl.ANY),
        scratch=[pltpu.VMEM((frames, local), BF16), pltpu.SemaphoreType.DMA((parts,))],
    )
    return head_out, input_grad


def solution(mesh):
    return jax.shard_map(
        on_device,
        mesh=mesh,
        in_specs=(
            P("seq", "head"),
            P("seq", "head"),
            P(None, "head"),
            P(None, "head"),
            P(None, "head"),
            P(None, "head"),
            P("head"),
            P(),
            P(),
            P(),
            P("seq", None),
        ),
        out_specs=(P("seq", "head"), P("seq", "head")),
        check_vma=False,
    )
```

```python
import functools

import jax
import jax.numpy as jnp
from jax import lax
from jax.experimental import pallas as pl
from jax.experimental.pallas import tpu as pltpu
from jax.sharding import PartitionSpec as P

EPSILON = 1e-06
F32 = jnp.float32
BF16 = jnp.bfloat16
HALO = 8
REACH = 16
LANES = 128
VMEM_LIMIT = 16 * 1024 * 1024


def halves(x):
    high = x.astype(BF16)
    return high, (x - high.astype(F32)).astype(BF16)


def dot(a, b):
    return jnp.dot(a, b, preferred_element_type=F32)


def dot_nt(a, b):
    return lax.dot_general(a, b, (((1,), (1,)), ((), ())), preferred_element_type=F32)


def mm(a, b):
    width = b.shape[1]
    b_high, b_low = halves(b)
    right = jnp.concatenate([b_high, b_low], axis=1)
    if a.dtype == BF16:
        both = dot(a, right)
    else:
        left = jnp.concatenate(halves(a), axis=1)
        both = dot(left, jnp.concatenate([right, right], axis=0))
    return both[:, :width] + both[:, width:]


def mm_nt(a, b):
    width = b.shape[0]
    left = jnp.concatenate(halves(a), axis=1)
    right = jnp.concatenate(halves(b), axis=0)
    both = dot_nt(left, jnp.concatenate([right, right], axis=1))
    return both[:, :width] + both[:, width:]


def begins(clips_ref, position):
    end = 0
    total = jnp.zeros_like(position)
    for clip in range(clips_ref.shape[0]):
        length = clips_ref[clip]
        end = end + length
        total = total + jnp.where(end <= position, length, 0)
    return total


def here():
    return lax.axis_index("seq"), lax.axis_index("head")


def solve_unit(low, right):
    size = low[0].shape[0]
    row = lax.broadcasted_iota(jnp.int32, (size, size), 0)
    col = lax.broadcasted_iota(jnp.int32, (size, size), 1)
    eye = jnp.where(row == col, 1.0, 0.0).astype(F32)

    def within(width):
        return (row // width) == (col // width)

    def wide_products(lefts, *rights):
        results = []
        for left, *several in zip(lefts, *rights):
            both, at, parts = mm(left, jnp.concatenate(several, axis=1)), 0, []
            for one in several:
                parts.append(both[:, at : at + one.shape[1]])
                at += one.shape[1]
            results.append(parts)
        return [list(part) for part in zip(*results)]

    block = 2
    inverse = [eye - jnp.where(within(block), x, 0.0) for x in low]
    while block < size:
        wide = min(8 * block, size)
        ring = within(wide) & jnp.logical_not(within(block))
        rest = [jnp.where(ring, n, 0.0) for n in low]
        if wide < size:
            (step,) = wide_products(inverse, rest)
            start = inverse
        else:
            step, solved = wide_products(inverse, rest, right)
            start = [jnp.concatenate(both, axis=1) for both in zip(inverse, solved)]
        square, moved = wide_products(step, step, start)
        start = [x - m for x, m in zip(start, moved)]
        fourth, moved = wide_products(square, square, start)
        start = [x + m for x, m in zip(start, moved)]
        inverse = [x + mm(f, x) for f, x in zip(fourth, start)]
        block = wide
    return [x[:, :size] for x in inverse], [x[:, size:] for x in inverse]


def prepare_kernel(kinds, local, order_ref, clips_ref, delays_ref, cap_ref, pick_ref, edge_ref, last_ref,
                   back_pick_ref, back_edge_ref, mask_ref, caps_ref):
    seq, head = here()
    frames = pick_ref.shape[1]
    parts = pick_ref.shape[0] // kinds
    width = local // parts
    group = (local * kinds) // delays_ref.shape[0]
    sources = order_ref.shape[1]
    rows_each = frames // sources
    base = seq * frames
    row = lax.broadcasted_iota(jnp.int32, (frames, frames), 0)
    col = lax.broadcasted_iota(jnp.int32, (frames, frames), 1)
    row_begin = begins(clips_ref, base + row) - base
    col_begin = begins(clips_ref, base + col[:1]) - base
    last_begin = begins(clips_ref, base + frames - 1) - base
    same = row_begin == col_begin
    carried_last = jnp.where(last_begin < 0, 1.0, 0.0)
    mask_ref[0] = jnp.where((row > col) & same, 1.0, 0.0).astype(F32)
    mask_ref[1] = jnp.where((row >= col) & same, 1.0, 0.0).astype(F32)
    mask_ref[2] = jnp.where(row_begin < 0, 1.0, 0.0).astype(F32)
    mask_ref[3] = jnp.where(row_begin == last_begin, 1.0, 0.0).astype(F32)
    mask_ref[4] = jnp.where(row == col, carried_last, 0.0).astype(F32)
    for index in range(caps_ref.shape[0]):
        caps_ref[index] = jnp.full(caps_ref.shape[1:], cap_ref[index], F32)
    lane = col[:1]
    landing = jnp.zeros((1, frames), jnp.int32)
    for source in range(sources):
        at = order_ref[0, source] * rows_each + (lane - source * rows_each)
        landing = jnp.where(lane // rows_each == source, at, landing)
    edge_row = row[:, :HALO]
    edge_col = lax.broadcasted_iota(jnp.int32, (frames, HALO), 1)
    last_ref[...] = jnp.where(landing == row[:HALO] + (frames - HALO), 1.0, 0.0).astype(BF16)
    for kind in range(kinds):
        owner = lax.rem(head + kinds - kind, kinds)
        for part in range(parts):
            source_row = row - delays_ref[(owner * local + part * width) // group]
            inside = source_row >= row_begin
            pick = jnp.where((landing == source_row) & inside, 1.0, 0.0).astype(BF16)
            pick_ref[kind * parts + part] = pick
            edge = (edge_col - HALO == source_row[:, :HALO]) & inside[:, :HALO]
            edge_ref[kind * parts + part] = jnp.where(edge, 1.0, 0.0).astype(BF16)
    edge_begin = begins(clips_ref, base + frames + edge_col[:1]) - base
    for part in range(parts):
        delay = delays_ref[(head * local + part * width) // group]
        pick = jnp.where((col == row + delay) & (col_begin <= row), 1.0, 0.0).astype(BF16)
        back_pick_ref[part] = pick
        edge = (edge_col + frames == edge_row + delay) & (edge_begin <= edge_row)
        back_edge_ref[part] = jnp.where(edge, 1.0, 0.0).astype(BF16)


def flip_kernel(*refs):
    for ref, out_ref in zip(refs[:4], refs[4:]):
        out_ref[...] = ref[...].T


def add_products(sums, kind, kinds, piece_ref, halo_ref, pick_ref, edge_ref, weights):
    local = halo_ref.shape[1] if piece_ref is None else piece_ref.shape[1]
    parts = pick_ref.shape[0] // kinds
    width = local // parts
    owner = lax.rem(here()[1] + kinds - kind, kinds)
    for part in range(parts):
        span = slice(part * width, (part + 1) * width)
        index = kind * parts + part
        if piece_ref is None:
            delayed = dot(edge_ref[index, :REACH], halo_ref[:, span])
        else:
            delayed = dot(pick_ref[index], piece_ref[:, span])
            if halo_ref is not None:
                delayed = delayed + dot(edge_ref[index], halo_ref[:, span])
        at = pl.ds(pl.multiple_of(owner * local + part * width, width), width)
        delayed = delayed.astype(BF16)
        new = [dot(delayed, weight[at, :]) for weight in weights]
        sums = new if sums is None else [a + b for a, b in zip(sums, new)]
    return sums


def own_kernel(kinds, piece_ref, pick_ref, edge_ref, *refs):
    sums = add_products(None, 0, kinds, piece_ref, None, pick_ref, edge_ref, refs[:4])
    for ref, part in zip(refs[4:], sums):
        ref[...] = part


def own_halo_kernel(kinds, halo_ref, edge_ref, *refs):
    sums = add_products(None, 0, kinds, None, halo_ref, edge_ref, edge_ref, refs[:4])
    for ref, part in zip(refs[4:], sums):
        ref[...] = part


def project_kernel(heads, kinds, mask_ref, cap_ref, *refs):
    sums, first, refs = [ref[...] for ref in refs[:4]], [ref[...] for ref in refs[4:8]], refs[8:]
    pieces, halos = refs[: kinds - 1], refs[kinds - 1 : 2 * kinds - 2]
    pick_ref, edge_ref = refs[2 * kinds - 2 : 2 * kinds]
    weights = refs[2 * kinds : 2 * kinds + 4]
    map_ref, q_ref, k_ref, v_ref, solve_ref, w_ref, aux_ref = refs[2 * kinds + 4 :]
    frames = sums[0].shape[0]
    strict, carried, final, eye = mask_ref[0], mask_ref[2], mask_ref[3], mask_ref[4]
    sums = [jnp.concatenate([x[:REACH] + a, x[REACH:]], axis=0) for x, a in zip(sums, first)]
    for kind in range(1, kinds):
        sums = add_products(
            sums, kind, kinds, pieces[kind - 1], halos[kind - 1], pick_ref, edge_ref, weights
        )
    q_all, k_all, v_all, logit_all = sums
    dk = q_all.shape[1] // heads
    dv = v_all.shape[1] // heads
    keys, rights, lows = [], [], []
    aux = jnp.zeros((frames, LANES), F32)
    aux_lane = lax.broadcasted_iota(jnp.int32, (frames, LANES), 1)
    for head in range(heads):
        q_raw = q_all[:, head * dk : (head + 1) * dk]
        k_raw = k_all[:, head * dk : (head + 1) * dk]
        value = v_all[:, head * dv : (head + 1) * dv]
        q_scale = lax.rsqrt(jnp.sum(q_raw * q_raw, axis=1, keepdims=True) + EPSILON)
        k_scale = lax.rsqrt(jnp.sum(k_raw * k_raw, axis=1, keepdims=True) + EPSILON)
        gate = 1.0 / (1.0 + jnp.exp(-logit_all[:, head : head + 1]))
        rate = cap_ref[head, :, :1] * gate
        key = k_raw * k_scale
        q_ref[head] = q_raw * q_scale
        k_ref[head] = key
        v_ref[head] = value
        for index, item in enumerate((q_scale, k_scale, rate, rate * (1.0 - gate))):
            aux = jnp.where(aux_lane == 4 * head + index, item, aux)
        gram = mm_nt(key, key)
        lows.append(strict * (rate * gram))
        keys.append(key)
        rights.append(rate * jnp.concatenate([key, value], axis=1))
    aux_ref[...] = aux
    solves, solutions = solve_unit(lows, rights)
    for head in range(heads):
        solved = solutions[head]
        solve_ref[head] = solves[head]
        w_ref[head] = solved
        ended = jnp.concatenate(
            [-(final * carried) * solved[:, :dk], final * solved[:, dk:]], axis=1
        )
        affine = mm(keys[head].T, ended)
        map_ref[head, :, :dk] = (affine[:, :dk] + eye).astype(BF16)
        map_ref[head, :, dk:] = affine[:, dk:].astype(BF16)


def local_kernel(heads, mask_ref, q_ref, k_ref, w_ref, solve_ref, early_ref, suffix_ref, prefix_ref,
                 gain_ref, grad_ref, score_t_ref, reach_ref, reach_t_ref, local_ref, solve_t_ref,
                 gram_ref, spread_ref, early_t_ref, suffix_t_ref, weighted_ref, gains_ref):
    frames, dk = q_ref.shape[1:]
    lower, carried, final = mask_ref[1], mask_ref[2], mask_ref[3]
    gains_ref[...] = gain_ref[...]
    for head in range(heads):
        query, key, solved = q_ref[head], k_ref[head], w_ref[head]
        scores = lower * mm_nt(query, key)
        both = mm(scores, solved)
        reach = carried * (query - both[:, :dk])
        score_t_ref[head] = scores.T
        prefix = prefix_ref[head]
        reach_t_ref[head] = reach.T
        grown = mm(reach, prefix.astype(F32))
        reach_ref[head] = grown[:, :dk]
        local_ref[head] = both[:, dk:] + grown[:, dk:]
        solve_t = solve_ref[head].T
        solve_t_ref[head] = solve_t
        gram_ref[head] = mm_nt(key, key)
        spread_ref[head] = mm(solve_t, final * key)
        early_t_ref[head] = early_ref[head].astype(F32).T
        suffix_t_ref[head] = suffix_ref[head].astype(F32).T
        dv = local_ref.shape[2]
        weighted_ref[head] = grad_ref[:, head * dv : (head + 1) * dv].astype(F32) * gain_ref[...]


def is_upper():
    return lax.rem(here()[0], 2) == 1


def join_kernel(heads, chips, own_ref, other_ref, *refs):
    joined_ref, prefix_ref, suffix_ref, early_ref = refs[:4]
    dk = own_ref.shape[1]
    upper = is_upper()
    row = lax.broadcasted_iota(jnp.int32, (dk, dk), 0)
    col = lax.broadcasted_iota(jnp.int32, (dk, dk), 1)
    eye = jnp.where(row == col, 1.0, 0.0)
    for head in range(heads):
        own, other = own_ref[head].astype(F32), other_ref[head].astype(F32)
        early = jnp.where(upper, other, own)
        late = jnp.where(upper, own, other)
        both = dot(late[:, :dk].astype(BF16), early.astype(BF16))
        offset = (both[:, dk:] + late[:, dk:]).astype(BF16)
        if chips > 1:
            joined_ref[head, :, :dk] = both[:, :dk].astype(BF16)
            joined_ref[head, :, dk:] = offset
            refs[4][head] = offset
        else:
            joined_ref[head] = offset
        early_ref[head] = early[:, :dk].astype(BF16)
        prefix_ref[head, :, :dk] = jnp.where(upper, other[:, :dk], eye).astype(BF16)
        prefix_ref[head, :, dk:] = jnp.where(upper, other[:, dk:], 0.0).astype(BF16)
        suffix_ref[head] = jnp.where(upper, eye, other[:, :dk]).astype(BF16)


def give_kernel(heads, even_ref, odd_ref, give_ref):
    upper = is_upper()
    width = odd_ref.shape[2]
    for head in range(heads):
        odd = odd_ref[head].astype(F32)
        even = even_ref[head].astype(F32)
        give_ref[head, :, -width:] = jnp.where(upper, odd, even[:, -width:]).astype(BF16)
        if width < even.shape[1]:
            give_ref[head, :, :-width] = even_ref[head, :, :-width]


def output_kernel(heads, chips, *refs):
    rows, swapped, refs = refs[:chips], refs[chips : chips + chips // 2], refs[chips + chips // 2 :]
    maps = []
    upper = is_upper()
    for index, row in enumerate(rows):
        other = swapped[index // 2]
        width = row.shape[2]
        mine = upper if index % 2 else jnp.logical_not(upper)
        maps.append([
            jnp.where(mine, row[head].astype(F32), other[head, :, -width:].astype(F32))
            for head in range(heads)
        ])
    (prefix_ref, reach_ref, reach_t_ref, local_ref, weighted_ref,
     state_ref, unit_ref, dout_ref, back_ref, send_ref) = refs[:10]
    flipped = refs[10:]
    seq = here()[0]
    dk = reach_ref.shape[2]
    for head in range(heads):
        state = jnp.where(seq >= 2 * chips, maps[-1][head], 0.0)
        for index in range(chips - 2, -1, -1):
            earlier = maps[index][head]
            state = earlier[:, dk:] + mm(earlier[:, :dk].astype(BF16), state)
            state = jnp.where(seq >= 2 * index + 2, state, 0.0)
        raw = local_ref[head] + mm(reach_ref[head], state)
        state_ref[head] = prefix_ref[head, :, dk:].astype(F32) + mm(prefix_ref[head, :, :dk], state)
        scale = lax.rsqrt(jnp.mean(raw * raw, axis=1, keepdims=True) + EPSILON)
        unit = raw * scale
        unit_ref[head] = unit
        weighted = weighted_ref[head]
        dout = scale * (weighted - unit * jnp.mean(unit * weighted, axis=1, keepdims=True))
        dout_ref[head] = dout
        back = mm(reach_t_ref[head], dout)
        back_ref[head] = back
        send_ref[head] = back.astype(BF16)
        product = None
        for earlier, flip_ref in zip(maps, flipped):
            move = earlier[head][:, :dk]
            product = move if product is None else mm(product, move)
            flip_ref[head] = product.T


def join_back_kernel(heads, chips, own_ref, other_ref, early_t_ref, *refs):
    flipped, later_ref, sends = refs[: chips - 1], refs[chips - 1], refs[chips:]
    upper = is_upper()
    for head in range(heads):
        own, other = own_ref[head], other_ref[head].astype(F32)
        late = jnp.where(upper, own, other)
        joined = jnp.where(upper, other, own) + mm(early_t_ref[head], late)
        later_ref[head] = jnp.where(upper, 0.0, other)
        sends[0][head] = joined.astype(BF16)
        for flip_ref, send in zip(flipped, sends[1:]):
            send[head] = mm(flip_ref[head], joined).astype(BF16)


def query_kernel(heads, mask_ref, dout_ref, state_ref, w_ref, score_t_ref, q_ref, k_ref, solve_t_ref,
                 aux_ref, unit_ref, gain_ref, spread_ref, suffix_t_ref, later_ref,
                 out_ref, gq_ref, u_ref, y_ref, dk_ref, reach_ref):
    frames, dk = q_ref.shape[1:]
    lower, carried, final = mask_ref[1], mask_ref[2], mask_ref[3]
    for head in range(heads):
        dv = unit_ref.shape[2]
        out_ref[:, head * dv : (head + 1) * dv] = (unit_ref[head] * gain_ref[...]).astype(BF16)
        dout, state, solved = dout_ref[head], state_ref[head], w_ref[head]
        query, key = q_ref[head], k_ref[head]
        fresh = solved[:, dk:] - carried * mm(solved[:, :dk], state)
        u_ref[head] = fresh
        later, suffix_t = later_ref[head], suffix_t_ref[head]
        ended = final * fresh
        reach = mm(spread_ref[head], jnp.concatenate([later, suffix_t], axis=1))
        reach_ref[head] = reach[:, dv:]
        y_ref[head] = mm(solve_t_ref[head], mm(score_t_ref[head], dout)) + reach[:, :dv]
        flow = lower * mm_nt(dout, fresh)
        dquery = carried * mm_nt(dout, state) + mm(flow, key)
        dk_ref[head] = mm(flow.T, query) + mm_nt(ended, later)
        scale = aux_ref[:, 4 * head : 4 * head + 1]
        along = jnp.sum(query * dquery, axis=1, keepdims=True)
        gq_ref[:, head * dk : (head + 1) * dk] = (scale * (dquery - query * along)).astype(BF16)


def key_kernel(heads, kinds, chips, count, mask_ref, *refs):
    arrived, row_ref, shared_ref, refs = refs[: chips - 1], refs[chips - 1], refs[chips], refs[chips + 1 :]
    (suffix_t_ref, reach_ref, gq_ref, u_ref, y_ref, dk0_ref, state_ref, k_ref, v_ref, gram_ref,
     aux_ref), refs = refs[:11], refs[11:]
    seq = here()[0]
    weights, refs = refs[:4], refs[4:]
    outs, grads_ref = refs[:-1], refs[-1]
    frames, dk = k_ref.shape[1:]
    strict, carried, final = mask_ref[0], mask_ref[2], mask_ref[3]
    key_grads, value_grads = [], []
    lane = lax.broadcasted_iota(jnp.int32, (frames, LANES), 1)
    logit_grad = jnp.zeros((frames, LANES), F32)
    for head in range(heads):
        after = sum(
            jnp.where(seq + 2 * index + 2 < count, ref[head].astype(F32), 0.0)
            for index, ref in enumerate(arrived)
        )
        farthest = jnp.where(is_upper(), row_ref[head], shared_ref[head])
        after = after + jnp.where(seq + 2 * chips < count, farthest.astype(F32), 0.0)
        key, fresh = k_ref[head], u_ref[head]
        k_scale = aux_ref[:, 4 * head + 1 : 4 * head + 2]
        rate = aux_ref[:, 4 * head + 2 : 4 * head + 3]
        slope = aux_ref[:, 4 * head + 3 : 4 * head + 4]
        y = y_ref[head] + mm(reach_ref[head], after)
        both = mm_nt(y, jnp.concatenate([state_ref[head], fresh], axis=0))
        from_state = -carried * both[:, :dk]
        system = strict * -both[:, dk:]
        scaled = rate * system
        dkey = dk0_ref[head] + mm_nt(mm_nt(final * fresh, after), suffix_t_ref[head])
        dkey = dkey + mm(scaled + scaled.T, key) + rate * from_state
        drate = jnp.sum(
            system * gram_ref[head] + from_state * key + y * v_ref[head], axis=1, keepdims=True
        )
        logit_grad = jnp.where(lane == head, drate * slope, logit_grad)
        along = jnp.sum(key * dkey, axis=1, keepdims=True)
        key_grads.append((k_scale * (dkey - key * along)).astype(BF16))
        value_grads.append((rate * y).astype(BF16))
    grads_ref[...] = jnp.concatenate(
        [gq_ref[...]] + key_grads + value_grads + [logit_grad.astype(BF16)], axis=1
    )
    others, halos = outs[: kinds - 1], outs[kinds - 1 :]
    for turn in range(1, kinds):
        back_products(grads_ref, weights, turn, kinds, others[turn - 1], halos[turn - 1])


def back_products(grads_ref, weights, turn, kinds, sum_ref, halo_ref):
    local = sum_ref.shape[1]
    width = min(512, local)
    for part in range(local // width):
        first = lax.rem(here()[1] + turn, kinds) * local + part * width
        at = pl.ds(pl.multiple_of(first, width), width)
        row, total = 0, 0.0
        for weight in weights:
            total = total + dot(grads_ref[:, row : row + weight.shape[0]], weight[:, at])
            row += weight.shape[0]
        span = slice(part * width, (part + 1) * width)
        halo_ref[:, span] = total[:HALO].astype(BF16)
        sum_ref[:, span] = total.astype(sum_ref.dtype)


def own_back_kernel(kinds, grads_ref, *refs):
    back_products(grads_ref, refs[:4], 0, kinds, *refs[4:])


def finish_kernel(kinds, pick_ref, edge_ref, mine_ref, *refs):
    others, halos = refs[: kinds - 1], refs[kinds - 1 : 2 * kinds - 1]
    out_ref, held_ref, semaphores = refs[-3:]
    parts = pick_ref.shape[0]
    copies = []
    width = mine_ref.shape[1] // parts
    for part in range(parts):
        span = slice(part * width, (part + 1) * width)
        total = mine_ref[:, span]
        for other in others:
            total = total + other[:, span].astype(F32)
        edge = halos[0][:, span].astype(F32)
        for halo in halos[1:]:
            edge = edge + halo[:, span].astype(F32)
        moved = dot(pick_ref[part], total.astype(BF16)) + dot(edge_ref[part], edge.astype(BF16))
        held_ref[:, span] = moved.astype(BF16)
        copies.append(
            pltpu.make_async_copy(held_ref.at[:, span], out_ref.at[:, span], semaphores.at[part])
        )
        copies[-1].start()
    for copy in copies:
        copy.wait()


SMEM = pl.BlockSpec(memory_space=pltpu.SMEM)
VMEM = pl.BlockSpec(memory_space=pltpu.VMEM)


def call(body, name, scalars, arrays, outs, flops=0, out_space=VMEM, scratch=()):
    moved = sum(a.size * a.dtype.itemsize for a in arrays)
    moved += sum(o.size * o.dtype.itemsize for o in outs)
    return pl.pallas_call(
        body,
        name=name,
        out_shape=tuple(outs),
        in_specs=[SMEM] * len(scalars) + [VMEM] * len(arrays),
        out_specs=tuple([out_space] * len(outs)),
        scratch_shapes=list(scratch),
        cost_estimate=pl.CostEstimate(flops=flops, bytes_accessed=moved, transcendentals=0),
        compiler_params=pltpu.CompilerParams(vmem_limit_bytes=VMEM_LIMIT),
    )(*scalars, *arrays)


def shape(dims, kind=F32):
    return jax.ShapeDtypeStruct(tuple(dims), kind)


def row_shift(x, by, rising, count):
    chips = count // 2
    pairs = []
    for chip in range(chips):
        up, down = chip + by, chip - by
        pairs.append((2 * chip + rising, 2 * up + rising if up < chips else 2 * chip + 1 - rising))
        pairs.append((2 * chip + 1 - rising, 2 * down + 1 - rising if down >= 0 else 2 * chip + rising))
    return lax.ppermute(x, "seq", pairs)


def seq_shift(x, by, count):
    return lax.ppermute(x, "seq", [(i, (i + by) % count) for i in range(count)])


def core_swap(x, count):
    return lax.ppermute(x, "seq", [(i, i ^ 1) for i in range(count)])


def corner_shift(x, by, turn, count, kinds):
    pairs = []
    for i in range(count):
        for h in range(kinds):
            pairs.append((i * kinds + h, (i + by) % count * kinds + (h + turn) % kinds))
    return lax.ppermute(x, ("seq", "head"), pairs)


def head_turn(x, turn, kinds):
    return lax.ppermute(x, "head", [(h, (h + turn) % kinds) for h in range(kinds)])


def on_device(loaded, out_grad, w_query, w_key, w_value, w_beta, beta_max, out_gain, clip_lengths,
              delay_offsets, block_order):
    count = lax.axis_size("seq")
    kinds = lax.axis_size("head")
    frames, local = loaded.shape
    rows_each = frames // count
    heads = w_beta.shape[1]
    dk = w_query.shape[1] // heads
    dv = w_value.shape[1] // heads
    chips = count // 8
    group = (local * kinds) // delay_offsets.shape[0]
    parts = local // min(group, local)
    columns = heads * (2 * dk + dv) + LANES
    wb = jnp.pad(w_beta, ((0, 0), (0, LANES - heads)))
    gain = out_gain.reshape(1, dv)

    received = lax.all_to_all(
        loaded.reshape(count, rows_each, local), "seq", split_axis=0, concat_axis=0, tiled=True
    ).reshape(frames, local)
    prepared = call(
        functools.partial(prepare_kernel, kinds, local),
        "prepare",
        [block_order, clip_lengths, delay_offsets, beta_max],
        [],
        [
            shape((kinds * parts, frames, frames), BF16),
            shape((kinds * parts, frames, HALO), BF16),
            shape((HALO, frames), BF16),
            shape((parts, frames, frames), BF16),
            shape((parts, frames, HALO), BF16),
            shape((5, frames, frames)),
            shape((heads, 1, LANES)),
        ],
    )
    received, wb, *prepared = lax.optimization_barrier((received, wb, *prepared))
    pick, edge, last, back_pick, back_edge, masks, caps = prepared
    tail = jnp.dot(last, received, preferred_element_type=F32).astype(BF16)
    pieces = [head_turn(received, turn, kinds) for turn in range(1, kinds)]
    halos = [corner_shift(tail, 1, turn, count, kinds) for turn in range(kinds)]
    weights = [w_query, w_key, w_value, wb]
    sums = call(
        functools.partial(own_kernel, kinds),
        "project_own",
        [],
        [received, pick, edge] + weights,
        [shape((frames, weight.shape[1])) for weight in weights],
        flops=2 * frames * local * columns,
    )
    first = call(
        functools.partial(own_halo_kernel, kinds),
        "project_halo",
        [],
        [halos[0], edge] + weights,
        [shape((REACH, weight.shape[1])) for weight in weights],
        flops=2 * REACH * local * columns,
    )
    flipped = call(
        flip_kernel, "flip", [], weights, [shape(w.shape[::-1], BF16) for w in weights]
    )
    sums, first, flipped = lax.optimization_barrier((sums, first, flipped))

    square = shape((heads, frames, dk))
    values = shape((heads, frames, dv))
    times = shape((heads, frames, frames))
    maps = shape((heads, dk, dk + dv), BF16)
    moves = shape((heads, dk, dk))
    states = shape((heads, dk, dv))
    offsets = shape((heads, dk, dv), BF16)
    affine, q, k, v, solve, solved, aux = call(
        functools.partial(project_kernel, heads, kinds),
        "project",
        [],
        [masks, caps] + list(sums) + list(first) + pieces + halos[1:] + [pick, edge] + weights,
        [maps, square, square, values, times, shape((heads, frames, dk + dv)),
         shape((frames, LANES))],
        flops=2 * frames * local * columns,
    )
    results = call(
        functools.partial(join_kernel, heads, chips),
        "join",
        [],
        [affine, core_swap(affine, count)],
        [maps if chips > 1 else offsets, maps, shape(moves.shape, BF16), shape(moves.shape, BF16)]
        + [offsets] * (chips > 1),
        flops=10**7,
    )
    joined, prefix, suffix, early = results[:4]
    arrived = [row_shift(joined, by, (by - 1) % 2, count) for by in range(1, chips)]
    arrived.append(row_shift(results[-1], chips, (chips - 1) % 2, count))
    local_terms = call(
        functools.partial(local_kernel, heads),
        "local_terms",
        [],
        [masks, q, k, solved, solve, early, suffix, prefix, gain, out_grad],
        [times, square, shape((heads, dk, frames)), values, times, times, square, moves, moves,
         values, shape((1, dv))],
        flops=2 * 10**8,
    )
    arrived, local_terms = lax.optimization_barrier((arrived, local_terms))
    (score_t, reach, reach_t, local_out, solve_t, gram, spread, early_t, suffix_t, weighted,
     gains) = local_terms
    swapped = []
    for at in range(0, chips, 2):
        (give,) = call(
            functools.partial(give_kernel, heads), "give", [], arrived[at : at + 2], [maps],
        )
        swapped.append(core_swap(give, count))
    results = call(
        functools.partial(output_kernel, heads, chips),
        "outputs",
        [],
        arrived + swapped + [prefix, reach, reach_t, local_out, weighted],
        [states, values, values, states, offsets] + [moves] * (chips - 1),
        flops=2 * 10**8,
    )
    state, unit, dout, back, send = results[:5]
    results = call(
        functools.partial(join_back_kernel, heads, chips),
        "join_back",
        [],
        [back, core_swap(send, count), early_t] + list(results[5:]),
        [states] + [offsets] * chips,
        flops=10**7,
    )
    later = results[0]
    arrived = [seq_shift(x, -2 * by, count) for by, x in enumerate(results[1:-1], 1)]
    farthest = row_shift(results[-1], chips, 0, count)
    query_terms = call(
        functools.partial(query_kernel, heads),
        "query_grad",
        [],
        [masks, dout, state, solved, score_t, q, k, solve_t, aux, unit, gains, spread, suffix_t,
         later],
        [shape((frames, heads * dv), BF16), shape((frames, heads * dk), BF16), values, values,
         square, square],
        flops=2 * 10**8,
    )
    farthest, query_terms = lax.optimization_barrier((farthest, query_terms))
    head_out, gq, fresh, y, dkey, reach = query_terms
    arrived += [farthest, core_swap(farthest, count)]
    results = call(
        functools.partial(key_kernel, heads, kinds, chips, count),
        "key_grad",
        [],
        [masks] + arrived + [suffix_t, reach, gq, fresh, y, dkey, state, k, v, gram, aux] + list(flipped),
        [shape((frames, local), BF16)] * (kinds - 1)
        + [shape((HALO, local), BF16)] * (kinds - 1)
        + [shape((frames, columns), BF16)],
        flops=2 * 10**8,
    )
    others, edges, grads = results[: kinds - 1], results[kinds - 1 : -1], results[-1]
    mine, edge = call(
        functools.partial(own_back_kernel, kinds),
        "own_back",
        [],
        [grads] + list(flipped),
        [shape((frames, local)), shape((HALO, local), BF16)],
        flops=2 * frames * local * columns,
    )
    others = [head_turn(x, turn, kinds) for turn, x in enumerate(others, 1)]
    edges = [corner_shift(x, -1, turn, count, kinds) for turn, x in enumerate([edge] + list(edges))]
    (input_grad,) = call(
        functools.partial(finish_kernel, kinds),
        "finish",
        [],
        [back_pick, back_edge, mine] + others + edges,
        [shape((frames, local), BF16)],
        flops=10**8,
        out_space=pl.BlockSpec(memory_space=pl.ANY),
        scratch=[pltpu.VMEM((frames, local), BF16), pltpu.SemaphoreType.DMA((parts,))],
    )
    return head_out, input_grad


def solution(mesh):
    return jax.shard_map(
        on_device,
        mesh=mesh,
        in_specs=(
            P("seq", "head"),
            P("seq", "head"),
            P(None, "head"),
            P(None, "head"),
            P(None, "head"),
            P(None, "head"),
            P("head"),
            P(),
            P(),
            P(),
            P("seq", None),
        ),
        out_specs=(P("seq", "head"), P("seq", "head")),
        check_vma=False,
    )
```

```python
import functools

import jax
import jax.numpy as jnp
from jax import lax
from jax.experimental import pallas as pl
from jax.experimental.pallas import tpu as pltpu
from jax.sharding import PartitionSpec as P

EPSILON = 1e-06
F32 = jnp.float32
BF16 = jnp.bfloat16
HALO = 8
REACH = 16
LANES = 128
VMEM_LIMIT = 16 * 1024 * 1024


def halves(x):
    high = x.astype(BF16)
    return high, (x - high.astype(F32)).astype(BF16)


def dot(a, b):
    return jnp.dot(a, b, preferred_element_type=F32)


def dot_nt(a, b):
    return lax.dot_general(a, b, (((1,), (1,)), ((), ())), preferred_element_type=F32)


def mm(a, b):
    width = b.shape[1]
    b_high, b_low = halves(b)
    right = jnp.concatenate([b_high, b_low], axis=1)
    if a.dtype == BF16:
        both = dot(a, right)
    else:
        left = jnp.concatenate(halves(a), axis=1)
        both = dot(left, jnp.concatenate([right, right], axis=0))
    return both[:, :width] + both[:, width:]


def mm_nt(a, b):
    width = b.shape[0]
    left = jnp.concatenate(halves(a), axis=1)
    right = jnp.concatenate(halves(b), axis=0)
    both = dot_nt(left, jnp.concatenate([right, right], axis=1))
    return both[:, :width] + both[:, width:]


def rough(a, b):
    return dot(a.astype(BF16), b.astype(BF16))


def rough_nt(a, b):
    return dot_nt(a.astype(BF16), b.astype(BF16))


def begins(clips_ref, position):
    end = 0
    total = jnp.zeros_like(position)
    for clip in range(clips_ref.shape[0]):
        length = clips_ref[clip]
        end = end + length
        total = total + jnp.where(end <= position, length, 0)
    return total


def here():
    return lax.axis_index("seq"), lax.axis_index("head")


def solve_unit(low, right):
    size = low[0].shape[0]
    row = lax.broadcasted_iota(jnp.int32, (size, size), 0)
    col = lax.broadcasted_iota(jnp.int32, (size, size), 1)
    eye = jnp.where(row == col, 1.0, 0.0).astype(F32)

    def within(width):
        return (row // width) == (col // width)

    def wide_products(lefts, *rights):
        results = []
        for left, *several in zip(lefts, *rights):
            both, at, parts = mm(left, jnp.concatenate(several, axis=1)), 0, []
            for one in several:
                parts.append(both[:, at : at + one.shape[1]])
                at += one.shape[1]
            results.append(parts)
        return [list(part) for part in zip(*results)]

    block = 2
    inverse = [eye - jnp.where(within(block), x, 0.0) for x in low]
    while block < size:
        wide = min(8 * block, size)
        ring = within(wide) & jnp.logical_not(within(block))
        rest = [jnp.where(ring, n, 0.0) for n in low]
        if wide < size:
            (step,) = wide_products(inverse, rest)
            start = inverse
        else:
            step, solved = wide_products(inverse, rest, right)
            start = [jnp.concatenate(both, axis=1) for both in zip(inverse, solved)]
        square, moved = wide_products(step, step, start)
        start = [x - m for x, m in zip(start, moved)]
        fourth, moved = wide_products(square, square, start)
        start = [x + m for x, m in zip(start, moved)]
        inverse = [x + mm(f, x) for f, x in zip(fourth, start)]
        block = wide
    return [x[:, :size] for x in inverse], [x[:, size:] for x in inverse]


def prepare_kernel(kinds, local, order_ref, clips_ref, delays_ref, cap_ref, pick_ref, edge_ref, last_ref,
                   back_pick_ref, back_edge_ref, mask_ref, caps_ref):
    seq, head = here()
    frames = pick_ref.shape[1]
    parts = pick_ref.shape[0] // kinds
    width = local // parts
    group = (local * kinds) // delays_ref.shape[0]
    sources = order_ref.shape[1]
    rows_each = frames // sources
    base = seq * frames
    row = lax.broadcasted_iota(jnp.int32, (frames, frames), 0)
    col = lax.broadcasted_iota(jnp.int32, (frames, frames), 1)
    row_begin = begins(clips_ref, base + row) - base
    col_begin = begins(clips_ref, base + col[:1]) - base
    last_begin = begins(clips_ref, base + frames - 1) - base
    same = row_begin == col_begin
    carried_last = jnp.where(last_begin < 0, 1.0, 0.0)
    mask_ref[0] = jnp.where((row > col) & same, 1.0, 0.0).astype(F32)
    mask_ref[1] = jnp.where((row >= col) & same, 1.0, 0.0).astype(F32)
    mask_ref[2] = jnp.where(row_begin < 0, 1.0, 0.0).astype(F32)
    mask_ref[3] = jnp.where(row_begin == last_begin, 1.0, 0.0).astype(F32)
    mask_ref[4] = jnp.where(row == col, carried_last, 0.0).astype(F32)
    for index in range(caps_ref.shape[0]):
        caps_ref[index] = jnp.full(caps_ref.shape[1:], cap_ref[index], F32)
    lane = col[:1]
    landing = jnp.zeros((1, frames), jnp.int32)
    for source in range(sources):
        at = order_ref[0, source] * rows_each + (lane - source * rows_each)
        landing = jnp.where(lane // rows_each == source, at, landing)
    edge_row = row[:, :HALO]
    edge_col = lax.broadcasted_iota(jnp.int32, (frames, HALO), 1)
    last_ref[...] = jnp.where(landing == row[:HALO] + (frames - HALO), 1.0, 0.0).astype(BF16)
    for kind in range(kinds):
        owner = lax.rem(head + kinds - kind, kinds)
        for part in range(parts):
            source_row = row - delays_ref[(owner * local + part * width) // group]
            inside = source_row >= row_begin
            pick = jnp.where((landing == source_row) & inside, 1.0, 0.0).astype(BF16)
            pick_ref[kind * parts + part] = pick
            edge = (edge_col - HALO == source_row[:, :HALO]) & inside[:, :HALO]
            edge_ref[kind * parts + part] = jnp.where(edge, 1.0, 0.0).astype(BF16)
    edge_begin = begins(clips_ref, base + frames + edge_col[:1]) - base
    for part in range(parts):
        delay = delays_ref[(head * local + part * width) // group]
        pick = jnp.where((col == row + delay) & (col_begin <= row), 1.0, 0.0).astype(BF16)
        back_pick_ref[part] = pick
        edge = (edge_col + frames == edge_row + delay) & (edge_begin <= edge_row)
        back_edge_ref[part] = jnp.where(edge, 1.0, 0.0).astype(BF16)


def flip_kernel(*refs):
    for ref, out_ref in zip(refs[:4], refs[4:]):
        out_ref[...] = ref[...].T


def add_products(sums, kind, kinds, piece_ref, halo_ref, pick_ref, edge_ref, weights):
    local = halo_ref.shape[1] if piece_ref is None else piece_ref.shape[1]
    parts = pick_ref.shape[0] // kinds
    width = local // parts
    owner = lax.rem(here()[1] + kinds - kind, kinds)
    for part in range(parts):
        span = slice(part * width, (part + 1) * width)
        index = kind * parts + part
        if piece_ref is None:
            delayed = dot(edge_ref[index, :REACH], halo_ref[:, span])
        else:
            delayed = dot(pick_ref[index], piece_ref[:, span])
            if halo_ref is not None:
                delayed = delayed + dot(edge_ref[index], halo_ref[:, span])
        at = pl.ds(pl.multiple_of(owner * local + part * width, width), width)
        delayed = delayed.astype(BF16)
        new = [dot(delayed, weight[at, :]) for weight in weights]
        sums = new if sums is None else [a + b for a, b in zip(sums, new)]
    return sums


def own_kernel(kinds, piece_ref, pick_ref, edge_ref, *refs):
    sums = add_products(None, 0, kinds, piece_ref, None, pick_ref, edge_ref, refs[:4])
    for ref, part in zip(refs[4:], sums):
        ref[...] = part


def own_halo_kernel(kinds, halo_ref, edge_ref, *refs):
    sums = add_products(None, 0, kinds, None, halo_ref, edge_ref, edge_ref, refs[:4])
    for ref, part in zip(refs[4:], sums):
        ref[...] = part


def project_kernel(heads, kinds, mask_ref, cap_ref, *refs):
    sums, first, refs = [ref[...] for ref in refs[:4]], [ref[...] for ref in refs[4:8]], refs[8:]
    pieces, halos = refs[: kinds - 1], refs[kinds - 1 : 2 * kinds - 2]
    pick_ref, edge_ref = refs[2 * kinds - 2 : 2 * kinds]
    weights = refs[2 * kinds : 2 * kinds + 4]
    map_ref, q_ref, k_ref, v_ref, solve_ref, w_ref, aux_ref = refs[2 * kinds + 4 :]
    frames = sums[0].shape[0]
    strict, carried, final, eye = mask_ref[0], mask_ref[2], mask_ref[3], mask_ref[4]
    sums = [jnp.concatenate([x[:REACH] + a, x[REACH:]], axis=0) for x, a in zip(sums, first)]
    for kind in range(1, kinds):
        sums = add_products(
            sums, kind, kinds, pieces[kind - 1], halos[kind - 1], pick_ref, edge_ref, weights
        )
    q_all, k_all, v_all, logit_all = sums
    dk = q_all.shape[1] // heads
    dv = v_all.shape[1] // heads
    keys, rights, lows = [], [], []
    aux = jnp.zeros((frames, LANES), F32)
    aux_lane = lax.broadcasted_iota(jnp.int32, (frames, LANES), 1)
    for head in range(heads):
        q_raw = q_all[:, head * dk : (head + 1) * dk]
        k_raw = k_all[:, head * dk : (head + 1) * dk]
        value = v_all[:, head * dv : (head + 1) * dv]
        q_scale = lax.rsqrt(jnp.sum(q_raw * q_raw, axis=1, keepdims=True) + EPSILON)
        k_scale = lax.rsqrt(jnp.sum(k_raw * k_raw, axis=1, keepdims=True) + EPSILON)
        gate = 1.0 / (1.0 + jnp.exp(-logit_all[:, head : head + 1]))
        rate = cap_ref[head, :, :1] * gate
        key = k_raw * k_scale
        q_ref[head] = q_raw * q_scale
        k_ref[head] = key
        v_ref[head] = value
        for index, item in enumerate((q_scale, k_scale, rate, rate * (1.0 - gate))):
            aux = jnp.where(aux_lane == 4 * head + index, item, aux)
        gram = mm_nt(key, key)
        lows.append(strict * (rate * gram))
        keys.append(key)
        rights.append(rate * jnp.concatenate([key, value], axis=1))
    aux_ref[...] = aux
    solves, solutions = solve_unit(lows, rights)
    for head in range(heads):
        solved = solutions[head]
        solve_ref[head] = solves[head]
        w_ref[head] = solved
        ended = jnp.concatenate(
            [-(final * carried) * solved[:, :dk], final * solved[:, dk:]], axis=1
        )
        affine = mm(keys[head].T, ended)
        map_ref[head, :, :dk] = (affine[:, :dk] + eye).astype(BF16)
        map_ref[head, :, dk:] = affine[:, dk:].astype(BF16)


def local_kernel(heads, mask_ref, q_ref, k_ref, w_ref, solve_ref, early_ref, suffix_ref, prefix_ref,
                 gain_ref, grad_ref, score_t_ref, reach_ref, reach_t_ref, local_ref, solve_t_ref,
                 gram_ref, spread_ref, early_t_ref, suffix_t_ref, weighted_ref, gains_ref):
    frames, dk = q_ref.shape[1:]
    lower, carried, final = mask_ref[1], mask_ref[2], mask_ref[3]
    gains_ref[...] = gain_ref[...]
    for head in range(heads):
        query, key, solved = q_ref[head], k_ref[head], w_ref[head]
        scores = lower * mm_nt(query, key)
        both = mm(scores, solved)
        reach = carried * (query - both[:, :dk])
        score_t_ref[head] = scores.T
        prefix = prefix_ref[head]
        reach_t_ref[head] = reach.T
        grown = mm(reach, prefix.astype(F32))
        reach_ref[head] = grown[:, :dk]
        local_ref[head] = both[:, dk:] + grown[:, dk:]
        solve_t = solve_ref[head].T
        solve_t_ref[head] = solve_t
        gram_ref[head] = mm_nt(key, key)
        spread_ref[head] = mm(solve_t, final * key)
        early_t_ref[head] = early_ref[head].astype(F32).T
        suffix_t_ref[head] = suffix_ref[head].astype(F32).T
        dv = local_ref.shape[2]
        weighted_ref[head] = grad_ref[:, head * dv : (head + 1) * dv].astype(F32) * gain_ref[...]


def is_upper():
    return lax.rem(here()[0], 2) == 1


def join_kernel(heads, chips, own_ref, other_ref, *refs):
    joined_ref, prefix_ref, suffix_ref, early_ref = refs[:4]
    dk = own_ref.shape[1]
    upper = is_upper()
    row = lax.broadcasted_iota(jnp.int32, (dk, dk), 0)
    col = lax.broadcasted_iota(jnp.int32, (dk, dk), 1)
    eye = jnp.where(row == col, 1.0, 0.0)
    for head in range(heads):
        own, other = own_ref[head].astype(F32), other_ref[head].astype(F32)
        early = jnp.where(upper, other, own)
        late = jnp.where(upper, own, other)
        both = dot(late[:, :dk].astype(BF16), early.astype(BF16))
        offset = (both[:, dk:] + late[:, dk:]).astype(BF16)
        if chips > 1:
            joined_ref[head, :, :dk] = both[:, :dk].astype(BF16)
            joined_ref[head, :, dk:] = offset
            refs[4][head] = offset
        else:
            joined_ref[head] = offset
        early_ref[head] = early[:, :dk].astype(BF16)
        prefix_ref[head, :, :dk] = jnp.where(upper, other[:, :dk], eye).astype(BF16)
        prefix_ref[head, :, dk:] = jnp.where(upper, other[:, dk:], 0.0).astype(BF16)
        suffix_ref[head] = jnp.where(upper, eye, other[:, :dk]).astype(BF16)


def give_kernel(heads, even_ref, odd_ref, give_ref):
    upper = is_upper()
    width = odd_ref.shape[2]
    for head in range(heads):
        odd = odd_ref[head].astype(F32)
        even = even_ref[head].astype(F32)
        give_ref[head, :, -width:] = jnp.where(upper, odd, even[:, -width:]).astype(BF16)
        if width < even.shape[1]:
            give_ref[head, :, :-width] = even_ref[head, :, :-width]


def output_kernel(heads, chips, *refs):
    rows, swapped, refs = refs[:chips], refs[chips : chips + chips // 2], refs[chips + chips // 2 :]
    maps = []
    upper = is_upper()
    for index, row in enumerate(rows):
        other = swapped[index // 2]
        width = row.shape[2]
        mine = upper if index % 2 else jnp.logical_not(upper)
        maps.append([
            jnp.where(mine, row[head].astype(F32), other[head, :, -width:].astype(F32))
            for head in range(heads)
        ])
    (prefix_ref, reach_ref, reach_t_ref, local_ref, weighted_ref,
     state_ref, unit_ref, dout_ref, back_ref, send_ref) = refs[:10]
    flipped = refs[10:]
    seq = here()[0]
    dk = reach_ref.shape[2]
    for head in range(heads):
        state = jnp.where(seq >= 2 * chips, maps[-1][head], 0.0)
        for index in range(chips - 2, -1, -1):
            earlier = maps[index][head]
            step = rough if index == chips - 2 else mm
            state = earlier[:, dk:] + step(earlier[:, :dk].astype(BF16), state)
            state = jnp.where(seq >= 2 * index + 2, state, 0.0)
        raw = local_ref[head] + mm(reach_ref[head], state)
        state_ref[head] = prefix_ref[head, :, dk:].astype(F32) + mm(prefix_ref[head, :, :dk], state)
        scale = lax.rsqrt(jnp.mean(raw * raw, axis=1, keepdims=True) + EPSILON)
        unit = raw * scale
        unit_ref[head] = unit
        weighted = weighted_ref[head]
        dout = scale * (weighted - unit * jnp.mean(unit * weighted, axis=1, keepdims=True))
        dout_ref[head] = dout
        back = rough(reach_t_ref[head], dout)
        back_ref[head] = back
        send_ref[head] = back.astype(BF16)
        product = None
        for earlier, flip_ref in zip(maps, flipped):
            move = earlier[head][:, :dk]
            product = move if product is None else mm(product, move)
            flip_ref[head] = product.T


def join_back_kernel(heads, chips, own_ref, other_ref, early_t_ref, *refs):
    flipped, later_ref, sends = refs[: chips - 1], refs[chips - 1], refs[chips:]
    upper = is_upper()
    for head in range(heads):
        own, other = own_ref[head], other_ref[head].astype(F32)
        late = jnp.where(upper, own, other)
        joined = jnp.where(upper, other, own) + mm(early_t_ref[head].astype(BF16), late)
        later_ref[head] = jnp.where(upper, 0.0, other)
        sends[0][head] = joined.astype(BF16)
        for flip_ref, send in zip(flipped, sends[1:]):
            send[head] = rough(flip_ref[head], joined).astype(BF16)


def query_kernel(heads, mask_ref, dout_ref, state_ref, w_ref, score_t_ref, q_ref, k_ref, solve_t_ref,
                 aux_ref, unit_ref, gain_ref, spread_ref, suffix_t_ref, later_ref,
                 out_ref, gq_ref, u_ref, y_ref, dk_ref, reach_ref):
    frames, dk = q_ref.shape[1:]
    lower, carried, final = mask_ref[1], mask_ref[2], mask_ref[3]
    for head in range(heads):
        dv = unit_ref.shape[2]
        out_ref[:, head * dv : (head + 1) * dv] = (unit_ref[head] * gain_ref[...]).astype(BF16)
        dout, state, solved = dout_ref[head], state_ref[head], w_ref[head]
        query, key = q_ref[head], k_ref[head]
        fresh = solved[:, dk:] - carried * mm(solved[:, :dk], state)
        u_ref[head] = fresh
        later, suffix_t = later_ref[head], suffix_t_ref[head]
        ended = final * fresh
        reach = mm(spread_ref[head], jnp.concatenate([later, suffix_t], axis=1))
        reach_ref[head] = reach[:, dv:]
        y_ref[head] = mm(solve_t_ref[head], mm(score_t_ref[head], dout)) + reach[:, :dv]
        flow = lower * mm_nt(dout, fresh)
        dquery = carried * mm_nt(dout, state) + mm(flow, key)
        dk_ref[head] = mm(flow.T, query) + mm_nt(ended, later)
        scale = aux_ref[:, 4 * head : 4 * head + 1]
        along = jnp.sum(query * dquery, axis=1, keepdims=True)
        gq_ref[:, head * dk : (head + 1) * dk] = (scale * (dquery - query * along)).astype(BF16)


def key_kernel(heads, kinds, chips, count, mask_ref, *refs):
    arrived, refs = refs[:chips], refs[chips:]
    (suffix_t_ref, reach_ref, gq_ref, u_ref, y_ref, dk0_ref, state_ref, k_ref, v_ref, gram_ref,
     aux_ref), refs = refs[:11], refs[11:]
    seq = here()[0]
    weights, refs = refs[:4], refs[4:]
    outs, grads_ref = refs[:-1], refs[-1]
    frames, dk = k_ref.shape[1:]
    strict, carried, final = mask_ref[0], mask_ref[2], mask_ref[3]
    key_grads, value_grads = [], []
    lane = lax.broadcasted_iota(jnp.int32, (frames, LANES), 1)
    logit_grad = jnp.zeros((frames, LANES), F32)
    for head in range(heads):
        after = sum(
            jnp.where(seq + 2 * index + 2 < count, ref[head].astype(F32), 0.0)
            for index, ref in enumerate(arrived)
        )
        key, fresh = k_ref[head], u_ref[head]
        k_scale = aux_ref[:, 4 * head + 1 : 4 * head + 2]
        rate = aux_ref[:, 4 * head + 2 : 4 * head + 3]
        slope = aux_ref[:, 4 * head + 3 : 4 * head + 4]
        y = y_ref[head] + rough(reach_ref[head], after)
        both = rough_nt(y, jnp.concatenate([state_ref[head], fresh], axis=0))
        from_state = -carried * both[:, :dk]
        system = strict * -both[:, dk:]
        scaled = rate * system
        dkey = dk0_ref[head] + rough_nt(rough_nt(final * fresh, after), suffix_t_ref[head])
        dkey = dkey + rough(scaled + scaled.T, key) + rate * from_state
        drate = jnp.sum(
            system * gram_ref[head] + from_state * key + y * v_ref[head], axis=1, keepdims=True
        )
        logit_grad = jnp.where(lane == head, drate * slope, logit_grad)
        along = jnp.sum(key * dkey, axis=1, keepdims=True)
        key_grads.append((k_scale * (dkey - key * along)).astype(BF16))
        value_grads.append((rate * y).astype(BF16))
    grads_ref[...] = jnp.concatenate(
        [gq_ref[...]] + key_grads + value_grads + [logit_grad.astype(BF16)], axis=1
    )
    others, halos = outs[: kinds - 1], outs[kinds - 1 :]
    for turn in range(1, kinds):
        back_products(grads_ref, weights, turn, kinds, others[turn - 1], halos[turn - 1])


def back_products(grads_ref, weights, turn, kinds, sum_ref, halo_ref):
    local = sum_ref.shape[1]
    width = min(512, local)
    for part in range(local // width):
        first = lax.rem(here()[1] + turn, kinds) * local + part * width
        at = pl.ds(pl.multiple_of(first, width), width)
        row, total = 0, 0.0
        for weight in weights:
            total = total + dot(grads_ref[:, row : row + weight.shape[0]], weight[:, at])
            row += weight.shape[0]
        span = slice(part * width, (part + 1) * width)
        halo_ref[:, span] = total[:HALO].astype(BF16)
        sum_ref[:, span] = total.astype(sum_ref.dtype)


def own_back_kernel(kinds, grads_ref, *refs):
    back_products(grads_ref, refs[:4], 0, kinds, *refs[4:])


def finish_kernel(kinds, pick_ref, edge_ref, mine_ref, *refs):
    others, halos = refs[: kinds - 1], refs[kinds - 1 : 2 * kinds - 1]
    out_ref, held_ref, semaphores = refs[-3:]
    parts = pick_ref.shape[0]
    copies = []
    width = mine_ref.shape[1] // parts
    for part in range(parts):
        span = slice(part * width, (part + 1) * width)
        total = mine_ref[:, span]
        for other in others:
            total = total + other[:, span].astype(F32)
        edge = halos[0][:, span].astype(F32)
        for halo in halos[1:]:
            edge = edge + halo[:, span].astype(F32)
        moved = dot(pick_ref[part], total.astype(BF16)) + dot(edge_ref[part], edge.astype(BF16))
        held_ref[:, span] = moved.astype(BF16)
        copies.append(
            pltpu.make_async_copy(held_ref.at[:, span], out_ref.at[:, span], semaphores.at[part])
        )
        copies[-1].start()
    for copy in copies:
        copy.wait()


SMEM = pl.BlockSpec(memory_space=pltpu.SMEM)
VMEM = pl.BlockSpec(memory_space=pltpu.VMEM)


def call(body, name, scalars, arrays, outs, flops=0, out_space=VMEM, scratch=()):
    moved = sum(a.size * a.dtype.itemsize for a in arrays)
    moved += sum(o.size * o.dtype.itemsize for o in outs)
    return pl.pallas_call(
        body,
        name=name,
        out_shape=tuple(outs),
        in_specs=[SMEM] * len(scalars) + [VMEM] * len(arrays),
        out_specs=tuple([out_space] * len(outs)),
        scratch_shapes=list(scratch),
        cost_estimate=pl.CostEstimate(flops=flops, bytes_accessed=moved, transcendentals=0),
        compiler_params=pltpu.CompilerParams(vmem_limit_bytes=VMEM_LIMIT),
    )(*scalars, *arrays)


def shape(dims, kind=F32):
    return jax.ShapeDtypeStruct(tuple(dims), kind)


def row_shift(x, by, rising, count):
    chips = count // 2
    pairs = []
    for chip in range(chips):
        up, down = chip + by, chip - by
        pairs.append((2 * chip + rising, 2 * up + rising if up < chips else 2 * chip + 1 - rising))
        pairs.append((2 * chip + 1 - rising, 2 * down + 1 - rising if down >= 0 else 2 * chip + rising))
    return lax.ppermute(x, "seq", pairs)


def seq_shift(x, by, count):
    return lax.ppermute(x, "seq", [(i, (i + by) % count) for i in range(count)])


def core_swap(x, count):
    return lax.ppermute(x, "seq", [(i, i ^ 1) for i in range(count)])


def corner_shift(x, by, turn, count, kinds):
    pairs = []
    for i in range(count):
        for h in range(kinds):
            pairs.append((i * kinds + h, (i + by) % count * kinds + (h + turn) % kinds))
    return lax.ppermute(x, ("seq", "head"), pairs)


def head_turn(x, turn, kinds):
    return lax.ppermute(x, "head", [(h, (h + turn) % kinds) for h in range(kinds)])


def on_device(loaded, out_grad, w_query, w_key, w_value, w_beta, beta_max, out_gain, clip_lengths,
              delay_offsets, block_order):
    count = lax.axis_size("seq")
    kinds = lax.axis_size("head")
    frames, local = loaded.shape
    rows_each = frames // count
    heads = w_beta.shape[1]
    dk = w_query.shape[1] // heads
    dv = w_value.shape[1] // heads
    chips = count // 8
    group = (local * kinds) // delay_offsets.shape[0]
    parts = local // min(group, local)
    columns = heads * (2 * dk + dv) + LANES
    wb = jnp.pad(w_beta, ((0, 0), (0, LANES - heads)))
    gain = out_gain.reshape(1, dv)

    received = lax.all_to_all(
        loaded.reshape(count, rows_each, local), "seq", split_axis=0, concat_axis=0, tiled=True
    ).reshape(frames, local)
    prepared = call(
        functools.partial(prepare_kernel, kinds, local),
        "prepare",
        [block_order, clip_lengths, delay_offsets, beta_max],
        [],
        [
            shape((kinds * parts, frames, frames), BF16),
            shape((kinds * parts, frames, HALO), BF16),
            shape((HALO, frames), BF16),
            shape((parts, frames, frames), BF16),
            shape((parts, frames, HALO), BF16),
            shape((5, frames, frames)),
            shape((heads, 1, LANES)),
        ],
    )
    received, wb, *prepared = lax.optimization_barrier((received, wb, *prepared))
    pick, edge, last, back_pick, back_edge, masks, caps = prepared
    tail = jnp.dot(last, received, preferred_element_type=F32).astype(BF16)
    pieces = [head_turn(received, turn, kinds) for turn in range(1, kinds)]
    halos = [corner_shift(tail, 1, turn, count, kinds) for turn in range(kinds)]
    weights = [w_query, w_key, w_value, wb]
    sums = call(
        functools.partial(own_kernel, kinds),
        "project_own",
        [],
        [received, pick, edge] + weights,
        [shape((frames, weight.shape[1])) for weight in weights],
        flops=2 * frames * local * columns,
    )
    first = call(
        functools.partial(own_halo_kernel, kinds),
        "project_halo",
        [],
        [halos[0], edge] + weights,
        [shape((REACH, weight.shape[1])) for weight in weights],
        flops=2 * REACH * local * columns,
    )
    flipped = call(
        flip_kernel, "flip", [], weights, [shape(w.shape[::-1], BF16) for w in weights]
    )
    sums, first, flipped = lax.optimization_barrier((sums, first, flipped))

    square = shape((heads, frames, dk))
    values = shape((heads, frames, dv))
    times = shape((heads, frames, frames))
    maps = shape((heads, dk, dk + dv), BF16)
    moves = shape((heads, dk, dk))
    states = shape((heads, dk, dv))
    offsets = shape((heads, dk, dv), BF16)
    affine, q, k, v, solve, solved, aux = call(
        functools.partial(project_kernel, heads, kinds),
        "project",
        [],
        [masks, caps] + list(sums) + list(first) + pieces + halos[1:] + [pick, edge] + weights,
        [maps, square, square, values, times, shape((heads, frames, dk + dv)),
         shape((frames, LANES))],
        flops=2 * frames * local * columns,
    )
    results = call(
        functools.partial(join_kernel, heads, chips),
        "join",
        [],
        [affine, core_swap(affine, count)],
        [maps if chips > 1 else offsets, maps, shape(moves.shape, BF16), shape(moves.shape, BF16)]
        + [offsets] * (chips > 1),
        flops=10**7,
    )
    joined, prefix, suffix, early = results[:4]
    arrived = [row_shift(joined, by, (by - 1) % 2, count) for by in range(1, chips)]
    arrived.append(row_shift(results[-1], chips, (chips - 1) % 2, count))
    local_terms = call(
        functools.partial(local_kernel, heads),
        "local_terms",
        [],
        [masks, q, k, solved, solve, early, suffix, prefix, gain, out_grad],
        [times, square, shape((heads, dk, frames)), values, times, times, square, moves, moves,
         values, shape((1, dv))],
        flops=2 * 10**8,
    )
    arrived, local_terms = lax.optimization_barrier((arrived, local_terms))
    (score_t, reach, reach_t, local_out, solve_t, gram, spread, early_t, suffix_t, weighted,
     gains) = local_terms
    swapped = []
    for at in range(0, chips, 2):
        (give,) = call(
            functools.partial(give_kernel, heads), "give", [], arrived[at : at + 2], [maps],
        )
        swapped.append(core_swap(give, count))
    results = call(
        functools.partial(output_kernel, heads, chips),
        "outputs",
        [],
        arrived + swapped + [prefix, reach, reach_t, local_out, weighted],
        [states, values, values, states, offsets] + [moves] * (chips - 1),
        flops=2 * 10**8,
    )
    state, unit, dout, back, send = results[:5]
    results = call(
        functools.partial(join_back_kernel, heads, chips),
        "join_back",
        [],
        [back, core_swap(send, count), early_t] + list(results[5:]),
        [states] + [offsets] * chips,
        flops=10**7,
    )
    later = results[0]
    arrived = [seq_shift(x, -2 * by, count) for by, x in enumerate(results[1:], 1)]
    query_terms = call(
        functools.partial(query_kernel, heads),
        "query_grad",
        [],
        [masks, dout, state, solved, score_t, q, k, solve_t, aux, unit, gains, spread, suffix_t,
         later],
        [shape((frames, heads * dv), BF16), shape((frames, heads * dk), BF16), values, values,
         square, square],
        flops=2 * 10**8,
    )
    head_out, gq, fresh, y, dkey, reach = query_terms
    results = call(
        functools.partial(key_kernel, heads, kinds, chips, count),
        "key_grad",
        [],
        [masks] + arrived + [suffix_t, reach, gq, fresh, y, dkey, state, k, v, gram, aux] + list(flipped),
        [shape((frames, local), BF16)] * (kinds - 1)
        + [shape((HALO, local), BF16)] * (kinds - 1)
        + [shape((frames, columns), BF16)],
        flops=2 * 10**8,
    )
    others, edges, grads = results[: kinds - 1], results[kinds - 1 : -1], results[-1]
    mine, edge = call(
        functools.partial(own_back_kernel, kinds),
        "own_back",
        [],
        [grads] + list(flipped),
        [shape((frames, local)), shape((HALO, local), BF16)],
        flops=2 * frames * local * columns,
    )
    others = [head_turn(x, turn, kinds) for turn, x in enumerate(others, 1)]
    edges = [corner_shift(x, -1, turn, count, kinds) for turn, x in enumerate([edge] + list(edges))]
    (input_grad,) = call(
        functools.partial(finish_kernel, kinds),
        "finish",
        [],
        [back_pick, back_edge, mine] + others + edges,
        [shape((frames, local), BF16)],
        flops=10**8,
        out_space=pl.BlockSpec(memory_space=pl.ANY),
        scratch=[pltpu.VMEM((frames, local), BF16), pltpu.SemaphoreType.DMA((parts,))],
    )
    return head_out, input_grad


def solution(mesh):
    return jax.shard_map(
        on_device,
        mesh=mesh,
        in_specs=(
            P("seq", "head"),
            P("seq", "head"),
            P(None, "head"),
            P(None, "head"),
            P(None, "head"),
            P(None, "head"),
            P("head"),
            P(),
            P(),
            P(),
            P("seq", None),
        ),
        out_specs=(P("seq", "head"), P("seq", "head")),
        check_vma=False,
    )
```

```python
import functools

import jax
import jax.numpy as jnp
from jax import lax
from jax.experimental import pallas as pl
from jax.experimental.pallas import tpu as pltpu
from jax.sharding import PartitionSpec as P

EPSILON = 1e-06
F32 = jnp.float32
BF16 = jnp.bfloat16
HALO = 8
REACH = 16
LANES = 128
VMEM_LIMIT = 16 * 1024 * 1024


def halves(x):
    high = x.astype(BF16)
    return high, (x - high.astype(F32)).astype(BF16)


def dot(a, b):
    return jnp.dot(a, b, preferred_element_type=F32)


def dot_nt(a, b):
    return lax.dot_general(a, b, (((1,), (1,)), ((), ())), preferred_element_type=F32)


def mm(a, b):
    width = b.shape[1]
    b_high, b_low = halves(b)
    right = jnp.concatenate([b_high, b_low], axis=1)
    if a.dtype == BF16:
        both = dot(a, right)
    else:
        left = jnp.concatenate(halves(a), axis=1)
        both = dot(left, jnp.concatenate([right, right], axis=0))
    return both[:, :width] + both[:, width:]


def mm_nt(a, b):
    width = b.shape[0]
    left = jnp.concatenate(halves(a), axis=1)
    right = jnp.concatenate(halves(b), axis=0)
    both = dot_nt(left, jnp.concatenate([right, right], axis=1))
    return both[:, :width] + both[:, width:]


def rough(a, b):
    return dot(a.astype(BF16), b.astype(BF16))


def rough_nt(a, b):
    return dot_nt(a.astype(BF16), b.astype(BF16))


def begins(clips_ref, position):
    end = 0
    total = jnp.zeros_like(position)
    for clip in range(clips_ref.shape[0]):
        length = clips_ref[clip]
        end = end + length
        total = total + jnp.where(end <= position, length, 0)
    return total


def here():
    return lax.axis_index("seq"), lax.axis_index("head")


def solve_unit(low, right):
    size = low[0].shape[0]
    row = lax.broadcasted_iota(jnp.int32, (size, size), 0)
    col = lax.broadcasted_iota(jnp.int32, (size, size), 1)
    eye = jnp.where(row == col, 1.0, 0.0).astype(F32)

    def within(width):
        return (row // width) == (col // width)

    def wide_products(lefts, *rights):
        results = []
        for left, *several in zip(lefts, *rights):
            both, at, parts = mm(left, jnp.concatenate(several, axis=1)), 0, []
            for one in several:
                parts.append(both[:, at : at + one.shape[1]])
                at += one.shape[1]
            results.append(parts)
        return [list(part) for part in zip(*results)]

    block = 2
    inverse = [eye - jnp.where(within(block), x, 0.0) for x in low]
    while block < size:
        wide = min(8 * block, size)
        ring = within(wide) & jnp.logical_not(within(block))
        rest = [jnp.where(ring, n, 0.0) for n in low]
        if wide < size:
            (step,) = wide_products(inverse, rest)
            start = inverse
        else:
            step, solved = wide_products(inverse, rest, right)
            start = [jnp.concatenate(both, axis=1) for both in zip(inverse, solved)]
        square, moved = wide_products(step, step, start)
        start = [x - m for x, m in zip(start, moved)]
        fourth, moved = wide_products(square, square, start)
        start = [x + m for x, m in zip(start, moved)]
        inverse = [x + mm(f, x) for f, x in zip(fourth, start)]
        block = wide
    return [x[:, :size] for x in inverse], [x[:, size:] for x in inverse]


def prepare_kernel(kinds, local, order_ref, clips_ref, delays_ref, cap_ref, pick_ref, edge_ref, last_ref,
                   back_pick_ref, back_edge_ref, mask_ref, caps_ref):
    seq, head = here()
    frames = pick_ref.shape[1]
    parts = pick_ref.shape[0] // kinds
    width = local // parts
    group = (local * kinds) // delays_ref.shape[0]
    sources = order_ref.shape[1]
    rows_each = frames // sources
    base = seq * frames
    row = lax.broadcasted_iota(jnp.int32, (frames, frames), 0)
    col = lax.broadcasted_iota(jnp.int32, (frames, frames), 1)
    row_begin = begins(clips_ref, base + row) - base
    col_begin = begins(clips_ref, base + col[:1]) - base
    last_begin = begins(clips_ref, base + frames - 1) - base
    same = row_begin == col_begin
    carried_last = jnp.where(last_begin < 0, 1.0, 0.0)
    mask_ref[0] = jnp.where((row > col) & same, 1.0, 0.0).astype(F32)
    mask_ref[1] = jnp.where((row >= col) & same, 1.0, 0.0).astype(F32)
    mask_ref[2] = jnp.where(row_begin < 0, 1.0, 0.0).astype(F32)
    mask_ref[3] = jnp.where(row_begin == last_begin, 1.0, 0.0).astype(F32)
    mask_ref[4] = jnp.where(row == col, carried_last, 0.0).astype(F32)
    for index in range(caps_ref.shape[0]):
        caps_ref[index] = jnp.full(caps_ref.shape[1:], cap_ref[index], F32)
    lane = col[:1]
    landing = jnp.zeros((1, frames), jnp.int32)
    for source in range(sources):
        at = order_ref[0, source] * rows_each + (lane - source * rows_each)
        landing = jnp.where(lane // rows_each == source, at, landing)
    edge_row = row[:, :HALO]
    edge_col = lax.broadcasted_iota(jnp.int32, (frames, HALO), 1)
    last_ref[...] = jnp.where(landing == row[:HALO] + (frames - HALO), 1.0, 0.0).astype(BF16)
    for kind in range(kinds):
        owner = lax.rem(head + kinds - kind, kinds)
        for part in range(parts):
            source_row = row - delays_ref[(owner * local + part * width) // group]
            inside = source_row >= row_begin
            pick = jnp.where((landing == source_row) & inside, 1.0, 0.0).astype(BF16)
            pick_ref[kind * parts + part] = pick
            edge = (edge_col - HALO == source_row[:, :HALO]) & inside[:, :HALO]
            edge_ref[kind * parts + part] = jnp.where(edge, 1.0, 0.0).astype(BF16)
    edge_begin = begins(clips_ref, base + frames + edge_col[:1]) - base
    for part in range(parts):
        delay = delays_ref[(head * local + part * width) // group]
        pick = jnp.where((col == row + delay) & (col_begin <= row), 1.0, 0.0).astype(BF16)
        back_pick_ref[part] = pick
        edge = (edge_col + frames == edge_row + delay) & (edge_begin <= edge_row)
        back_edge_ref[part] = jnp.where(edge, 1.0, 0.0).astype(BF16)


def flip_kernel(*refs):
    for ref, out_ref in zip(refs[:4], refs[4:]):
        out_ref[...] = ref[...].T


def add_products(sums, kind, kinds, piece_ref, halo_ref, pick_ref, edge_ref, weights):
    local = halo_ref.shape[1] if piece_ref is None else piece_ref.shape[1]
    parts = pick_ref.shape[0] // kinds
    width = local // parts
    owner = lax.rem(here()[1] + kinds - kind, kinds)
    for part in range(parts):
        span = slice(part * width, (part + 1) * width)
        index = kind * parts + part
        if piece_ref is None:
            delayed = dot(edge_ref[index, :REACH], halo_ref[:, span])
        else:
            delayed = dot(pick_ref[index], piece_ref[:, span])
            if halo_ref is not None:
                delayed = delayed + dot(edge_ref[index], halo_ref[:, span])
        at = pl.ds(pl.multiple_of(owner * local + part * width, width), width)
        delayed = delayed.astype(BF16)
        new = [dot(delayed, weight[at, :]) for weight in weights]
        sums = new if sums is None else [a + b for a, b in zip(sums, new)]
    return sums


def own_kernel(kinds, piece_ref, pick_ref, edge_ref, *refs):
    sums = add_products(None, 0, kinds, piece_ref, None, pick_ref, edge_ref, refs[:4])
    for ref, part in zip(refs[4:], sums):
        ref[...] = part


def own_halo_kernel(kinds, halo_ref, edge_ref, *refs):
    sums = add_products(None, 0, kinds, None, halo_ref, edge_ref, edge_ref, refs[:4])
    for ref, part in zip(refs[4:], sums):
        ref[...] = part


def project_kernel(heads, kinds, mask_ref, cap_ref, *refs):
    sums, first, refs = [ref[...] for ref in refs[:4]], [ref[...] for ref in refs[4:8]], refs[8:]
    pieces, halos = refs[: kinds - 1], refs[kinds - 1 : 2 * kinds - 2]
    pick_ref, edge_ref = refs[2 * kinds - 2 : 2 * kinds]
    weights = refs[2 * kinds : 2 * kinds + 4]
    map_ref, q_ref, k_ref, v_ref, solve_ref, w_ref, aux_ref = refs[2 * kinds + 4 :]
    frames = sums[0].shape[0]
    strict, carried, final, eye = mask_ref[0], mask_ref[2], mask_ref[3], mask_ref[4]
    sums = [jnp.concatenate([x[:REACH] + a, x[REACH:]], axis=0) for x, a in zip(sums, first)]
    for kind in range(1, kinds):
        sums = add_products(
            sums, kind, kinds, pieces[kind - 1], halos[kind - 1], pick_ref, edge_ref, weights
        )
    q_all, k_all, v_all, logit_all = sums
    dk = q_all.shape[1] // heads
    dv = v_all.shape[1] // heads
    keys, rights, lows = [], [], []
    aux = jnp.zeros((frames, LANES), F32)
    aux_lane = lax.broadcasted_iota(jnp.int32, (frames, LANES), 1)
    for head in range(heads):
        q_raw = q_all[:, head * dk : (head + 1) * dk]
        k_raw = k_all[:, head * dk : (head + 1) * dk]
        value = v_all[:, head * dv : (head + 1) * dv]
        q_scale = lax.rsqrt(jnp.sum(q_raw * q_raw, axis=1, keepdims=True) + EPSILON)
        k_scale = lax.rsqrt(jnp.sum(k_raw * k_raw, axis=1, keepdims=True) + EPSILON)
        gate = 1.0 / (1.0 + jnp.exp(-logit_all[:, head : head + 1]))
        rate = cap_ref[head, :, :1] * gate
        key = k_raw * k_scale
        q_ref[head] = q_raw * q_scale
        k_ref[head] = key
        v_ref[head] = value
        for index, item in enumerate((q_scale, k_scale, rate, rate * (1.0 - gate))):
            aux = jnp.where(aux_lane == 4 * head + index, item, aux)
        gram = mm_nt(key, key)
        lows.append(strict * (rate * gram))
        keys.append(key)
        rights.append(rate * jnp.concatenate([key, value], axis=1))
    aux_ref[...] = aux
    solves, solutions = solve_unit(lows, rights)
    for head in range(heads):
        solved = solutions[head]
        solve_ref[head] = solves[head]
        w_ref[head] = solved
        ended = jnp.concatenate(
            [-(final * carried) * solved[:, :dk], final * solved[:, dk:]], axis=1
        )
        affine = rough(keys[head].T, ended)
        map_ref[head, :, :dk] = (affine[:, :dk] + eye).astype(BF16)
        map_ref[head, :, dk:] = affine[:, dk:].astype(BF16)


def local_kernel(heads, mask_ref, q_ref, k_ref, w_ref, solve_ref, early_ref, suffix_ref, prefix_ref,
                 gain_ref, grad_ref, score_t_ref, reach_ref, reach_t_ref, local_ref, solve_t_ref,
                 gram_ref, spread_ref, early_t_ref, suffix_t_ref, weighted_ref, gains_ref):
    frames, dk = q_ref.shape[1:]
    lower, carried, final = mask_ref[1], mask_ref[2], mask_ref[3]
    gains_ref[...] = gain_ref[...]
    for head in range(heads):
        query, key, solved = q_ref[head], k_ref[head], w_ref[head]
        scores = lower * mm_nt(query, key)
        both = mm(scores, solved)
        reach = carried * (query - both[:, :dk])
        score_t_ref[head] = scores.T
        prefix = prefix_ref[head]
        reach_t_ref[head] = reach.T
        grown = mm(reach, prefix.astype(F32))
        reach_ref[head] = grown[:, :dk]
        local_ref[head] = both[:, dk:] + grown[:, dk:]
        solve_t = solve_ref[head].T
        solve_t_ref[head] = solve_t
        gram_ref[head] = mm_nt(key, key)
        spread_ref[head] = mm(solve_t, final * key)
        early_t_ref[head] = early_ref[head].astype(F32).T
        suffix_t_ref[head] = suffix_ref[head].astype(F32).T
        dv = local_ref.shape[2]
        weighted_ref[head] = grad_ref[:, head * dv : (head + 1) * dv].astype(F32) * gain_ref[...]


def is_upper():
    return lax.rem(here()[0], 2) == 1


def join_kernel(heads, chips, own_ref, other_ref, *refs):
    joined_ref, prefix_ref, suffix_ref, early_ref = refs[:4]
    dk = own_ref.shape[1]
    upper = is_upper()
    row = lax.broadcasted_iota(jnp.int32, (dk, dk), 0)
    col = lax.broadcasted_iota(jnp.int32, (dk, dk), 1)
    eye = jnp.where(row == col, 1.0, 0.0)
    for head in range(heads):
        own, other = own_ref[head].astype(F32), other_ref[head].astype(F32)
        early = jnp.where(upper, other, own)
        late = jnp.where(upper, own, other)
        both = dot(late[:, :dk].astype(BF16), early.astype(BF16))
        offset = (both[:, dk:] + late[:, dk:]).astype(BF16)
        if chips > 1:
            joined_ref[head, :, :dk] = both[:, :dk].astype(BF16)
            joined_ref[head, :, dk:] = offset
            refs[4][head] = offset
        else:
            joined_ref[head] = offset
        early_ref[head] = early[:, :dk].astype(BF16)
        prefix_ref[head, :, :dk] = jnp.where(upper, other[:, :dk], eye).astype(BF16)
        prefix_ref[head, :, dk:] = jnp.where(upper, other[:, dk:], 0.0).astype(BF16)
        suffix_ref[head] = jnp.where(upper, eye, other[:, :dk]).astype(BF16)


def give_kernel(heads, even_ref, odd_ref, give_ref):
    upper = is_upper()
    width = odd_ref.shape[2]
    for head in range(heads):
        odd = odd_ref[head].astype(F32)
        even = even_ref[head].astype(F32)
        give_ref[head, :, -width:] = jnp.where(upper, odd, even[:, -width:]).astype(BF16)
        if width < even.shape[1]:
            give_ref[head, :, :-width] = even_ref[head, :, :-width]


def shared_maps(heads, rows, swapped):
    maps = []
    upper = is_upper()
    for index, row in enumerate(rows):
        other = swapped[index // 2]
        width = row.shape[2]
        mine = upper if index % 2 else jnp.logical_not(upper)
        maps.append([
            jnp.where(mine, row[head].astype(F32), other[head, :, -width:].astype(F32))
            for head in range(heads)
        ])
    return maps


def chain_kernel(heads, chips, *refs):
    rows, swapped, refs = refs[:chips], refs[chips : chips + chips // 2], refs[chips + chips // 2 :]
    maps = shared_maps(heads, rows[:-1], swapped)
    early_t_ref, flipped, chained = refs[0], refs[1:chips], refs[chips:]
    dk = early_t_ref.shape[1]
    for head in range(heads):
        product = None
        for earlier, flip_ref, chain_ref in zip(maps, flipped, chained):
            move = earlier[head][:, :dk]
            product = move if product is None else mm(product, move)
            flip = product.T
            flip_ref[head] = flip
            chain_ref[head] = rough(flip, early_t_ref[head])


def output_kernel(heads, chips, *refs):
    rows, swapped, refs = refs[:chips], refs[chips : chips + chips // 2], refs[chips + chips // 2 :]
    maps = shared_maps(heads, rows, swapped)
    (prefix_ref, reach_ref, reach_t_ref, local_ref, weighted_ref,
     state_ref, unit_ref, dout_ref, back_ref, send_ref) = refs
    seq = here()[0]
    dk = reach_ref.shape[2]
    for head in range(heads):
        state = jnp.where(seq >= 2 * chips, maps[-1][head], 0.0)
        for index in range(chips - 2, -1, -1):
            earlier = maps[index][head]
            step = rough if index == chips - 2 else mm
            state = earlier[:, dk:] + step(earlier[:, :dk].astype(BF16), state)
            state = jnp.where(seq >= 2 * index + 2, state, 0.0)
        raw = local_ref[head] + mm(reach_ref[head], state)
        state_ref[head] = prefix_ref[head, :, dk:].astype(F32) + mm(prefix_ref[head, :, :dk], state)
        scale = lax.rsqrt(jnp.mean(raw * raw, axis=1, keepdims=True) + EPSILON)
        unit = raw * scale
        unit_ref[head] = unit
        weighted = weighted_ref[head]
        dout = scale * (weighted - unit * jnp.mean(unit * weighted, axis=1, keepdims=True))
        dout_ref[head] = dout
        back = rough(reach_t_ref[head], dout)
        back_ref[head] = back
        send_ref[head] = back.astype(BF16)


def join_back_kernel(heads, chips, own_ref, other_ref, early_t_ref, *refs):
    flipped, chained = refs[: chips - 1], refs[chips - 1 : 2 * chips - 2]
    later_ref, sends = refs[2 * chips - 2], refs[2 * chips - 1 :]
    upper = is_upper()
    for head in range(heads):
        own, other = own_ref[head], other_ref[head].astype(F32)
        late = jnp.where(upper, own, other)
        first = jnp.where(upper, other, own)
        later_ref[head] = jnp.where(upper, 0.0, other)
        sends[0][head] = (first + rough(early_t_ref[head], late)).astype(BF16)
        for flip_ref, chain_ref, send in zip(flipped, chained, sends[1:]):
            send[head] = (rough(flip_ref[head], first) + rough(chain_ref[head], late)).astype(BF16)


def query_kernel(heads, mask_ref, dout_ref, state_ref, w_ref, score_t_ref, q_ref, k_ref, solve_t_ref,
                 aux_ref, unit_ref, gain_ref, spread_ref, suffix_t_ref, later_ref,
                 out_ref, gq_ref, u_ref, y_ref, dk_ref, reach_ref):
    frames, dk = q_ref.shape[1:]
    lower, carried, final = mask_ref[1], mask_ref[2], mask_ref[3]
    for head in range(heads):
        dv = unit_ref.shape[2]
        out_ref[:, head * dv : (head + 1) * dv] = (unit_ref[head] * gain_ref[...]).astype(BF16)
        dout, state, solved = dout_ref[head], state_ref[head], w_ref[head]
        query, key = q_ref[head], k_ref[head]
        fresh = solved[:, dk:] - carried * mm(solved[:, :dk], state)
        u_ref[head] = fresh
        later, suffix_t = later_ref[head], suffix_t_ref[head]
        ended = final * fresh
        reach = mm(spread_ref[head], jnp.concatenate([later, suffix_t], axis=1))
        reach_ref[head] = reach[:, dv:]
        y_ref[head] = mm(solve_t_ref[head], mm(score_t_ref[head], dout)) + reach[:, :dv]
        flow = lower * mm_nt(dout, fresh)
        dquery = carried * mm_nt(dout, state) + mm(flow, key)
        dk_ref[head] = mm(flow.T, query) + mm_nt(ended, later)
        scale = aux_ref[:, 4 * head : 4 * head + 1]
        along = jnp.sum(query * dquery, axis=1, keepdims=True)
        gq_ref[:, head * dk : (head + 1) * dk] = (scale * (dquery - query * along)).astype(BF16)


def key_kernel(heads, kinds, chips, count, mask_ref, *refs):
    arrived, refs = refs[:chips], refs[chips:]
    (suffix_t_ref, reach_ref, gq_ref, u_ref, y_ref, dk0_ref, state_ref, k_ref, v_ref, gram_ref,
     aux_ref), refs = refs[:11], refs[11:]
    seq = here()[0]
    weights, refs = refs[:4], refs[4:]
    outs, grads_ref = refs[:-1], refs[-1]
    frames, dk = k_ref.shape[1:]
    strict, carried, final = mask_ref[0], mask_ref[2], mask_ref[3]
    key_grads, value_grads = [], []
    lane = lax.broadcasted_iota(jnp.int32, (frames, LANES), 1)
    logit_grad = jnp.zeros((frames, LANES), F32)
    for head in range(heads):
        after = sum(
            jnp.where(seq + 2 * index + 2 < count, ref[head].astype(F32), 0.0)
            for index, ref in enumerate(arrived)
        )
        key, fresh = k_ref[head], u_ref[head]
        k_scale = aux_ref[:, 4 * head + 1 : 4 * head + 2]
        rate = aux_ref[:, 4 * head + 2 : 4 * head + 3]
        slope = aux_ref[:, 4 * head + 3 : 4 * head + 4]
        y = y_ref[head] + rough(reach_ref[head], after)
        both = rough_nt(y, jnp.concatenate([state_ref[head], fresh], axis=0))
        from_state = -carried * both[:, :dk]
        system = strict * -both[:, dk:]
        scaled = rate * system
        dkey = dk0_ref[head] + rough_nt(rough_nt(final * fresh, after), suffix_t_ref[head])
        dkey = dkey + rough(scaled + scaled.T, key) + rate * from_state
        drate = jnp.sum(
            system * gram_ref[head] + from_state * key + y * v_ref[head], axis=1, keepdims=True
        )
        logit_grad = jnp.where(lane == head, drate * slope, logit_grad)
        along = jnp.sum(key * dkey, axis=1, keepdims=True)
        key_grads.append((k_scale * (dkey - key * along)).astype(BF16))
        value_grads.append((rate * y).astype(BF16))
    grads_ref[...] = jnp.concatenate(
        [gq_ref[...]] + key_grads + value_grads + [logit_grad.astype(BF16)], axis=1
    )
    others, halos = outs[: kinds - 1], outs[kinds - 1 :]
    for turn in range(1, kinds):
        back_products(grads_ref, weights, turn, kinds, others[turn - 1], halos[turn - 1])


def back_products(grads_ref, weights, turn, kinds, sum_ref, halo_ref):
    local = sum_ref.shape[1]
    width = min(512, local)
    for part in range(local // width):
        first = lax.rem(here()[1] + turn, kinds) * local + part * width
        at = pl.ds(pl.multiple_of(first, width), width)
        row, total = 0, 0.0
        for weight in weights:
            total = total + dot(grads_ref[:, row : row + weight.shape[0]], weight[:, at])
            row += weight.shape[0]
        span = slice(part * width, (part + 1) * width)
        halo_ref[:, span] = total[:HALO].astype(BF16)
        sum_ref[:, span] = total.astype(sum_ref.dtype)


def own_back_kernel(kinds, grads_ref, *refs):
    back_products(grads_ref, refs[:4], 0, kinds, *refs[4:])


def finish_kernel(kinds, pick_ref, edge_ref, mine_ref, *refs):
    others, halos = refs[: kinds - 1], refs[kinds - 1 : 2 * kinds - 1]
    out_ref, held_ref, semaphores = refs[-3:]
    parts = pick_ref.shape[0]
    copies = []
    width = mine_ref.shape[1] // parts
    for part in range(parts):
        span = slice(part * width, (part + 1) * width)
        total = mine_ref[:, span]
        for other in others:
            total = total + other[:, span].astype(F32)
        edge = halos[0][:, span].astype(F32)
        for halo in halos[1:]:
            edge = edge + halo[:, span].astype(F32)
        moved = dot(pick_ref[part], total.astype(BF16)) + dot(edge_ref[part], edge.astype(BF16))
        held_ref[:, span] = moved.astype(BF16)
        copies.append(
            pltpu.make_async_copy(held_ref.at[:, span], out_ref.at[:, span], semaphores.at[part])
        )
        copies[-1].start()
    for copy in copies:
        copy.wait()


SMEM = pl.BlockSpec(memory_space=pltpu.SMEM)
VMEM = pl.BlockSpec(memory_space=pltpu.VMEM)


def call(body, name, scalars, arrays, outs, flops=0, out_space=VMEM, scratch=()):
    moved = sum(a.size * a.dtype.itemsize for a in arrays)
    moved += sum(o.size * o.dtype.itemsize for o in outs)
    return pl.pallas_call(
        body,
        name=name,
        out_shape=tuple(outs),
        in_specs=[SMEM] * len(scalars) + [VMEM] * len(arrays),
        out_specs=tuple([out_space] * len(outs)),
        scratch_shapes=list(scratch),
        cost_estimate=pl.CostEstimate(flops=flops, bytes_accessed=moved, transcendentals=0),
        compiler_params=pltpu.CompilerParams(vmem_limit_bytes=VMEM_LIMIT),
    )(*scalars, *arrays)


def shape(dims, kind=F32):
    return jax.ShapeDtypeStruct(tuple(dims), kind)


def row_shift(x, by, rising, count):
    chips = count // 2
    pairs = []
    for chip in range(chips):
        up, down = chip + by, chip - by
        pairs.append((2 * chip + rising, 2 * up + rising if up < chips else 2 * chip + 1 - rising))
        pairs.append((2 * chip + 1 - rising, 2 * down + 1 - rising if down >= 0 else 2 * chip + rising))
    return lax.ppermute(x, "seq", pairs)


def seq_shift(x, by, count):
    return lax.ppermute(x, "seq", [(i, (i + by) % count) for i in range(count)])


def core_swap(x, count):
    return lax.ppermute(x, "seq", [(i, i ^ 1) for i in range(count)])


def corner_shift(x, by, turn, count, kinds):
    pairs = []
    for i in range(count):
        for h in range(kinds):
            pairs.append((i * kinds + h, (i + by) % count * kinds + (h + turn) % kinds))
    return lax.ppermute(x, ("seq", "head"), pairs)


def head_turn(x, turn, kinds):
    return lax.ppermute(x, "head", [(h, (h + turn) % kinds) for h in range(kinds)])


def on_device(loaded, out_grad, w_query, w_key, w_value, w_beta, beta_max, out_gain, clip_lengths,
              delay_offsets, block_order):
    count = lax.axis_size("seq")
    kinds = lax.axis_size("head")
    frames, local = loaded.shape
    rows_each = frames // count
    heads = w_beta.shape[1]
    dk = w_query.shape[1] // heads
    dv = w_value.shape[1] // heads
    chips = count // 8
    group = (local * kinds) // delay_offsets.shape[0]
    parts = local // min(group, local)
    columns = heads * (2 * dk + dv) + LANES
    wb = jnp.pad(w_beta, ((0, 0), (0, LANES - heads)))
    gain = out_gain.reshape(1, dv)

    received = lax.all_to_all(
        loaded.reshape(count, rows_each, local), "seq", split_axis=0, concat_axis=0, tiled=True
    ).reshape(frames, local)
    prepared = call(
        functools.partial(prepare_kernel, kinds, local),
        "prepare",
        [block_order, clip_lengths, delay_offsets, beta_max],
        [],
        [
            shape((kinds * parts, frames, frames), BF16),
            shape((kinds * parts, frames, HALO), BF16),
            shape((HALO, frames), BF16),
            shape((parts, frames, frames), BF16),
            shape((parts, frames, HALO), BF16),
            shape((5, frames, frames)),
            shape((heads, 1, LANES)),
        ],
    )
    received, wb, *prepared = lax.optimization_barrier((received, wb, *prepared))
    pick, edge, last, back_pick, back_edge, masks, caps = prepared
    tail = jnp.dot(last, received, preferred_element_type=F32).astype(BF16)
    pieces = [head_turn(received, turn, kinds) for turn in range(1, kinds)]
    halos = [corner_shift(tail, 1, turn, count, kinds) for turn in range(kinds)]
    weights = [w_query, w_key, w_value, wb]
    sums = call(
        functools.partial(own_kernel, kinds),
        "project_own",
        [],
        [received, pick, edge] + weights,
        [shape((frames, weight.shape[1])) for weight in weights],
        flops=2 * frames * local * columns,
    )
    first = call(
        functools.partial(own_halo_kernel, kinds),
        "project_halo",
        [],
        [halos[0], edge] + weights,
        [shape((REACH, weight.shape[1])) for weight in weights],
        flops=2 * REACH * local * columns,
    )
    flipped = call(
        flip_kernel, "flip", [], weights, [shape(w.shape[::-1], BF16) for w in weights]
    )
    sums, first, flipped = lax.optimization_barrier((sums, first, flipped))

    square = shape((heads, frames, dk))
    values = shape((heads, frames, dv))
    times = shape((heads, frames, frames))
    maps = shape((heads, dk, dk + dv), BF16)
    moves = shape((heads, dk, dk))
    states = shape((heads, dk, dv))
    offsets = shape((heads, dk, dv), BF16)
    affine, q, k, v, solve, solved, aux = call(
        functools.partial(project_kernel, heads, kinds),
        "project",
        [],
        [masks, caps] + list(sums) + list(first) + pieces + halos[1:] + [pick, edge] + weights,
        [maps, square, square, values, times, shape((heads, frames, dk + dv)),
         shape((frames, LANES))],
        flops=2 * frames * local * columns,
    )
    results = call(
        functools.partial(join_kernel, heads, chips),
        "join",
        [],
        [affine, core_swap(affine, count)],
        [maps if chips > 1 else offsets, maps, shape(moves.shape, BF16), shape(moves.shape, BF16)]
        + [offsets] * (chips > 1),
        flops=10**7,
    )
    joined, prefix, suffix, early = results[:4]
    arrived = [row_shift(joined, by, (by - 1) % 2, count) for by in range(1, chips)]
    arrived.append(row_shift(results[-1], chips, (chips - 1) % 2, count))
    local_terms = call(
        functools.partial(local_kernel, heads),
        "local_terms",
        [],
        [masks, q, k, solved, solve, early, suffix, prefix, gain, out_grad],
        [times, square, shape((heads, dk, frames)), values, times, times, square, moves, moves,
         values, shape((1, dv))],
        flops=2 * 10**8,
    )
    arrived, local_terms = lax.optimization_barrier((arrived, local_terms))
    (score_t, reach, reach_t, local_out, solve_t, gram, spread, early_t, suffix_t, weighted,
     gains) = local_terms
    swapped = []
    for at in range(0, chips, 2):
        (give,) = call(
            functools.partial(give_kernel, heads), "give", [], arrived[at : at + 2], [maps],
        )
        swapped.append(core_swap(give, count))
    results = call(
        functools.partial(output_kernel, heads, chips),
        "outputs",
        [],
        arrived + swapped + [prefix, reach, reach_t, local_out, weighted],
        [states, values, values, states, offsets],
        flops=2 * 10**8,
    )
    state, unit, dout, back, send = results
    chained = call(
        functools.partial(chain_kernel, heads, chips),
        "chain",
        [],
        arrived + swapped + [early_t],
        [moves] * (2 * chips - 2),
        flops=10**7,
    )
    results = call(
        functools.partial(join_back_kernel, heads, chips),
        "join_back",
        [],
        [back, core_swap(send, count), early_t] + list(chained),
        [states] + [offsets] * chips,
        flops=10**7,
    )
    later = results[0]
    arrived = [seq_shift(x, -2 * by, count) for by, x in enumerate(results[1:], 1)]
    query_terms = call(
        functools.partial(query_kernel, heads),
        "query_grad",
        [],
        [masks, dout, state, solved, score_t, q, k, solve_t, aux, unit, gains, spread, suffix_t,
         later],
        [shape((frames, heads * dv), BF16), shape((frames, heads * dk), BF16), values, values,
         square, square],
        flops=2 * 10**8,
    )
    head_out, gq, fresh, y, dkey, reach = query_terms
    results = call(
        functools.partial(key_kernel, heads, kinds, chips, count),
        "key_grad",
        [],
        [masks] + arrived + [suffix_t, reach, gq, fresh, y, dkey, state, k, v, gram, aux] + list(flipped),
        [shape((frames, local), BF16)] * (kinds - 1)
        + [shape((HALO, local), BF16)] * (kinds - 1)
        + [shape((frames, columns), BF16)],
        flops=2 * 10**8,
    )
    others, edges, grads = results[: kinds - 1], results[kinds - 1 : -1], results[-1]
    mine, edge = call(
        functools.partial(own_back_kernel, kinds),
        "own_back",
        [],
        [grads] + list(flipped),
        [shape((frames, local)), shape((HALO, local), BF16)],
        flops=2 * frames * local * columns,
    )
    others = [head_turn(x, turn, kinds) for turn, x in enumerate(others, 1)]
    edges = [corner_shift(x, -1, turn, count, kinds) for turn, x in enumerate([edge] + list(edges))]
    (input_grad,) = call(
        functools.partial(finish_kernel, kinds),
        "finish",
        [],
        [back_pick, back_edge, mine] + others + edges,
        [shape((frames, local), BF16)],
        flops=10**8,
        out_space=pl.BlockSpec(memory_space=pl.ANY),
        scratch=[pltpu.VMEM((frames, local), BF16), pltpu.SemaphoreType.DMA((parts,))],
    )
    return head_out, input_grad


def solution(mesh):
    return jax.shard_map(
        on_device,
        mesh=mesh,
        in_specs=(
            P("seq", "head"),
            P("seq", "head"),
            P(None, "head"),
            P(None, "head"),
            P(None, "head"),
            P(None, "head"),
            P("head"),
            P(),
            P(),
            P(),
            P("seq", None),
        ),
        out_specs=(P("seq", "head"), P("seq", "head")),
        check_vma=False,
    )
```

```python
import functools

import jax
import jax.numpy as jnp
from jax import lax
from jax.experimental import pallas as pl
from jax.experimental.pallas import tpu as pltpu
from jax.sharding import PartitionSpec as P

EPSILON = 1e-06
F32 = jnp.float32
BF16 = jnp.bfloat16
HALO = 8
REACH = 16
LANES = 128
VMEM_LIMIT = 16 * 1024 * 1024


def halves(x):
    high = x.astype(BF16)
    return high, (x - high.astype(F32)).astype(BF16)


def dot(a, b):
    return jnp.dot(a, b, preferred_element_type=F32)


def dot_nt(a, b):
    return lax.dot_general(a, b, (((1,), (1,)), ((), ())), preferred_element_type=F32)


def mm(a, b):
    width = b.shape[1]
    b_high, b_low = halves(b)
    right = jnp.concatenate([b_high, b_low], axis=1)
    if a.dtype == BF16:
        both = dot(a, right)
    else:
        left = jnp.concatenate(halves(a), axis=1)
        both = dot(left, jnp.concatenate([right, right], axis=0))
    return both[:, :width] + both[:, width:]


def mm_nt(a, b):
    width = b.shape[0]
    left = jnp.concatenate(halves(a), axis=1)
    right = jnp.concatenate(halves(b), axis=0)
    both = dot_nt(left, jnp.concatenate([right, right], axis=1))
    return both[:, :width] + both[:, width:]


def rough(a, b):
    return dot(a.astype(BF16), b.astype(BF16))


def rough_nt(a, b):
    return dot_nt(a.astype(BF16), b.astype(BF16))


def begins(clips_ref, position):
    end = 0
    total = jnp.zeros_like(position)
    for clip in range(clips_ref.shape[0]):
        length = clips_ref[clip]
        end = end + length
        total = total + jnp.where(end <= position, length, 0)
    return total


def here():
    return lax.axis_index("seq"), lax.axis_index("head")


def solve_unit(low, right):
    size = low[0].shape[0]
    row = lax.broadcasted_iota(jnp.int32, (size, size), 0)
    col = lax.broadcasted_iota(jnp.int32, (size, size), 1)
    eye = jnp.where(row == col, 1.0, 0.0).astype(F32)

    def within(width):
        return (row // width) == (col // width)

    def wide_products(lefts, *rights):
        results = []
        for left, *several in zip(lefts, *rights):
            both, at, parts = mm(left, jnp.concatenate(several, axis=1)), 0, []
            for one in several:
                parts.append(both[:, at : at + one.shape[1]])
                at += one.shape[1]
            results.append(parts)
        return [list(part) for part in zip(*results)]

    block = 2
    inverse = [eye - jnp.where(within(block), x, 0.0) for x in low]
    while block < size:
        wide = min(8 * block, size)
        ring = within(wide) & jnp.logical_not(within(block))
        rest = [jnp.where(ring, n, 0.0) for n in low]
        if wide < size:
            (step,) = wide_products(inverse, rest)
            start = inverse
        else:
            step, solved = wide_products(inverse, rest, right)
            start = [jnp.concatenate(both, axis=1) for both in zip(inverse, solved)]
        square, moved = wide_products(step, step, start)
        start = [x - m for x, m in zip(start, moved)]
        fourth, moved = wide_products(square, square, start)
        start = [x + m for x, m in zip(start, moved)]
        inverse = [x + mm(f, x) for f, x in zip(fourth, start)]
        block = wide
    return [x[:, :size] for x in inverse], [x[:, size:] for x in inverse]


def prepare_kernel(kinds, local, order_ref, clips_ref, delays_ref, cap_ref, pick_ref, edge_ref, last_ref,
                   back_pick_ref, back_edge_ref, mask_ref, caps_ref):
    seq, head = here()
    frames = pick_ref.shape[1]
    parts = pick_ref.shape[0] // kinds
    width = local // parts
    group = (local * kinds) // delays_ref.shape[0]
    sources = order_ref.shape[1]
    rows_each = frames // sources
    base = seq * frames
    row = lax.broadcasted_iota(jnp.int32, (frames, frames), 0)
    col = lax.broadcasted_iota(jnp.int32, (frames, frames), 1)
    row_begin = begins(clips_ref, base + row) - base
    col_begin = begins(clips_ref, base + col[:1]) - base
    last_begin = begins(clips_ref, base + frames - 1) - base
    same = row_begin == col_begin
    carried_last = jnp.where(last_begin < 0, 1.0, 0.0)
    mask_ref[0] = jnp.where((row > col) & same, 1.0, 0.0).astype(F32)
    mask_ref[1] = jnp.where((row >= col) & same, 1.0, 0.0).astype(F32)
    mask_ref[2] = jnp.where(row_begin < 0, 1.0, 0.0).astype(F32)
    mask_ref[3] = jnp.where(row_begin == last_begin, 1.0, 0.0).astype(F32)
    mask_ref[4] = jnp.where(row == col, carried_last, 0.0).astype(F32)
    for index in range(caps_ref.shape[0]):
        caps_ref[index] = jnp.full(caps_ref.shape[1:], cap_ref[index], F32)
    lane = col[:1]
    landing = jnp.zeros((1, frames), jnp.int32)
    for source in range(sources):
        at = order_ref[0, source] * rows_each + (lane - source * rows_each)
        landing = jnp.where(lane // rows_each == source, at, landing)
    edge_row = row[:, :HALO]
    edge_col = lax.broadcasted_iota(jnp.int32, (frames, HALO), 1)
    last_ref[...] = jnp.where(landing == row[:HALO] + (frames - HALO), 1.0, 0.0).astype(BF16)
    for kind in range(kinds):
        owner = lax.rem(head + kinds - kind, kinds)
        for part in range(parts):
            source_row = row - delays_ref[(owner * local + part * width) // group]
            inside = source_row >= row_begin
            pick = jnp.where((landing == source_row) & inside, 1.0, 0.0).astype(BF16)
            pick_ref[kind * parts + part] = pick
            edge = (edge_col - HALO == source_row[:, :HALO]) & inside[:, :HALO]
            edge_ref[kind * parts + part] = jnp.where(edge, 1.0, 0.0).astype(BF16)
    edge_begin = begins(clips_ref, base + frames + edge_col[:1]) - base
    for part in range(parts):
        delay = delays_ref[(head * local + part * width) // group]
        pick = jnp.where((col == row + delay) & (col_begin <= row), 1.0, 0.0).astype(BF16)
        back_pick_ref[part] = pick
        edge = (edge_col + frames == edge_row + delay) & (edge_begin <= edge_row)
        back_edge_ref[part] = jnp.where(edge, 1.0, 0.0).astype(BF16)


def flip_kernel(*refs):
    for ref, out_ref in zip(refs[:4], refs[4:]):
        out_ref[...] = ref[...].T


def add_products(sums, kind, kinds, piece_ref, halo_ref, pick_ref, edge_ref, weights):
    local = halo_ref.shape[1] if piece_ref is None else piece_ref.shape[1]
    parts = pick_ref.shape[0] // kinds
    width = local // parts
    owner = lax.rem(here()[1] + kinds - kind, kinds)
    for part in range(parts):
        span = slice(part * width, (part + 1) * width)
        index = kind * parts + part
        if piece_ref is None:
            delayed = dot(edge_ref[index, :REACH], halo_ref[:, span])
        else:
            delayed = dot(pick_ref[index], piece_ref[:, span])
            if halo_ref is not None:
                delayed = delayed + dot(edge_ref[index], halo_ref[:, span])
        at = pl.ds(pl.multiple_of(owner * local + part * width, width), width)
        delayed = delayed.astype(BF16)
        new = [dot(delayed, weight[at, :]) for weight in weights]
        sums = new if sums is None else [a + b for a, b in zip(sums, new)]
    return sums


def own_kernel(kinds, piece_ref, pick_ref, edge_ref, *refs):
    sums = add_products(None, 0, kinds, piece_ref, None, pick_ref, edge_ref, refs[:4])
    for ref, part in zip(refs[4:], sums):
        ref[...] = part


def own_halo_kernel(kinds, halo_ref, edge_ref, *refs):
    sums = add_products(None, 0, kinds, None, halo_ref, edge_ref, edge_ref, refs[:4])
    for ref, part in zip(refs[4:], sums):
        ref[...] = part


def project_kernel(heads, kinds, mask_ref, cap_ref, *refs):
    sums, first, refs = [ref[...] for ref in refs[:4]], [ref[...] for ref in refs[4:8]], refs[8:]
    pieces, halos = refs[: kinds - 1], refs[kinds - 1 : 2 * kinds - 2]
    pick_ref, edge_ref = refs[2 * kinds - 2 : 2 * kinds]
    weights = refs[2 * kinds : 2 * kinds + 4]
    map_ref, q_ref, k_ref, v_ref, solve_ref, w_ref, aux_ref = refs[2 * kinds + 4 :]
    frames = sums[0].shape[0]
    strict, carried, final, eye = mask_ref[0], mask_ref[2], mask_ref[3], mask_ref[4]
    sums = [jnp.concatenate([x[:REACH] + a, x[REACH:]], axis=0) for x, a in zip(sums, first)]
    for kind in range(1, kinds):
        sums = add_products(
            sums, kind, kinds, pieces[kind - 1], halos[kind - 1], pick_ref, edge_ref, weights
        )
    q_all, k_all, v_all, logit_all = sums
    dk = q_all.shape[1] // heads
    dv = v_all.shape[1] // heads
    keys, rights, lows = [], [], []
    aux = jnp.zeros((frames, LANES), F32)
    aux_lane = lax.broadcasted_iota(jnp.int32, (frames, LANES), 1)
    for head in range(heads):
        q_raw = q_all[:, head * dk : (head + 1) * dk]
        k_raw = k_all[:, head * dk : (head + 1) * dk]
        value = v_all[:, head * dv : (head + 1) * dv]
        q_scale = lax.rsqrt(jnp.sum(q_raw * q_raw, axis=1, keepdims=True) + EPSILON)
        k_scale = lax.rsqrt(jnp.sum(k_raw * k_raw, axis=1, keepdims=True) + EPSILON)
        gate = 1.0 / (1.0 + jnp.exp(-logit_all[:, head : head + 1]))
        rate = cap_ref[head, :, :1] * gate
        key = k_raw * k_scale
        q_ref[head] = q_raw * q_scale
        k_ref[head] = key
        v_ref[head] = value
        for index, item in enumerate((q_scale, k_scale, rate, rate * (1.0 - gate))):
            aux = jnp.where(aux_lane == 4 * head + index, item, aux)
        gram = mm_nt(key, key)
        lows.append(strict * (rate * gram))
        keys.append(key)
        rights.append(rate * jnp.concatenate([key, value], axis=1))
    aux_ref[...] = aux
    solves, solutions = solve_unit(lows, rights)
    for head in range(heads):
        solved = solutions[head]
        solve_ref[head] = solves[head]
        w_ref[head] = solved
        ended = jnp.concatenate(
            [-(final * carried) * solved[:, :dk], final * solved[:, dk:]], axis=1
        )
        affine = rough(keys[head].T, ended)
        map_ref[head, :, :dk] = (affine[:, :dk] + eye).astype(BF16)
        map_ref[head, :, dk:] = affine[:, dk:].astype(BF16)


def local_kernel(heads, mask_ref, q_ref, k_ref, w_ref, solve_ref, early_ref, suffix_ref, prefix_ref,
                 gain_ref, grad_ref, score_t_ref, reach_ref, reach_t_ref, local_ref, solve_t_ref,
                 gram_ref, spread_ref, early_t_ref, suffix_t_ref, weighted_ref, gains_ref):
    frames, dk = q_ref.shape[1:]
    lower, carried, final = mask_ref[1], mask_ref[2], mask_ref[3]
    gains_ref[...] = gain_ref[...]
    for head in range(heads):
        query, key, solved = q_ref[head], k_ref[head], w_ref[head]
        scores = lower * mm_nt(query, key)
        both = mm(scores, solved)
        reach = carried * (query - both[:, :dk])
        score_t_ref[head] = scores.T
        prefix = prefix_ref[head]
        reach_t_ref[head] = reach.T
        grown = mm(reach, prefix.astype(F32))
        reach_ref[head] = grown[:, :dk]
        local_ref[head] = both[:, dk:] + grown[:, dk:]
        solve_t = solve_ref[head].T
        solve_t_ref[head] = solve_t
        gram_ref[head] = mm_nt(key, key)
        spread_ref[head] = mm(solve_t, final * key)
        early_t_ref[head] = early_ref[head].astype(F32).T
        suffix_t_ref[head] = suffix_ref[head].astype(F32).T
        dv = local_ref.shape[2]
        weighted_ref[head] = grad_ref[:, head * dv : (head + 1) * dv].astype(F32) * gain_ref[...]


def is_upper():
    return lax.rem(here()[0], 2) == 1


def join_kernel(heads, chips, own_ref, other_ref, *refs):
    joined_ref, prefix_ref, suffix_ref, early_ref = refs[:4]
    dk = own_ref.shape[1]
    upper = is_upper()
    row = lax.broadcasted_iota(jnp.int32, (dk, dk), 0)
    col = lax.broadcasted_iota(jnp.int32, (dk, dk), 1)
    eye = jnp.where(row == col, 1.0, 0.0)
    for head in range(heads):
        own, other = own_ref[head].astype(F32), other_ref[head].astype(F32)
        early = jnp.where(upper, other, own)
        late = jnp.where(upper, own, other)
        both = dot(late[:, :dk].astype(BF16), early.astype(BF16))
        offset = (both[:, dk:] + late[:, dk:]).astype(BF16)
        if chips > 1:
            joined_ref[head, :, :dk] = both[:, :dk].astype(BF16)
            joined_ref[head, :, dk:] = offset
            refs[4][head] = offset
        else:
            joined_ref[head] = offset
        early_ref[head] = early[:, :dk].astype(BF16)
        prefix_ref[head, :, :dk] = jnp.where(upper, other[:, :dk], eye).astype(BF16)
        prefix_ref[head, :, dk:] = jnp.where(upper, other[:, dk:], 0.0).astype(BF16)
        suffix_ref[head] = jnp.where(upper, eye, other[:, :dk]).astype(BF16)


def give_kernel(heads, even_ref, odd_ref, give_ref):
    upper = is_upper()
    width = odd_ref.shape[2]
    for head in range(heads):
        odd = odd_ref[head].astype(F32)
        even = even_ref[head].astype(F32)
        give_ref[head, :, -width:] = jnp.where(upper, odd, even[:, -width:]).astype(BF16)
        if width < even.shape[1]:
            give_ref[head, :, :-width] = even_ref[head, :, :-width]


def shared_maps(heads, rows, swapped):
    maps = []
    upper = is_upper()
    for index, row in enumerate(rows):
        other = swapped[index // 2]
        width = row.shape[2]
        mine = upper if index % 2 else jnp.logical_not(upper)
        maps.append([
            jnp.where(mine, row[head].astype(F32), other[head, :, -width:].astype(F32))
            for head in range(heads)
        ])
    return maps


def chain_kernel(heads, chips, *refs):
    rows, swapped, refs = refs[:chips], refs[chips : chips + chips // 2], refs[chips + chips // 2 :]
    maps = shared_maps(heads, rows[:-1], swapped)
    early_t_ref, flipped, chained = refs[0], refs[1:chips], refs[chips:]
    dk = early_t_ref.shape[1]
    for head in range(heads):
        product = None
        for earlier, flip_ref, chain_ref in zip(maps, flipped, chained):
            move = earlier[head][:, :dk]
            product = move if product is None else mm(product, move)
            flip = product.T
            flip_ref[head] = flip
            chain_ref[head] = rough(flip, early_t_ref[head])


def output_kernel(heads, chips, *refs):
    rows, swapped, refs = refs[:chips], refs[chips : chips + chips // 2], refs[chips + chips // 2 :]
    maps = shared_maps(heads, rows, swapped)
    (prefix_ref, reach_ref, reach_t_ref, local_ref, weighted_ref,
     state_ref, unit_ref, dout_ref, back_ref, send_ref) = refs
    seq = here()[0]
    dk = reach_ref.shape[2]
    for head in range(heads):
        state = jnp.where(seq >= 2 * chips, maps[-1][head], 0.0)
        for index in range(chips - 2, -1, -1):
            earlier = maps[index][head]
            step = rough if index == chips - 2 else mm
            state = earlier[:, dk:] + step(earlier[:, :dk].astype(BF16), state)
            state = jnp.where(seq >= 2 * index + 2, state, 0.0)
        raw = local_ref[head] + rough(reach_ref[head], state)
        state_ref[head] = prefix_ref[head, :, dk:].astype(F32) + mm(prefix_ref[head, :, :dk], state)
        scale = lax.rsqrt(jnp.mean(raw * raw, axis=1, keepdims=True) + EPSILON)
        unit = raw * scale
        unit_ref[head] = unit
        weighted = weighted_ref[head]
        along = scale * jnp.mean(raw * weighted, axis=1, keepdims=True)
        dout = scale * (weighted - unit * along)
        dout_ref[head] = dout
        back = rough(reach_t_ref[head], dout)
        back_ref[head] = back
        send_ref[head] = back.astype(BF16)


def join_back_kernel(heads, chips, own_ref, other_ref, early_t_ref, *refs):
    flipped, chained = refs[: chips - 1], refs[chips - 1 : 2 * chips - 2]
    later_ref, sends = refs[2 * chips - 2], refs[2 * chips - 1 :]
    upper = is_upper()
    for head in range(heads):
        own, other = own_ref[head], other_ref[head].astype(F32)
        late = jnp.where(upper, own, other)
        first = jnp.where(upper, other, own)
        later_ref[head] = jnp.where(upper, 0.0, other)
        sends[0][head] = (first + rough(early_t_ref[head], late)).astype(BF16)
        for flip_ref, chain_ref, send in zip(flipped, chained, sends[1:]):
            send[head] = (rough(flip_ref[head], first) + rough(chain_ref[head], late)).astype(BF16)


def query_kernel(heads, mask_ref, dout_ref, state_ref, w_ref, score_t_ref, q_ref, k_ref, solve_t_ref,
                 aux_ref, unit_ref, gain_ref, spread_ref, suffix_t_ref, later_ref,
                 weight_ref, out_ref, gq_ref, u_ref, y_ref, dk_ref, reach_ref, *sums):
    frames, dk = q_ref.shape[1:]
    lower, carried, final = mask_ref[1], mask_ref[2], mask_ref[3]
    for head in range(heads):
        dv = unit_ref.shape[2]
        out_ref[:, head * dv : (head + 1) * dv] = (unit_ref[head] * gain_ref[...]).astype(BF16)
        dout, state, solved = dout_ref[head], state_ref[head], w_ref[head]
        query, key = q_ref[head], k_ref[head]
        fresh = solved[:, dk:] - carried * mm(solved[:, :dk], state)
        u_ref[head] = fresh
        later, suffix_t = later_ref[head], suffix_t_ref[head]
        ended = final * fresh
        reach = mm(spread_ref[head], jnp.concatenate([later, suffix_t], axis=1))
        reach_ref[head] = reach[:, dv:]
        y_ref[head] = mm(solve_t_ref[head], mm(score_t_ref[head], dout)) + reach[:, :dv]
        flow = lower * mm_nt(dout, fresh)
        dquery = carried * mm_nt(dout, state) + mm(flow, key)
        dk_ref[head] = mm(flow.T, query) + mm_nt(ended, later)
        scale = aux_ref[:, 4 * head : 4 * head + 1]
        along = jnp.sum(query * dquery, axis=1, keepdims=True)
        gq_ref[:, head * dk : (head + 1) * dk] = (scale * (dquery - query * along)).astype(BF16)
    local = sums[0].shape[1]
    for turn, sum_ref in enumerate(sums, 1):
        first = lax.rem(here()[1] + turn, len(sums) + 1) * local
        sum_ref[...] = dot(gq_ref[...], weight_ref[:, pl.ds(pl.multiple_of(first, local), local)])


def key_kernel(heads, kinds, chips, count, mask_ref, *refs):
    arrived, refs = refs[:chips], refs[chips:]
    (suffix_t_ref, reach_ref, gq_ref, u_ref, y_ref, dk0_ref, state_ref, k_ref, v_ref, gram_ref,
     aux_ref), refs = refs[:11], refs[11:]
    seq = here()[0]
    weights, sums, refs = refs[:4], refs[4 : 3 + kinds], refs[3 + kinds :]
    outs, grads_ref = refs[:-1], refs[-1]
    frames, dk = k_ref.shape[1:]
    strict, carried, final = mask_ref[0], mask_ref[2], mask_ref[3]
    key_grads, value_grads = [], []
    lane = lax.broadcasted_iota(jnp.int32, (frames, LANES), 1)
    logit_grad = jnp.zeros((frames, LANES), F32)
    for head in range(heads):
        after = sum(
            jnp.where(seq + 2 * index + 2 < count, ref[head].astype(F32), 0.0)
            for index, ref in enumerate(arrived)
        )
        key, fresh = k_ref[head], u_ref[head]
        k_scale = aux_ref[:, 4 * head + 1 : 4 * head + 2]
        rate = aux_ref[:, 4 * head + 2 : 4 * head + 3]
        slope = aux_ref[:, 4 * head + 3 : 4 * head + 4]
        y = y_ref[head] + rough(reach_ref[head], after)
        both = rough_nt(y, jnp.concatenate([state_ref[head], fresh], axis=0))
        from_state = -carried * both[:, :dk]
        system = strict * -both[:, dk:]
        scaled = rate * system
        dkey = dk0_ref[head] + rough_nt(rough_nt(final * fresh, after), suffix_t_ref[head])
        dkey = dkey + rough(scaled + scaled.T, key) + rate * from_state
        drate = jnp.sum(
            system * gram_ref[head] + from_state * key + y * v_ref[head], axis=1, keepdims=True
        )
        logit_grad = jnp.where(lane == head, drate * slope, logit_grad)
        along = jnp.sum(key * dkey, axis=1, keepdims=True)
        key_grads.append((k_scale * (dkey - key * along)).astype(BF16))
        value_grads.append((rate * y).astype(BF16))
    grads_ref[...] = jnp.concatenate(
        [gq_ref[...]] + key_grads + value_grads + [logit_grad.astype(BF16)], axis=1
    )
    others, halos = outs[: kinds - 1], outs[kinds - 1 :]
    for turn in range(1, kinds):
        back_products(
            grads_ref, weights, turn, kinds, others[turn - 1], halos[turn - 1], sums[turn - 1]
        )


def back_products(grads_ref, weights, turn, kinds, sum_ref, halo_ref, query_ref=None):
    local = sum_ref.shape[1]
    width = min(512, local)
    for part in range(local // width):
        first = lax.rem(here()[1] + turn, kinds) * local + part * width
        at = pl.ds(pl.multiple_of(first, width), width)
        span = slice(part * width, (part + 1) * width)
        row, total = 0, 0.0
        for index, weight in enumerate(weights):
            if index == 0 and query_ref is not None:
                total = query_ref[:, span]
            else:
                total = total + dot(grads_ref[:, row : row + weight.shape[0]], weight[:, at])
            row += weight.shape[0]
        halo_ref[:, span] = total[:HALO].astype(BF16)
        sum_ref[:, span] = total.astype(sum_ref.dtype)


def own_back_kernel(kinds, grads_ref, *refs):
    back_products(grads_ref, refs[:4], 0, kinds, *refs[4:])


def finish_kernel(kinds, pick_ref, edge_ref, mine_ref, *refs):
    others, halos = refs[: kinds - 1], refs[kinds - 1 : 2 * kinds - 1]
    out_ref, held_ref, semaphores = refs[-3:]
    parts = pick_ref.shape[0]
    copies = []
    width = mine_ref.shape[1] // parts
    for part in range(parts):
        span = slice(part * width, (part + 1) * width)
        total = mine_ref[:, span]
        for other in others:
            total = total + other[:, span].astype(F32)
        edge = halos[0][:, span].astype(F32)
        for halo in halos[1:]:
            edge = edge + halo[:, span].astype(F32)
        moved = dot(pick_ref[part], total.astype(BF16)) + dot(edge_ref[part], edge.astype(BF16))
        held_ref[:, span] = moved.astype(BF16)
        copies.append(
            pltpu.make_async_copy(held_ref.at[:, span], out_ref.at[:, span], semaphores.at[part])
        )
        copies[-1].start()
    for copy in copies:
        copy.wait()


SMEM = pl.BlockSpec(memory_space=pltpu.SMEM)
VMEM = pl.BlockSpec(memory_space=pltpu.VMEM)


def call(body, name, scalars, arrays, outs, flops=0, out_space=VMEM, scratch=()):
    moved = sum(a.size * a.dtype.itemsize for a in arrays)
    moved += sum(o.size * o.dtype.itemsize for o in outs)
    return pl.pallas_call(
        body,
        name=name,
        out_shape=tuple(outs),
        in_specs=[SMEM] * len(scalars) + [VMEM] * len(arrays),
        out_specs=tuple([out_space] * len(outs)),
        scratch_shapes=list(scratch),
        cost_estimate=pl.CostEstimate(flops=flops, bytes_accessed=moved, transcendentals=0),
        compiler_params=pltpu.CompilerParams(vmem_limit_bytes=VMEM_LIMIT),
    )(*scalars, *arrays)


def shape(dims, kind=F32):
    return jax.ShapeDtypeStruct(tuple(dims), kind)


def row_shift(x, by, rising, count):
    chips = count // 2
    pairs = []
    for chip in range(chips):
        up, down = chip + by, chip - by
        pairs.append((2 * chip + rising, 2 * up + rising if up < chips else 2 * chip + 1 - rising))
        pairs.append((2 * chip + 1 - rising, 2 * down + 1 - rising if down >= 0 else 2 * chip + rising))
    return lax.ppermute(x, "seq", pairs)


def seq_shift(x, by, count):
    return lax.ppermute(x, "seq", [(i, (i + by) % count) for i in range(count)])


def core_swap(x, count):
    return lax.ppermute(x, "seq", [(i, i ^ 1) for i in range(count)])


def corner_shift(x, by, turn, count, kinds):
    pairs = []
    for i in range(count):
        for h in range(kinds):
            pairs.append((i * kinds + h, (i + by) % count * kinds + (h + turn) % kinds))
    return lax.ppermute(x, ("seq", "head"), pairs)


def head_turn(x, turn, kinds):
    return lax.ppermute(x, "head", [(h, (h + turn) % kinds) for h in range(kinds)])


def on_device(loaded, out_grad, w_query, w_key, w_value, w_beta, beta_max, out_gain, clip_lengths,
              delay_offsets, block_order):
    count = lax.axis_size("seq")
    kinds = lax.axis_size("head")
    frames, local = loaded.shape
    rows_each = frames // count
    heads = w_beta.shape[1]
    dk = w_query.shape[1] // heads
    dv = w_value.shape[1] // heads
    chips = count // 8
    group = (local * kinds) // delay_offsets.shape[0]
    parts = local // min(group, local)
    columns = heads * (2 * dk + dv) + LANES
    wb = jnp.pad(w_beta, ((0, 0), (0, LANES - heads)))
    gain = out_gain.reshape(1, dv)

    received = lax.all_to_all(
        loaded.reshape(count, rows_each, local), "seq", split_axis=0, concat_axis=0, tiled=True
    ).reshape(frames, local)
    prepared = call(
        functools.partial(prepare_kernel, kinds, local),
        "prepare",
        [block_order, clip_lengths, delay_offsets, beta_max],
        [],
        [
            shape((kinds * parts, frames, frames), BF16),
            shape((kinds * parts, frames, HALO), BF16),
            shape((HALO, frames), BF16),
            shape((parts, frames, frames), BF16),
            shape((parts, frames, HALO), BF16),
            shape((5, frames, frames)),
            shape((heads, 1, LANES)),
        ],
    )
    received, wb, *prepared = lax.optimization_barrier((received, wb, *prepared))
    pick, edge, last, back_pick, back_edge, masks, caps = prepared
    tail = jnp.dot(last, received, preferred_element_type=F32).astype(BF16)
    pieces = [head_turn(received, turn, kinds) for turn in range(1, kinds)]
    halos = [corner_shift(tail, 1, turn, count, kinds) for turn in range(kinds)]
    weights = [w_query, w_key, w_value, wb]
    sums = call(
        functools.partial(own_kernel, kinds),
        "project_own",
        [],
        [received, pick, edge] + weights,
        [shape((frames, weight.shape[1])) for weight in weights],
        flops=2 * frames * local * columns,
    )
    first = call(
        functools.partial(own_halo_kernel, kinds),
        "project_halo",
        [],
        [halos[0], edge] + weights,
        [shape((REACH, weight.shape[1])) for weight in weights],
        flops=2 * REACH * local * columns,
    )
    flipped = call(
        flip_kernel, "flip", [], weights, [shape(w.shape[::-1], BF16) for w in weights]
    )
    sums, first, flipped = lax.optimization_barrier((sums, first, flipped))

    square = shape((heads, frames, dk))
    values = shape((heads, frames, dv))
    times = shape((heads, frames, frames))
    maps = shape((heads, dk, dk + dv), BF16)
    moves = shape((heads, dk, dk))
    states = shape((heads, dk, dv))
    offsets = shape((heads, dk, dv), BF16)
    affine, q, k, v, solve, solved, aux = call(
        functools.partial(project_kernel, heads, kinds),
        "project",
        [],
        [masks, caps] + list(sums) + list(first) + pieces + halos[1:] + [pick, edge] + weights,
        [maps, square, square, values, times, shape((heads, frames, dk + dv)),
         shape((frames, LANES))],
        flops=2 * frames * local * columns,
    )
    results = call(
        functools.partial(join_kernel, heads, chips),
        "join",
        [],
        [affine, core_swap(affine, count)],
        [maps if chips > 1 else offsets, maps, shape(moves.shape, BF16), shape(moves.shape, BF16)]
        + [offsets] * (chips > 1),
        flops=10**7,
    )
    joined, prefix, suffix, early = results[:4]
    arrived = [row_shift(joined, by, (by - 1) % 2, count) for by in range(1, chips)]
    arrived.append(row_shift(results[-1], chips, (chips - 1) % 2, count))
    local_terms = call(
        functools.partial(local_kernel, heads),
        "local_terms",
        [],
        [masks, q, k, solved, solve, early, suffix, prefix, gain, out_grad],
        [times, square, shape((heads, dk, frames)), values, times, times, square, moves, moves,
         values, shape((1, dv))],
        flops=2 * 10**8,
    )
    arrived, local_terms = lax.optimization_barrier((arrived, local_terms))
    (score_t, reach, reach_t, local_out, solve_t, gram, spread, early_t, suffix_t, weighted,
     gains) = local_terms
    swapped = []
    for at in range(0, chips, 2):
        (give,) = call(
            functools.partial(give_kernel, heads), "give", [], arrived[at : at + 2], [maps],
        )
        swapped.append(core_swap(give, count))
    results = call(
        functools.partial(output_kernel, heads, chips),
        "outputs",
        [],
        arrived + swapped + [prefix, reach, reach_t, local_out, weighted],
        [states, values, values, states, offsets],
        flops=2 * 10**8,
    )
    state, unit, dout, back, send = results
    chained = call(
        functools.partial(chain_kernel, heads, chips),
        "chain",
        [],
        arrived + swapped + [early_t],
        [moves] * (2 * chips - 2),
        flops=10**7,
    )
    results = call(
        functools.partial(join_back_kernel, heads, chips),
        "join_back",
        [],
        [back, core_swap(send, count), early_t] + list(chained),
        [states] + [offsets] * chips,
        flops=10**7,
    )
    later = results[0]
    arrived = [seq_shift(x, -2 * by, count) for by, x in enumerate(results[1:], 1)]
    query_terms = call(
        functools.partial(query_kernel, heads),
        "query_grad",
        [],
        [masks, dout, state, solved, score_t, q, k, solve_t, aux, unit, gains, spread, suffix_t,
         later, flipped[0]],
        [shape((frames, heads * dv), BF16), shape((frames, heads * dk), BF16), values, values,
         square, square] + [shape((frames, local))] * (kinds - 1),
        flops=2 * 10**8,
    )
    head_out, gq, fresh, y, dkey, reach = query_terms[:6]
    results = call(
        functools.partial(key_kernel, heads, kinds, chips, count),
        "key_grad",
        [],
        [masks] + arrived + [suffix_t, reach, gq, fresh, y, dkey, state, k, v, gram, aux] + list(flipped)
        + list(query_terms[6:]),
        [shape((frames, local), BF16)] * (kinds - 1)
        + [shape((HALO, local), BF16)] * (kinds - 1)
        + [shape((frames, columns), BF16)],
        flops=2 * 10**8,
    )
    others, edges, grads = results[: kinds - 1], results[kinds - 1 : -1], results[-1]
    mine, edge = call(
        functools.partial(own_back_kernel, kinds),
        "own_back",
        [],
        [grads] + list(flipped),
        [shape((frames, local)), shape((HALO, local), BF16)],
        flops=2 * frames * local * columns,
    )
    others = [head_turn(x, turn, kinds) for turn, x in enumerate(others, 1)]
    edges = [corner_shift(x, -1, turn, count, kinds) for turn, x in enumerate([edge] + list(edges))]
    (input_grad,) = call(
        functools.partial(finish_kernel, kinds),
        "finish",
        [],
        [back_pick, back_edge, mine] + others + edges,
        [shape((frames, local), BF16)],
        flops=10**8,
        out_space=pl.BlockSpec(memory_space=pl.ANY),
        scratch=[pltpu.VMEM((frames, local), BF16), pltpu.SemaphoreType.DMA((parts,))],
    )
    return head_out, input_grad


def solution(mesh):
    return jax.shard_map(
        on_device,
        mesh=mesh,
        in_specs=(
            P("seq", "head"),
            P("seq", "head"),
            P(None, "head"),
            P(None, "head"),
            P(None, "head"),
            P(None, "head"),
            P("head"),
            P(),
            P(),
            P(),
            P("seq", None),
        ),
        out_specs=(P("seq", "head"), P("seq", "head")),
        check_vma=False,
    )
```

```python
import functools

import jax
import jax.numpy as jnp
from jax import lax
from jax.experimental import pallas as pl
from jax.experimental.pallas import tpu as pltpu
from jax.sharding import PartitionSpec as P

EPSILON = 1e-06
F32 = jnp.float32
BF16 = jnp.bfloat16
HALO = 8
REACH = 16
LANES = 128
VMEM_LIMIT = 16 * 1024 * 1024


def halves(x):
    high = x.astype(BF16)
    return high, (x - high.astype(F32)).astype(BF16)


def dot(a, b):
    return jnp.dot(a, b, preferred_element_type=F32)


def dot_nt(a, b):
    return lax.dot_general(a, b, (((1,), (1,)), ((), ())), preferred_element_type=F32)


def mm(a, b):
    width = b.shape[1]
    b_high, b_low = halves(b)
    right = jnp.concatenate([b_high, b_low], axis=1)
    if a.dtype == BF16:
        both = dot(a, right)
    else:
        left = jnp.concatenate(halves(a), axis=1)
        both = dot(left, jnp.concatenate([right, right], axis=0))
    return both[:, :width] + both[:, width:]


def mm_nt(a, b):
    width = b.shape[0]
    left = jnp.concatenate(halves(a), axis=1)
    right = jnp.concatenate(halves(b), axis=0)
    both = dot_nt(left, jnp.concatenate([right, right], axis=1))
    return both[:, :width] + both[:, width:]


def rough(a, b):
    return dot(a.astype(BF16), b.astype(BF16))


def rough_nt(a, b):
    return dot_nt(a.astype(BF16), b.astype(BF16))


def begins(clips_ref, position):
    end = 0
    total = jnp.zeros_like(position)
    for clip in range(clips_ref.shape[0]):
        length = clips_ref[clip]
        end = end + length
        total = total + jnp.where(end <= position, length, 0)
    return total


def here():
    return lax.axis_index("seq"), lax.axis_index("head")


def solve_unit(low, right):
    size = low[0].shape[0]
    row = lax.broadcasted_iota(jnp.int32, (size, size), 0)
    col = lax.broadcasted_iota(jnp.int32, (size, size), 1)
    eye = jnp.where(row == col, 1.0, 0.0).astype(F32)

    def within(width):
        return (row // width) == (col // width)

    def wide_products(lefts, *rights):
        results = []
        for left, *several in zip(lefts, *rights):
            both, at, parts = mm(left, jnp.concatenate(several, axis=1)), 0, []
            for one in several:
                parts.append(both[:, at : at + one.shape[1]])
                at += one.shape[1]
            results.append(parts)
        return [list(part) for part in zip(*results)]

    block = 2
    inverse = [eye - jnp.where(within(block), x, 0.0) for x in low]
    while block < size:
        wide = min(8 * block, size)
        ring = within(wide) & jnp.logical_not(within(block))
        rest = [jnp.where(ring, n, 0.0) for n in low]
        if wide < size:
            (step,) = wide_products(inverse, rest)
            start = inverse
        else:
            step, solved = wide_products(inverse, rest, right)
            start = [jnp.concatenate(both, axis=1) for both in zip(inverse, solved)]
        square, moved = wide_products(step, step, start)
        start = [x - m for x, m in zip(start, moved)]
        fourth, moved = wide_products(square, square, start)
        start = [x + m for x, m in zip(start, moved)]
        inverse = [x + mm(f, x) for f, x in zip(fourth, start)]
        block = wide
    return [x[:, :size] for x in inverse], [x[:, size:] for x in inverse]


def prepare_kernel(kinds, local, order_ref, clips_ref, delays_ref, cap_ref, pick_ref, edge_ref, last_ref,
                   back_pick_ref, back_edge_ref, mask_ref, caps_ref):
    seq, head = here()
    frames = pick_ref.shape[1]
    parts = pick_ref.shape[0] // kinds
    width = local // parts
    group = (local * kinds) // delays_ref.shape[0]
    sources = order_ref.shape[1]
    rows_each = frames // sources
    base = seq * frames
    row = lax.broadcasted_iota(jnp.int32, (frames, frames), 0)
    col = lax.broadcasted_iota(jnp.int32, (frames, frames), 1)
    row_begin = begins(clips_ref, base + row) - base
    col_begin = begins(clips_ref, base + col[:1]) - base
    last_begin = begins(clips_ref, base + frames - 1) - base
    same = row_begin == col_begin
    carried_last = jnp.where(last_begin < 0, 1.0, 0.0)
    mask_ref[0] = jnp.where((row > col) & same, 1.0, 0.0).astype(F32)
    mask_ref[1] = jnp.where((row >= col) & same, 1.0, 0.0).astype(F32)
    mask_ref[2] = jnp.where(row_begin < 0, 1.0, 0.0).astype(F32)
    mask_ref[3] = jnp.where(row_begin == last_begin, 1.0, 0.0).astype(F32)
    mask_ref[4] = jnp.where(row == col, carried_last, 0.0).astype(F32)
    for index in range(caps_ref.shape[0]):
        caps_ref[index] = jnp.full(caps_ref.shape[1:], cap_ref[index], F32)
    lane = col[:1]
    landing = jnp.zeros((1, frames), jnp.int32)
    for source in range(sources):
        at = order_ref[0, source] * rows_each + (lane - source * rows_each)
        landing = jnp.where(lane // rows_each == source, at, landing)
    edge_row = row[:, :HALO]
    edge_col = lax.broadcasted_iota(jnp.int32, (frames, HALO), 1)
    last_ref[...] = jnp.where(landing == row[:HALO] + (frames - HALO), 1.0, 0.0).astype(BF16)
    for kind in range(kinds):
        owner = lax.rem(head + kinds - kind, kinds)
        for part in range(parts):
            source_row = row - delays_ref[(owner * local + part * width) // group]
            inside = source_row >= row_begin
            pick = jnp.where((landing == source_row) & inside, 1.0, 0.0).astype(BF16)
            pick_ref[kind * parts + part] = pick
            edge = (edge_col - HALO == source_row[:, :HALO]) & inside[:, :HALO]
            edge_ref[kind * parts + part] = jnp.where(edge, 1.0, 0.0).astype(BF16)
    edge_begin = begins(clips_ref, base + frames + edge_col[:1]) - base
    for part in range(parts):
        delay = delays_ref[(head * local + part * width) // group]
        pick = jnp.where((col == row + delay) & (col_begin <= row), 1.0, 0.0).astype(BF16)
        back_pick_ref[part] = pick
        edge = (edge_col + frames == edge_row + delay) & (edge_begin <= edge_row)
        back_edge_ref[part] = jnp.where(edge, 1.0, 0.0).astype(BF16)


def flip_kernel(*refs):
    for ref, out_ref in zip(refs[:4], refs[4:]):
        out_ref[...] = ref[...].T


def add_products(sums, kind, kinds, piece_ref, halo_ref, pick_ref, edge_ref, weights):
    local = halo_ref.shape[1] if piece_ref is None else piece_ref.shape[1]
    parts = pick_ref.shape[0] // kinds
    width = local // parts
    owner = lax.rem(here()[1] + kinds - kind, kinds)
    for part in range(parts):
        span = slice(part * width, (part + 1) * width)
        index = kind * parts + part
        if piece_ref is None:
            delayed = dot(edge_ref[index, :REACH], halo_ref[:, span])
        else:
            delayed = dot(pick_ref[index], piece_ref[:, span])
            if halo_ref is not None:
                delayed = delayed + dot(edge_ref[index], halo_ref[:, span])
        at = pl.ds(pl.multiple_of(owner * local + part * width, width), width)
        delayed = delayed.astype(BF16)
        new = [dot(delayed, weight[at, :]) for weight in weights]
        sums = new if sums is None else [a + b for a, b in zip(sums, new)]
    return sums


def own_kernel(kinds, piece_ref, pick_ref, edge_ref, *refs):
    sums = add_products(None, 0, kinds, piece_ref, None, pick_ref, edge_ref, refs[:4])
    for ref, part in zip(refs[4:], sums):
        ref[...] = part


def own_halo_kernel(kinds, halo_ref, edge_ref, *refs):
    sums = add_products(None, 0, kinds, None, halo_ref, edge_ref, edge_ref, refs[:4])
    for ref, part in zip(refs[4:], sums):
        ref[...] = part


def project_kernel(heads, kinds, mask_ref, cap_ref, *refs):
    sums, first, refs = [ref[...] for ref in refs[:4]], [ref[...] for ref in refs[4:8]], refs[8:]
    pieces, halos = refs[: kinds - 1], refs[kinds - 1 : 2 * kinds - 2]
    pick_ref, edge_ref = refs[2 * kinds - 2 : 2 * kinds]
    weights = refs[2 * kinds : 2 * kinds + 4]
    map_ref, q_ref, k_ref, v_ref, solve_ref, w_ref, aux_ref = refs[2 * kinds + 4 :]
    frames = sums[0].shape[0]
    strict, carried, final, eye = mask_ref[0], mask_ref[2], mask_ref[3], mask_ref[4]
    sums = [jnp.concatenate([x[:REACH] + a, x[REACH:]], axis=0) for x, a in zip(sums, first)]
    for kind in range(1, kinds):
        sums = add_products(
            sums, kind, kinds, pieces[kind - 1], halos[kind - 1], pick_ref, edge_ref, weights
        )
    q_all, k_all, v_all, logit_all = sums
    dk = q_all.shape[1] // heads
    dv = v_all.shape[1] // heads
    keys, rights, lows = [], [], []
    aux = jnp.zeros((frames, LANES), F32)
    aux_lane = lax.broadcasted_iota(jnp.int32, (frames, LANES), 1)
    for head in range(heads):
        q_raw = q_all[:, head * dk : (head + 1) * dk]
        k_raw = k_all[:, head * dk : (head + 1) * dk]
        value = v_all[:, head * dv : (head + 1) * dv]
        q_scale = lax.rsqrt(jnp.sum(q_raw * q_raw, axis=1, keepdims=True) + EPSILON)
        k_scale = lax.rsqrt(jnp.sum(k_raw * k_raw, axis=1, keepdims=True) + EPSILON)
        gate = 1.0 / (1.0 + jnp.exp(-logit_all[:, head : head + 1]))
        rate = cap_ref[head, :, :1] * gate
        key = k_raw * k_scale
        q_ref[head] = q_raw * q_scale
        k_ref[head] = key
        v_ref[head] = value
        for index, item in enumerate((q_scale, k_scale, rate, rate * (1.0 - gate))):
            aux = jnp.where(aux_lane == 4 * head + index, item, aux)
        gram = mm_nt(key, key)
        lows.append(strict * (rate * gram))
        keys.append(key)
        rights.append(rate * jnp.concatenate([key, value], axis=1))
    aux_ref[...] = aux
    solves, solutions = solve_unit(lows, rights)
    for head in range(heads):
        solved = solutions[head]
        solve_ref[head] = solves[head]
        w_ref[head] = solved
        ended = jnp.concatenate(
            [-(final * carried) * solved[:, :dk], final * solved[:, dk:]], axis=1
        )
        affine = rough(keys[head].T, ended)
        map_ref[head, :, :dk] = (affine[:, :dk] + eye).astype(BF16)
        map_ref[head, :, dk:] = affine[:, dk:].astype(BF16)


def local_kernel(heads, mask_ref, q_ref, k_ref, w_ref, solve_ref, early_ref, suffix_ref, prefix_ref,
                 gain_ref, grad_ref, score_t_ref, reach_ref, reach_t_ref, local_ref, solve_t_ref,
                 gram_ref, spread_ref, early_t_ref, suffix_t_ref, weighted_ref, gains_ref):
    frames, dk = q_ref.shape[1:]
    lower, carried, final = mask_ref[1], mask_ref[2], mask_ref[3]
    gains_ref[...] = gain_ref[...]
    for head in range(heads):
        query, key, solved = q_ref[head], k_ref[head], w_ref[head]
        scores = lower * mm_nt(query, key)
        both = mm(scores, solved)
        reach = carried * (query - both[:, :dk])
        score_t_ref[head] = scores.T
        prefix = prefix_ref[head]
        reach_t_ref[head] = reach.T
        grown = mm(reach, prefix.astype(F32))
        reach_ref[head] = grown[:, :dk]
        local_ref[head] = both[:, dk:] + grown[:, dk:]
        solve_t = solve_ref[head].T
        solve_t_ref[head] = solve_t
        gram_ref[head] = mm_nt(key, key)
        spread_ref[head] = mm(solve_t, final * key)
        early_t_ref[head] = early_ref[head].astype(F32).T
        suffix_t_ref[head] = suffix_ref[head].astype(F32).T
        dv = local_ref.shape[2]
        weighted_ref[head] = grad_ref[:, head * dv : (head + 1) * dv].astype(F32) * gain_ref[...]


def is_upper():
    return lax.rem(here()[0], 2) == 1


def join_kernel(heads, chips, own_ref, other_ref, *refs):
    joined_ref, prefix_ref, suffix_ref, early_ref = refs[:4]
    dk = own_ref.shape[1]
    upper = is_upper()
    row = lax.broadcasted_iota(jnp.int32, (dk, dk), 0)
    col = lax.broadcasted_iota(jnp.int32, (dk, dk), 1)
    eye = jnp.where(row == col, 1.0, 0.0)
    for head in range(heads):
        own, other = own_ref[head].astype(F32), other_ref[head].astype(F32)
        early = jnp.where(upper, other, own)
        late = jnp.where(upper, own, other)
        both = dot(late[:, :dk].astype(BF16), early.astype(BF16))
        offset = (both[:, dk:] + late[:, dk:]).astype(BF16)
        if chips > 1:
            joined_ref[head, :, :dk] = both[:, :dk].astype(BF16)
            joined_ref[head, :, dk:] = offset
            refs[4][head] = offset
        else:
            joined_ref[head] = offset
        early_ref[head] = early[:, :dk].astype(BF16)
        prefix_ref[head, :, :dk] = jnp.where(upper, other[:, :dk], eye).astype(BF16)
        prefix_ref[head, :, dk:] = jnp.where(upper, other[:, dk:], 0.0).astype(BF16)
        suffix_ref[head] = jnp.where(upper, eye, other[:, :dk]).astype(BF16)


def give_kernel(heads, even_ref, odd_ref, give_ref):
    upper = is_upper()
    width = odd_ref.shape[2]
    for head in range(heads):
        odd = odd_ref[head].astype(F32)
        even = even_ref[head].astype(F32)
        give_ref[head, :, -width:] = jnp.where(upper, odd, even[:, -width:]).astype(BF16)
        if width < even.shape[1]:
            give_ref[head, :, :-width] = even_ref[head, :, :-width]


def shared_maps(heads, rows, swapped):
    maps = []
    upper = is_upper()
    for index, row in enumerate(rows):
        other = swapped[index // 2]
        width = row.shape[2]
        mine = upper if index % 2 else jnp.logical_not(upper)
        maps.append([
            jnp.where(mine, row[head].astype(F32), other[head, :, -width:].astype(F32))
            for head in range(heads)
        ])
    return maps


def chain_kernel(heads, chips, *refs):
    rows, swapped, refs = refs[:chips], refs[chips : chips + chips // 2], refs[chips + chips // 2 :]
    maps = shared_maps(heads, rows[:-1], swapped)
    early_t_ref, flipped, chained = refs[0], refs[1:chips], refs[chips:]
    dk = early_t_ref.shape[1]
    for head in range(heads):
        product = None
        for earlier, flip_ref, chain_ref in zip(maps, flipped, chained):
            move = earlier[head][:, :dk]
            product = move if product is None else mm(product, move)
            flip = product.T
            flip_ref[head] = flip
            chain_ref[head] = rough(flip, early_t_ref[head])


def output_kernel(heads, chips, *refs):
    rows, swapped, refs = refs[:chips], refs[chips : chips + chips // 2], refs[chips + chips // 2 :]
    maps = shared_maps(heads, rows, swapped)
    (prefix_ref, reach_ref, reach_t_ref, local_ref, weighted_ref,
     state_ref, unit_ref, dout_ref, back_ref, send_ref) = refs
    seq = here()[0]
    dk = reach_ref.shape[2]
    for head in range(heads):
        state = jnp.where(seq >= 2 * chips, maps[-1][head], 0.0)
        for index in range(chips - 2, -1, -1):
            earlier = maps[index][head]
            step = rough if index == chips - 2 else mm
            state = earlier[:, dk:] + step(earlier[:, :dk].astype(BF16), state)
            state = jnp.where(seq >= 2 * index + 2, state, 0.0)
        raw = local_ref[head] + rough(reach_ref[head], state)
        state_ref[head] = prefix_ref[head, :, dk:].astype(F32) + rough(prefix_ref[head, :, :dk], state)
        scale = lax.rsqrt(jnp.mean(raw * raw, axis=1, keepdims=True) + EPSILON)
        unit = raw * scale
        unit_ref[head] = unit
        weighted = weighted_ref[head]
        dout = scale * (weighted - unit * jnp.mean(unit * weighted, axis=1, keepdims=True))
        dout_ref[head] = dout
        back = rough(reach_t_ref[head], dout)
        back_ref[head] = back
        send_ref[head] = back.astype(BF16)


def join_back_kernel(heads, chips, own_ref, other_ref, early_t_ref, *refs):
    flipped, chained = refs[: chips - 1], refs[chips - 1 : 2 * chips - 2]
    later_ref, sends = refs[2 * chips - 2], refs[2 * chips - 1 :]
    upper = is_upper()
    for head in range(heads):
        own, other = own_ref[head], other_ref[head].astype(F32)
        late = jnp.where(upper, own, other)
        first = jnp.where(upper, other, own)
        later_ref[head] = jnp.where(upper, 0.0, other)
        sends[0][head] = (first + rough(early_t_ref[head], late)).astype(BF16)
        for flip_ref, chain_ref, send in zip(flipped, chained, sends[1:]):
            send[head] = (rough(flip_ref[head], first) + rough(chain_ref[head], late)).astype(BF16)


def query_kernel(heads, mask_ref, dout_ref, state_ref, w_ref, score_t_ref, q_ref, k_ref, solve_t_ref,
                 aux_ref, unit_ref, gain_ref, spread_ref, suffix_t_ref, later_ref,
                 weight_ref, out_ref, gq_ref, u_ref, y_ref, dk_ref, reach_ref, *sums):
    frames, dk = q_ref.shape[1:]
    lower, carried, final = mask_ref[1], mask_ref[2], mask_ref[3]
    for head in range(heads):
        dv = unit_ref.shape[2]
        out_ref[:, head * dv : (head + 1) * dv] = (unit_ref[head] * gain_ref[...]).astype(BF16)
        dout, state, solved = dout_ref[head], state_ref[head], w_ref[head]
        query, key = q_ref[head], k_ref[head]
        fresh = solved[:, dk:] - carried * mm(solved[:, :dk], state)
        u_ref[head] = fresh
        later, suffix_t = later_ref[head], suffix_t_ref[head]
        ended = final * fresh
        reach = mm(spread_ref[head], jnp.concatenate([later, suffix_t], axis=1))
        reach_ref[head] = reach[:, dv:]
        y_ref[head] = mm(solve_t_ref[head], mm(score_t_ref[head], dout)) + reach[:, :dv]
        flow = lower * mm_nt(dout, fresh)
        dquery = carried * mm_nt(dout, state) + mm(flow, key)
        dk_ref[head] = mm(flow.T, query) + mm_nt(ended, later)
        scale = aux_ref[:, 4 * head : 4 * head + 1]
        along = jnp.sum(query * dquery, axis=1, keepdims=True)
        gq_ref[:, head * dk : (head + 1) * dk] = (scale * (dquery - query * along)).astype(BF16)
    local = sums[0].shape[1]
    for turn, sum_ref in enumerate(sums, 1):
        first = lax.rem(here()[1] + turn, len(sums) + 1) * local
        sum_ref[...] = dot(gq_ref[...], weight_ref[:, pl.ds(pl.multiple_of(first, local), local)])


def key_kernel(heads, kinds, chips, count, mask_ref, *refs):
    arrived, refs = refs[:chips], refs[chips:]
    (suffix_t_ref, reach_ref, gq_ref, u_ref, y_ref, dk0_ref, state_ref, k_ref, v_ref, gram_ref,
     aux_ref), refs = refs[:11], refs[11:]
    seq = here()[0]
    weights, sums, refs = refs[:4], refs[4 : 3 + kinds], refs[3 + kinds :]
    outs, grads_ref = refs[:-1], refs[-1]
    frames, dk = k_ref.shape[1:]
    strict, carried, final = mask_ref[0], mask_ref[2], mask_ref[3]
    key_grads, value_grads = [], []
    lane = lax.broadcasted_iota(jnp.int32, (frames, LANES), 1)
    logit_grad = jnp.zeros((frames, LANES), F32)
    for head in range(heads):
        after = sum(
            jnp.where(seq + 2 * index + 2 < count, ref[head].astype(F32), 0.0)
            for index, ref in enumerate(arrived)
        )
        key, fresh = k_ref[head], u_ref[head]
        k_scale = aux_ref[:, 4 * head + 1 : 4 * head + 2]
        rate = aux_ref[:, 4 * head + 2 : 4 * head + 3]
        slope = aux_ref[:, 4 * head + 3 : 4 * head + 4]
        y = y_ref[head] + rough(reach_ref[head], after)
        both = rough_nt(y, jnp.concatenate([state_ref[head], fresh], axis=0))
        from_state = -carried * both[:, :dk]
        system = strict * -both[:, dk:]
        scaled = rate * system
        dkey = dk0_ref[head] + rough_nt(rough_nt(final * fresh, after), suffix_t_ref[head])
        dkey = dkey + rough(scaled + scaled.T, key) + rate * from_state
        drate = jnp.sum(
            system * gram_ref[head] + from_state * key + y * v_ref[head], axis=1, keepdims=True
        )
        logit_grad = jnp.where(lane == head, drate * slope, logit_grad)
        along = jnp.sum(key * dkey, axis=1, keepdims=True)
        key_grads.append((k_scale * (dkey - key * along)).astype(BF16))
        value_grads.append((rate * y).astype(BF16))
    grads_ref[...] = jnp.concatenate(
        [gq_ref[...]] + key_grads + value_grads + [logit_grad.astype(BF16)], axis=1
    )
    others, halos = outs[: kinds - 1], outs[kinds - 1 :]
    for turn in range(1, kinds):
        back_products(
            grads_ref, weights, turn, kinds, others[turn - 1], halos[turn - 1], sums[turn - 1]
        )


def back_products(grads_ref, weights, turn, kinds, sum_ref, halo_ref, query_ref=None):
    local = sum_ref.shape[1]
    width = min(512, local)
    for part in range(local // width):
        first = lax.rem(here()[1] + turn, kinds) * local + part * width
        at = pl.ds(pl.multiple_of(first, width), width)
        span = slice(part * width, (part + 1) * width)
        row, total = 0, 0.0
        for index, weight in enumerate(weights):
            if index == 0 and query_ref is not None:
                total = query_ref[:, span]
            else:
                total = total + dot(grads_ref[:, row : row + weight.shape[0]], weight[:, at])
            row += weight.shape[0]
        halo_ref[:, span] = total[:HALO].astype(BF16)
        sum_ref[:, span] = total.astype(sum_ref.dtype)


def own_back_kernel(kinds, grads_ref, *refs):
    back_products(grads_ref, refs[:4], 0, kinds, *refs[4:])


def finish_kernel(kinds, pick_ref, edge_ref, mine_ref, *refs):
    others, halos = refs[: kinds - 1], refs[kinds - 1 : 2 * kinds - 1]
    out_ref, held_ref, semaphores = refs[-3:]
    parts = pick_ref.shape[0]
    copies = []
    width = mine_ref.shape[1] // parts
    for part in range(parts):
        span = slice(part * width, (part + 1) * width)
        total = mine_ref[:, span]
        for other in others:
            total = total + other[:, span].astype(F32)
        edge = halos[0][:, span].astype(F32)
        for halo in halos[1:]:
            edge = edge + halo[:, span].astype(F32)
        moved = dot(pick_ref[part], total.astype(BF16)) + dot(edge_ref[part], edge.astype(BF16))
        held_ref[:, span] = moved.astype(BF16)
        copies.append(
            pltpu.make_async_copy(held_ref.at[:, span], out_ref.at[:, span], semaphores.at[part])
        )
        copies[-1].start()
    for copy in copies:
        copy.wait()


SMEM = pl.BlockSpec(memory_space=pltpu.SMEM)
VMEM = pl.BlockSpec(memory_space=pltpu.VMEM)


def call(body, name, scalars, arrays, outs, flops=0, out_space=VMEM, scratch=()):
    moved = sum(a.size * a.dtype.itemsize for a in arrays)
    moved += sum(o.size * o.dtype.itemsize for o in outs)
    return pl.pallas_call(
        body,
        name=name,
        out_shape=tuple(outs),
        in_specs=[SMEM] * len(scalars) + [VMEM] * len(arrays),
        out_specs=tuple([out_space] * len(outs)),
        scratch_shapes=list(scratch),
        cost_estimate=pl.CostEstimate(flops=flops, bytes_accessed=moved, transcendentals=0),
        compiler_params=pltpu.CompilerParams(vmem_limit_bytes=VMEM_LIMIT),
    )(*scalars, *arrays)


def shape(dims, kind=F32):
    return jax.ShapeDtypeStruct(tuple(dims), kind)


def row_shift(x, by, rising, count):
    chips = count // 2
    pairs = []
    for chip in range(chips):
        up, down = chip + by, chip - by
        pairs.append((2 * chip + rising, 2 * up + rising if up < chips else 2 * chip + 1 - rising))
        pairs.append((2 * chip + 1 - rising, 2 * down + 1 - rising if down >= 0 else 2 * chip + rising))
    return lax.ppermute(x, "seq", pairs)


def seq_shift(x, by, count):
    return lax.ppermute(x, "seq", [(i, (i + by) % count) for i in range(count)])


def core_swap(x, count):
    return lax.ppermute(x, "seq", [(i, i ^ 1) for i in range(count)])


def corner_shift(x, by, turn, count, kinds):
    pairs = []
    for i in range(count):
        for h in range(kinds):
            pairs.append((i * kinds + h, (i + by) % count * kinds + (h + turn) % kinds))
    return lax.ppermute(x, ("seq", "head"), pairs)


def head_turn(x, turn, kinds):
    return lax.ppermute(x, "head", [(h, (h + turn) % kinds) for h in range(kinds)])


def on_device(loaded, out_grad, w_query, w_key, w_value, w_beta, beta_max, out_gain, clip_lengths,
              delay_offsets, block_order):
    count = lax.axis_size("seq")
    kinds = lax.axis_size("head")
    frames, local = loaded.shape
    rows_each = frames // count
    heads = w_beta.shape[1]
    dk = w_query.shape[1] // heads
    dv = w_value.shape[1] // heads
    chips = count // 8
    group = (local * kinds) // delay_offsets.shape[0]
    parts = local // min(group, local)
    columns = heads * (2 * dk + dv) + LANES
    wb = jnp.pad(w_beta, ((0, 0), (0, LANES - heads)))
    gain = out_gain.reshape(1, dv)

    received = lax.all_to_all(
        loaded.reshape(count, rows_each, local), "seq", split_axis=0, concat_axis=0, tiled=True
    ).reshape(frames, local)
    prepared = call(
        functools.partial(prepare_kernel, kinds, local),
        "prepare",
        [block_order, clip_lengths, delay_offsets, beta_max],
        [],
        [
            shape((kinds * parts, frames, frames), BF16),
            shape((kinds * parts, frames, HALO), BF16),
            shape((HALO, frames), BF16),
            shape((parts, frames, frames), BF16),
            shape((parts, frames, HALO), BF16),
            shape((5, frames, frames)),
            shape((heads, 1, LANES)),
        ],
    )
    received, wb, *prepared = lax.optimization_barrier((received, wb, *prepared))
    pick, edge, last, back_pick, back_edge, masks, caps = prepared
    tail = jnp.dot(last, received, preferred_element_type=F32).astype(BF16)
    pieces = [head_turn(received, turn, kinds) for turn in range(1, kinds)]
    halos = [corner_shift(tail, 1, turn, count, kinds) for turn in range(kinds)]
    weights = [w_query, w_key, w_value, wb]
    sums = call(
        functools.partial(own_kernel, kinds),
        "project_own",
        [],
        [received, pick, edge] + weights,
        [shape((frames, weight.shape[1])) for weight in weights],
        flops=2 * frames * local * columns,
    )
    first = call(
        functools.partial(own_halo_kernel, kinds),
        "project_halo",
        [],
        [halos[0], edge] + weights,
        [shape((REACH, weight.shape[1])) for weight in weights],
        flops=2 * REACH * local * columns,
    )
    flipped = call(
        flip_kernel, "flip", [], weights, [shape(w.shape[::-1], BF16) for w in weights]
    )
    sums, first, flipped = lax.optimization_barrier((sums, first, flipped))

    square = shape((heads, frames, dk))
    values = shape((heads, frames, dv))
    times = shape((heads, frames, frames))
    maps = shape((heads, dk, dk + dv), BF16)
    moves = shape((heads, dk, dk))
    states = shape((heads, dk, dv))
    offsets = shape((heads, dk, dv), BF16)
    affine, q, k, v, solve, solved, aux = call(
        functools.partial(project_kernel, heads, kinds),
        "project",
        [],
        [masks, caps] + list(sums) + list(first) + pieces + halos[1:] + [pick, edge] + weights,
        [maps, square, square, values, times, shape((heads, frames, dk + dv)),
         shape((frames, LANES))],
        flops=2 * frames * local * columns,
    )
    results = call(
        functools.partial(join_kernel, heads, chips),
        "join",
        [],
        [affine, core_swap(affine, count)],
        [maps if chips > 1 else offsets, maps, shape(moves.shape, BF16), shape(moves.shape, BF16)]
        + [offsets] * (chips > 1),
        flops=10**7,
    )
    joined, prefix, suffix, early = results[:4]
    arrived = [row_shift(joined, by, (by - 1) % 2, count) for by in range(1, chips)]
    arrived.append(row_shift(results[-1], chips, (chips - 1) % 2, count))
    local_terms = call(
        functools.partial(local_kernel, heads),
        "local_terms",
        [],
        [masks, q, k, solved, solve, early, suffix, prefix, gain, out_grad],
        [times, square, shape((heads, dk, frames)), values, times, times, square, moves, moves,
         values, shape((1, dv))],
        flops=2 * 10**8,
    )
    arrived, local_terms = lax.optimization_barrier((arrived, local_terms))
    (score_t, reach, reach_t, local_out, solve_t, gram, spread, early_t, suffix_t, weighted,
     gains) = local_terms
    swapped = []
    for at in range(0, chips, 2):
        (give,) = call(
            functools.partial(give_kernel, heads), "give", [], arrived[at : at + 2], [maps],
        )
        swapped.append(core_swap(give, count))
    results = call(
        functools.partial(output_kernel, heads, chips),
        "outputs",
        [],
        arrived + swapped + [prefix, reach, reach_t, local_out, weighted],
        [states, values, values, states, offsets],
        flops=2 * 10**8,
    )
    state, unit, dout, back, send = results
    chained = call(
        functools.partial(chain_kernel, heads, chips),
        "chain",
        [],
        arrived + swapped + [early_t],
        [moves] * (2 * chips - 2),
        flops=10**7,
    )
    results = call(
        functools.partial(join_back_kernel, heads, chips),
        "join_back",
        [],
        [back, core_swap(send, count), early_t] + list(chained),
        [states] + [offsets] * chips,
        flops=10**7,
    )
    later = results[0]
    arrived = [seq_shift(x, -2 * by, count) for by, x in enumerate(results[1:], 1)]
    query_terms = call(
        functools.partial(query_kernel, heads),
        "query_grad",
        [],
        [masks, dout, state, solved, score_t, q, k, solve_t, aux, unit, gains, spread, suffix_t,
         later, flipped[0]],
        [shape((frames, heads * dv), BF16), shape((frames, heads * dk), BF16), values, values,
         square, square] + [shape((frames, local))] * (kinds - 1),
        flops=2 * 10**8,
    )
    head_out, gq, fresh, y, dkey, reach = query_terms[:6]
    results = call(
        functools.partial(key_kernel, heads, kinds, chips, count),
        "key_grad",
        [],
        [masks] + arrived + [suffix_t, reach, gq, fresh, y, dkey, state, k, v, gram, aux] + list(flipped)
        + list(query_terms[6:]),
        [shape((frames, local), BF16)] * (kinds - 1)
        + [shape((HALO, local), BF16)] * (kinds - 1)
        + [shape((frames, columns), BF16)],
        flops=2 * 10**8,
    )
    others, edges, grads = results[: kinds - 1], results[kinds - 1 : -1], results[-1]
    mine, edge = call(
        functools.partial(own_back_kernel, kinds),
        "own_back",
        [],
        [grads] + list(flipped),
        [shape((frames, local)), shape((HALO, local), BF16)],
        flops=2 * frames * local * columns,
    )
    others = [head_turn(x, turn, kinds) for turn, x in enumerate(others, 1)]
    edges = [corner_shift(x, -1, turn, count, kinds) for turn, x in enumerate([edge] + list(edges))]
    (input_grad,) = call(
        functools.partial(finish_kernel, kinds),
        "finish",
        [],
        [back_pick, back_edge, mine] + others + edges,
        [shape((frames, local), BF16)],
        flops=10**8,
        out_space=pl.BlockSpec(memory_space=pl.ANY),
        scratch=[pltpu.VMEM((frames, local), BF16), pltpu.SemaphoreType.DMA((parts,))],
    )
    return head_out, input_grad


def solution(mesh):
    return jax.shard_map(
        on_device,
        mesh=mesh,
        in_specs=(
            P("seq", "head"),
            P("seq", "head"),
            P(None, "head"),
            P(None, "head"),
            P(None, "head"),
            P(None, "head"),
            P("head"),
            P(),
            P(),
            P(),
            P("seq", None),
        ),
        out_specs=(P("seq", "head"), P("seq", "head")),
        check_vma=False,
    )
```
